32 devices in a mesh: dp: 2 (over x), expert: 16 (over z, y, core).
Axes of the slice: x: 2, y: 2, z: 4, core: 2. Of those that a mesh axis runs over, the one named last changes fastest.
Arguments:
- tokens: bfloat16 [4096, 1024], P(('dp', 'expert')), may hold values from -6 to 6
- d_output: bfloat16 [4096, 1024], P(('dp', 'expert')), may hold values from -6 to 6
- combine: float32 [4096, 8], P(('dp', 'expert')), may hold values from 0.05 to 1
- routes: int32 [4096, 8], P(('dp', 'expert')), may hold values from 0 to 15, all different within a row; in each aligned block of 128 rows (0 to 127, 128 to 255, ...) at most 72 rows name the same one
- gate_weight: bfloat16 [16, 1024, 384], P('expert', 'dp'), may hold values from -0.1875 to 0.1875
- up_weight: bfloat16 [16, 1024, 384], P('expert', 'dp'), may hold values from -0.1875 to 0.1875
- down_weight: bfloat16 [16, 384, 1024], P('expert', None, 'dp'), may hold values from -0.3125 to 0.3125
Outputs:
- d_tokens: bfloat16 [4096, 1024], P(('dp', 'expert'))
- d_gate_weight: float32 [16, 1024, 384], P('expert', 'dp')
- d_up_weight: float32 [16, 1024, 384], P('expert', 'dp')
- d_down_weight: float32 [16, 384, 1024], P('expert', None, 'dp')
The draws below stay inside these ranges and needn't reach their ends.
Inputs may be any that keep to these rules, and one draw needn't show every extreme that they name: `routes`: among the 128 tokens of one device, each expert id is named by at most 72 rows; some expert is named by exactly 72 rows on some device. The ids of one token differ.
All inputs are finite; a program needn't handle non-finite values.
Results may differ from the reference program's by a relative error of at most 0.015.
Values may be sent and summed in bfloat16 or wider, within the bound.
No kernel may reach another device: no remote copies, remote signals or barrier semaphores. Data moves between devices by JAX's collectives and lax.ppermute only.
A program may use at most 64 MiB of HBM per device.

```python
import math
import jax
import jax.numpy as jnp
import numpy as np
from jax import lax

D = 1024
H = 384
TOP = 8
TOK_DEV = 128
EXPERTS = 16
CAP = 72
TOKENS = 4096
N_DP = 2
N_EXPERT = 16


def level_of(key, dims, split, smallest, high):
    def one(dim, shards_of):
        draws = jax.random.uniform(jax.random.fold_in(jax.random.fold_in(key, 6), dim), (shards_of,), jnp.float32, smallest / len(split), high / len(split))
        return jnp.repeat(jnp.exp(draws), dims[dim] // shards_of).reshape((-1,) + (1,) * (len(dims) - dim - 1))

    gain = one(*split[0])
    for cut in split[1:]:
        gain = gain * one(*cut)
    return gain


def shared_out(rng, own, number, rows, count, top, limit, slope):
    sequence = jax.random.permutation(rng, count)
    crowded, ordinary = load_shares(count, rows * top, limit, slope, True), load_shares(count, rows * top, limit, slope, False)
    places = jnp.arange(count)

    def named(sizes, rotation):
        used = int((sizes > 0).sum())
        fixed = max(1, used // 4)
        passed = fixed + (places - fixed + rotation * (used - fixed)) % max(1, count - fixed)
        return jnp.zeros((count,), jnp.int32).at[sequence[jnp.where(places < fixed, places, passed)]].set(jnp.asarray(sizes, jnp.int32))

    sizes = jnp.where(number % 4 == 0, named(crowded, number // 4), named(ordinary, number - number // 4 - 1))
    mixed = jax.random.permutation(jax.random.fold_in(own, 3), count)
    giver, receiver = mixed[0:count // 2 * 2:2], mixed[1:count // 2 * 2:2]
    room = jnp.minimum(sizes[giver] - 1, limit - sizes[receiver]) // 2
    room = jnp.where((giver == sequence[0]) | (receiver == sequence[0]) | (sizes[receiver] == 0), 0, jnp.maximum(room, 0))
    passed = jax.random.randint(jax.random.fold_in(own, 4), (count // 2,), 0, 1 << 20) % (room + 1)
    sizes = sizes.at[giver].add(-passed).at[receiver].add(passed)
    items = jnp.searchsorted(jnp.cumsum(sizes), jnp.arange(rows * top), side="right").astype(jnp.int32)
    listing = items.reshape(top, rows).T
    listing = listing[jax.random.permutation(jax.random.fold_in(own, 1), rows)]
    rotation = jax.random.randint(jax.random.fold_in(own, 2), (rows, 1), 0, top)
    return jnp.take_along_axis(listing, (jnp.arange(top)[None, :] + rotation) % top, axis=1)


def load_shares(number_of, total, reach, lean, full):
    weights = [(1 << 20) // math.isqrt(standing ** lean) + 1 for standing in range(1, number_of + 1)]
    largest = reach if full else min(reach, max(-(-total // number_of), total * weights[0] // sum(weights)))
    least = 1 if total - largest >= number_of - 1 else 0
    counts, rest = [largest] + [least] * (number_of - 1), total - largest - least * (number_of - 1)
    while rest > 0:
        candidates = [i for i in range(1, number_of) if counts[i] < largest] or [i for i in range(1, number_of) if counts[i] < reach]
        pool, left = sum([weights[i] for i in candidates]), rest
        for i in candidates:
            addition = min(reach - counts[i], max(1, left * weights[i] // pool), rest)
            counts[i] = counts[i] + addition
            rest = rest - addition
    return np.array(counts)


def normal_values(key, extent, width, limit, shards=(), kind=jnp.bfloat16):
    drawn = width * jax.random.normal(key, extent, jnp.float32)
    if shards:
        drawn = drawn * level_of(key, extent, shards, -0.22, 0.18)
    return jnp.clip(drawn, -limit, limit).astype(kind)


def setup_inputs(seed: int = 0) -> dict:
    keys = jax.random.split(jax.random.key(seed), 8)
    tokens = normal_values(keys[0], (TOKENS, D), 1.0, 6.0, ((0, 32),))
    d_output = normal_values(keys[1], (TOKENS, D), 1.0, 6.0, ((0, 32),))
    combine = jnp.clip(jnp.exp(math.log(1.0) - 2.9957323 * jax.random.uniform(keys[2], (TOKENS, TOP), jnp.float32) ** level_of(keys[2], (TOKENS, TOP), ((0, 32),), -0.2, 0.2)), 0.05, 1.0)
    routes_keys = jax.random.split(jax.random.fold_in(keys[3], 1), TOKENS // TOK_DEV)
    routes_turns = jax.random.permutation(jax.random.fold_in(keys[3], 3), TOKENS // TOK_DEV)
    routes = jax.vmap(lambda own, number: shared_out(jax.random.fold_in(keys[3], 2), own, number, TOK_DEV, EXPERTS, TOP, CAP, 1))(routes_keys, routes_turns).reshape((TOKENS, TOP))
    gate_weight = normal_values(keys[4], (EXPERTS, D, H), D ** -0.5, 0.1875, ((0, 16), (1, 2)))
    up_weight = normal_values(keys[5], (EXPERTS, D, H), D ** -0.5, 0.1875, ((0, 16), (1, 2)))
    down_weight = normal_values(keys[6], (EXPERTS, H, D), H ** -0.5, 0.3125, ((0, 16), (2, 2)))
    return dict(tokens=tokens, d_output=d_output, combine=combine, routes=routes, gate_weight=gate_weight, up_weight=up_weight, down_weight=down_weight)


def route_slots(routes, experts):
    matches = (routes[:, :, None] == jnp.arange(experts, dtype=jnp.int32)[None, None, :]).astype(jnp.int32)
    per_token = jnp.sum(matches, axis=1)
    earlier = jnp.cumsum(per_token, axis=0) - per_token
    return jnp.sum(matches * earlier[:, None, :], axis=2).astype(jnp.int32)


def row_work(row_inputs, row_grads, gate_up, down_matrix):
    hidden_units = down_matrix.shape[0]
    preact = jnp.dot(row_inputs, gate_up, preferred_element_type=jnp.float32)
    gate_pre = preact[:, :hidden_units]
    up_pre = preact[:, hidden_units:]
    gate_sigmoid = jax.nn.sigmoid(gate_pre)
    hidden = (gate_pre * gate_sigmoid * up_pre).astype(jnp.bfloat16)
    d_hidden = jnp.dot(row_grads, down_matrix.T, preferred_element_type=jnp.float32)
    d_gate_pre = d_hidden * up_pre * gate_sigmoid * (1.0 + gate_pre * (1.0 - gate_sigmoid))
    d_up_pre = d_hidden * gate_pre * gate_sigmoid
    d_preact = jnp.concatenate([d_gate_pre, d_up_pre], axis=1).astype(jnp.bfloat16)
    d_rows = jnp.dot(d_preact, gate_up.T, preferred_element_type=jnp.float32).astype(jnp.bfloat16)
    return d_rows, hidden, d_preact


def expert_grads(row_inputs, row_grads, hidden, d_preact):
    gate_up_grad = jnp.dot(row_inputs.T, d_preact, preferred_element_type=jnp.float32)
    down_grad = jnp.dot(row_grads.T, hidden, preferred_element_type=jnp.float32)
    return jnp.concatenate([gate_up_grad, down_grad], axis=1)


def reference(tokens, d_output, combine, routes, gate_weight, up_weight, down_weight):
    gate_up = jnp.concatenate([gate_weight, up_weight], axis=2)
    tok_groups = tokens.reshape(N_DP, N_EXPERT, TOK_DEV, D)
    grad_groups = d_output.reshape(N_DP, N_EXPERT, TOK_DEV, D)
    combine_groups = combine.reshape(N_DP, N_EXPERT, TOK_DEV, TOP)
    route_groups = routes.reshape(N_DP, N_EXPERT, TOK_DEV, TOP)
    source_ids = jnp.arange(N_EXPERT, dtype=jnp.int32)[:, None, None]

    def one_group(summed, pieces):
        group_tokens, group_grads, group_combine, group_routes = pieces
        slot_index = jax.vmap(lambda one: route_slots(one, N_EXPERT))(group_routes)
        position = (source_ids * CAP + slot_index).astype(jnp.int32)
        scaled = (group_combine[:, :, :, None] * group_grads[:, :, None, :].astype(jnp.float32)).astype(jnp.bfloat16)
        spread_inputs = jnp.broadcast_to(group_tokens[:, :, None, :], (N_EXPERT, TOK_DEV, TOP, D))
        buffer_inputs = jnp.zeros((N_EXPERT, N_EXPERT * CAP, D), jnp.bfloat16).at[group_routes, position].set(spread_inputs)
        buffer_grads = jnp.zeros((N_EXPERT, N_EXPERT * CAP, D), jnp.bfloat16).at[group_routes, position].set(scaled)

        def one_expert(items):
            row_inputs, row_grads, one_gate_up, one_down = items
            d_rows, hidden, d_preact = row_work(row_inputs, row_grads, one_gate_up, one_down)
            partial_value = expert_grads(row_inputs, row_grads, hidden, d_preact).astype(jnp.bfloat16)
            return d_rows, partial_value

        d_buffer, partials = lax.map(one_expert, (buffer_inputs, buffer_grads, gate_up, down_weight))
        route_rows = d_buffer[group_routes, position]
        d_group = jnp.sum(route_rows.astype(jnp.float32), axis=2).astype(jnp.bfloat16)
        return summed + partials.astype(jnp.float32), d_group

    start = jnp.zeros((N_EXPERT, D, 3 * H), jnp.float32)
    summed, d_groups = lax.scan(one_group, start, (tok_groups, grad_groups, combine_groups, route_groups))
    d_tokens = d_groups.reshape(TOKENS, D)
    d_gate_weight = summed[:, :, :H]
    d_up_weight = summed[:, :, H:2 * H]
    d_down_weight = jnp.transpose(summed[:, :, 2 * H:], (0, 2, 1))
    return d_tokens, d_gate_weight, d_up_weight, d_down_weight
```

```python
import functools

import jax
import jax.numpy as jnp
from jax import lax
from jax.experimental import pallas as pl
from jax.experimental.pallas import tpu as pltpu
from jax.sharding import PartitionSpec as P

F32 = jnp.float32
BF16 = jnp.bfloat16
LANES = 128
VMEM_BYTES = 56 * 1024 * 1024


def vmem():
    return pl.BlockSpec(memory_space=pltpu.VMEM)


def smem():
    return pl.BlockSpec(memory_space=pltpu.SMEM)


def hbm():
    return pl.BlockSpec(memory_space=pl.ANY)


def params():
    return pltpu.CompilerParams(vmem_limit_bytes=VMEM_BYTES)


def pack_kernel(experts, tokens, d_output, combine, routes, out):
    rows, width = tokens.shape
    out[:, :width] = tokens[...]
    out[:, width : 2 * width] = d_output[...]
    lane = lax.broadcasted_iota(jnp.int32, (rows, LANES), 1)
    expert = lax.rem(lane, experts)
    dense = jnp.zeros((rows, LANES), F32)
    for k in range(routes.shape[1]):
        dense = dense + jnp.where(expert == routes[:, k : k + 1], combine[:, k : k + 1], 0.0)
    high = dense.astype(BF16).astype(F32)
    rest = dense - high
    middle = rest.astype(BF16).astype(F32)
    low = rest - middle
    parts = jnp.where(
        lane < experts,
        high,
        jnp.where(lane < 2 * experts, middle, jnp.where(lane < 3 * experts, low, 0.0)),
    )
    out[:, 2 * width :] = parts.astype(BF16)


def pack(experts, tokens, d_output, combine, routes):
    rows, width = tokens.shape
    return pl.pallas_call(
        functools.partial(pack_kernel, experts),
        out_shape=jax.ShapeDtypeStruct((rows, 2 * width + LANES), BF16),
        in_specs=[vmem()] * 4,
        out_specs=vmem(),
        compiler_params=params(),
    )(tokens, d_output, combine, routes)


def dot(a, b, dims):
    return lax.dot_general(a, b, (dims, ((), ())), preferred_element_type=F32)


def row_math(experts, expert, blocks, gate_up, down):
    width, hidden_units = gate_up.shape[0], down.shape[0]
    tok = jnp.concatenate([b[:, :width] for b in blocks], axis=0)
    grad = jnp.concatenate([b[:, width : 2 * width] for b in blocks], axis=0)
    parts = jnp.concatenate([b[:, 2 * width :] for b in blocks], axis=0).astype(F32)
    lane = lax.broadcasted_iota(jnp.int32, parts.shape, 1)
    mine = (lax.rem(lane, experts) == expert) & (lane < 3 * experts)
    weight = jnp.sum(jnp.where(mine, parts, 0.0), axis=1, keepdims=True)
    scaled = (weight * grad.astype(F32)).astype(BF16)
    preact = dot(tok, gate_up[...], ((1,), (0,)))
    gate_pre = preact[:, :hidden_units]
    up_pre = preact[:, hidden_units:]
    sig = jax.nn.sigmoid(gate_pre)
    silu = gate_pre * sig
    hidden = (silu * up_pre).astype(BF16)
    d_hidden = dot(scaled, down[...], ((1,), (1,)))
    d_gate = (d_hidden * up_pre * sig * (1.0 + gate_pre * (1.0 - sig))).astype(BF16)
    d_up = (d_hidden * silu).astype(BF16)
    d_preact = jnp.concatenate([d_gate, d_up], axis=1)
    d_rows = dot(d_preact, gate_up[...], ((1,), (1,))).astype(BF16)
    return tok, scaled, hidden, d_preact, d_rows


def rows_kernel(experts, count, first, last, *refs):
    refs = list(refs)
    scal = refs.pop(0)
    blocks = [refs.pop(0) for _ in range(count)]
    if first:
        halves = [refs.pop(0) for _ in range(6)]
    else:
        gate_up, down = refs.pop(0), refs.pop(0)
        if not last:
            sum_gu_in, sum_d_in = refs.pop(0), refs.pop(0)
    own_rows, pair_rows = refs.pop(0), refs.pop(0)
    if last:
        sv_dpre, sv_scaled, sv_hidden = refs.pop(0), refs.pop(0), refs.pop(0)
    else:
        sum_gu, sum_d = refs.pop(0), refs.pop(0)
        if first:
            gate_up, down = refs.pop(0), refs.pop(0)
        sv_tok, sv_scaled, sv_hidden, sv_dpre = (refs.pop(0) for _ in range(4))
        if first:
            sems = refs.pop(0)
    part, expert = scal[0], scal[1]
    if first:
        size, hidden_units = halves[0].shape[0], halves[0].shape[1]
        copies = []
        for i in range(2):
            at = pl.multiple_of((part if i == 0 else 1 - part) * size, size)
            gate, up, dn = halves[3 * i : 3 * i + 3]
            copies += [
                pltpu.make_async_copy(gate, gate_up.at[pl.ds(at, size), pl.ds(0, hidden_units)], sems.at[3 * i]),
                pltpu.make_async_copy(up, gate_up.at[pl.ds(at, size), pl.ds(hidden_units, hidden_units)], sems.at[3 * i + 1]),
                pltpu.make_async_copy(dn, down.at[:, pl.ds(at, size)], sems.at[3 * i + 2]),
            ]
        for c in copies:
            c.start()
        for c in copies:
            c.wait()
    rows = blocks[0].shape[0]
    half = count // 2
    for i in range(0, count, 2):
        tok, scaled, hidden, d_preact, d_rows = row_math(experts, expert, blocks[i : i + 2], gate_up, down)
        span = pl.ds(i * rows, 2 * rows)
        if not last:
            sv_tok[span, :] = tok
        sv_scaled[span, :] = scaled
        sv_hidden[span, :] = hidden
        sv_dpre[span, :] = d_preact
        for j in (i, i + 1):
            piece = d_rows[(j - i) * rows : (j - i + 1) * rows]
            if j < half:
                own_rows[pl.ds(j * rows, rows), :] = piece
            else:
                pair_rows[pl.ds((j - half) * rows, rows), :] = piece
    if last:
        return
    width = sum_gu.shape[0]
    step = 256
    for at in range(0, width, step):
        new = dot(sv_tok[:, at : at + step], sv_dpre[...], ((0,), (0,)))
        if not first:
            new = new + sum_gu_in[at : at + step, :]
        sum_gu[at : at + step, :] = new
    for at in range(0, width, step):
        new = dot(sv_hidden[...], sv_scaled[:, at : at + step], ((0,), (0,)))
        if not first:
            new = new + sum_d_in[:, at : at + step]
        sum_d[:, at : at + step] = new


def rows_call(experts, scal, blocks, weights, sums, width, hidden_units):
    first = len(weights) == 6
    last = not first and sums is None
    count = len(blocks)
    rows = blocks[0].shape[0]
    total = count * rows
    sds = jax.ShapeDtypeStruct
    out = [sds((total // 2, width), BF16)] * 2
    scratch = []
    if last:
        out += [sds((total, 2 * hidden_units), BF16), sds((total, width), BF16), sds((total, hidden_units), BF16)]
    else:
        out += [sds((width, 2 * hidden_units), F32), sds((hidden_units, width), F32)]
        if first:
            out += [sds((width, 2 * hidden_units), BF16), sds((hidden_units, width), BF16)]
        scratch += [
            pltpu.VMEM((total, width), BF16),
            pltpu.VMEM((total, width), BF16),
            pltpu.VMEM((total, hidden_units), BF16),
            pltpu.VMEM((total, 2 * hidden_units), BF16),
        ]
        if first:
            scratch += [pltpu.SemaphoreType.DMA((6,))]
    operands = [scal] + list(blocks) + list(weights)
    specs = [smem()] + [vmem()] * count + [hbm() if first else vmem()] * len(weights)
    if sums is not None:
        operands += list(sums)
        specs += [vmem()] * 2
    macs = total * width * hidden_units * (4 if last else 8)
    return pl.pallas_call(
        functools.partial(rows_kernel, experts, count, first, last),
        out_shape=out,
        in_specs=specs,
        out_specs=[vmem()] * len(out),
        scratch_shapes=scratch,
        cost_estimate=pl.CostEstimate(flops=2 * macs, bytes_accessed=12 * 1024 * 1024, transcendentals=total * hidden_units),
        compiler_params=params(),
    )(*operands)


def half_kernel(count, scal, *refs):
    blocks = refs[:count]
    dpre, scaled, hidden, sum_gu, sum_d, out_gu, out_d = refs[count:]
    tok = jnp.concatenate([b[...] for b in blocks], axis=0)
    out_gu[...] = (sum_gu[...] + dot(tok, dpre[...], ((0,), (0,)))).astype(BF16)
    out_d[...] = (sum_d[...] + dot(hidden[...], scaled[...], ((0,), (0,)))).astype(BF16)


def half_call(which, blocks, dpre, scaled, hidden, sum_gu, sum_d):
    width = sum_gu.shape[0]
    size = width // 2
    hidden_units = hidden.shape[1]
    count = len(blocks)
    rows = blocks[0].shape[0]
    whole = lambda a: pl.BlockSpec(a.shape, lambda i, s: (0, 0))
    side = lambda r: pl.BlockSpec((r, size), lambda i, s: (0, s[0]))
    return pl.pallas_call(
        functools.partial(half_kernel, count),
        out_shape=[
            jax.ShapeDtypeStruct((size, 2 * hidden_units), BF16),
            jax.ShapeDtypeStruct((hidden_units, size), BF16),
        ],
        grid_spec=pltpu.PrefetchScalarGridSpec(
            num_scalar_prefetch=1,
            grid=(1,),
            in_specs=[side(rows)] * count
            + [whole(dpre), side(scaled.shape[0]), whole(hidden)]
            + [pl.BlockSpec((size, 2 * hidden_units), lambda i, s: (s[0], 0)), side(hidden_units)],
            out_specs=[
                pl.BlockSpec((size, 2 * hidden_units), lambda i, s: (0, 0)),
                pl.BlockSpec((hidden_units, size), lambda i, s: (0, 0)),
            ],
        ),
        cost_estimate=pl.CostEstimate(flops=2 * 256 * size * 1152, bytes_accessed=5 * 1024 * 1024, transcendentals=0),
        compiler_params=params(),
    )(which, *blocks, dpre, scaled, hidden, sum_gu, sum_d)


Z, Y, CORES = 4, 2, 2


def pairs_of(move):
    out = []
    for z in range(Z):
        for y in range(Y):
            for c in range(CORES):
                to = move(z, y, c)
                if to is not None:
                    out.append(((z * Y + y) * CORES + c, (to[0] * Y + to[1]) * CORES + to[2]))
    return out


def along_z(table):
    return pairs_of(lambda z, y, c: (table[z], y, c) if z in table else None)


SWAP_CORE = pairs_of(lambda z, y, c: (z, y, 1 - c))
SWAP_Y = pairs_of(lambda z, y, c: (z, 1 - y, c))
OUTER = along_z({0: 1, 1: 0, 2: 3, 3: 2})
INNER = along_z({1: 2, 2: 1})
OUTWARD = along_z({1: 0, 2: 3})
SKIP_TO_INNER = along_z({0: 2, 3: 1})
SKIP_TO_OUTER = along_z({1: 3, 2: 0})
ENDS = along_z({0: 3, 3: 0})


def dense_body(tokens, d_output, combine, routes, gate_weight, up_weight, down_weight):
    experts = lax.axis_size("expert")
    width = tokens.shape[1]
    rows = tokens.shape[0]
    hidden_units = gate_weight.shape[2]
    part = lax.axis_index("dp")
    expert = lax.axis_index("expert")
    z = expert // (Y * CORES)
    inner = (z == 1) | (z == 2)
    scal = jnp.stack([part, expert]).astype(jnp.int32)

    move = lambda a, pairs: lax.ppermute(a, "expert", pairs)
    across = lambda a: lax.ppermute(a, "dp", [(0, 1), (1, 0)])

    gate, up, down = gate_weight[0], up_weight[0], down_weight[0]
    own = pack(experts, tokens, d_output, combine, routes)
    gate2, up2, down2 = across(gate), across(up), across(down)

    b1 = move(own, OUTER)
    f1 = move(own, INNER)
    y0 = move(own, SWAP_Y)
    c0 = move(own, SWAP_CORE)
    f2 = move(b1, INNER)
    g1 = move(f1, OUTWARD)
    y1 = move(b1, SWAP_Y)
    c1 = move(b1, SWAP_CORE)
    cy0 = move(y0, SWAP_CORE)
    b2 = jnp.where(inner, f1, g1)
    y2 = move(b2, SWAP_Y)
    c2 = move(b2, SWAP_CORE)
    cy1 = move(y1, SWAP_CORE)
    g2 = move(f2, OUTWARD)
    b3 = jnp.where(inner, f2, g2)
    y3 = move(b3, SWAP_Y)
    c3 = move(b3, SWAP_CORE)
    cy2 = move(y2, SWAP_CORE)
    cy3 = move(y3, SWAP_CORE)

    call = lambda blocks, weights, sums: rows_call(experts, scal, blocks, weights, sums, width, hidden_units)
    own_a, pair_a, sum_gu, sum_d, gate_up, down_whole = call(
        [own, b1, y0, c0, c1, cy0], [gate, up, down, gate2, up2, down2], None
    )
    back_a = move(pair_a, SWAP_CORE)
    own_b, pair_b, sum_gu, sum_d = call(
        [b2, b3, y1, y2, c2, c3, cy1, cy2], [gate_up, down_whole], [sum_gu, sum_d]
    )
    back_b = move(pair_b, SWAP_CORE)
    own_c, pair_c, dpre, scaled, hidden = call([y3, cy3], [gate_up, down_whole], None)
    back_c = move(pair_c, SWAP_CORE)

    last = [y3, cy3]
    send_gu, send_d = half_call((1 - part)[None].astype(jnp.int32), last, dpre, scaled, hidden, sum_gu, sum_d)
    got_gu, got_d = across(send_gu), across(send_d)
    keep_gu, keep_d = half_call(part[None].astype(jnp.int32), last, dpre, scaled, hidden, sum_gu, sum_d)

    add = lambda *terms: sum(t.astype(F32) for t in terms).astype(BF16)
    ry0 = move(add(own_a[2 * rows :], back_a[2 * rows :]), SWAP_Y)
    ry12 = move(add(own_b[2 * rows :], back_b[2 * rows :]), SWAP_Y)
    ry3 = move(add(own_c, back_c), SWAP_Y)
    s0 = add(own_a[:rows], back_a[:rows], ry0)
    s1 = add(own_a[rows : 2 * rows], back_a[rows : 2 * rows], ry12[:rows])
    s2 = add(own_b[:rows], back_b[:rows], ry12[rows:])
    s3 = add(own_b[rows : 2 * rows], back_b[rows : 2 * rows], ry3)
    d_tokens = add(
        s0,
        move(s1, OUTER),
        move(s2, INNER),
        move(s2, SKIP_TO_INNER),
        move(s3, SKIP_TO_OUTER),
        move(s3, ENDS),
    )
    d_gate = (keep_gu[:, :hidden_units].astype(F32) + got_gu[:, :hidden_units].astype(F32))[None]
    d_up = (keep_gu[:, hidden_units:].astype(F32) + got_gu[:, hidden_units:].astype(F32))[None]
    d_down = (keep_d.astype(F32) + got_d.astype(F32))[None]
    return (d_tokens, d_gate, d_up, d_down)
def route_slots(routes, experts):
    matches = (routes[:, :, None] == jnp.arange(experts, dtype=jnp.int32)[None, None, :]).astype(
        jnp.int32
    )
    per_token = jnp.sum(matches, axis=1)
    earlier = jnp.cumsum(per_token, axis=0) - per_token
    return jnp.sum(matches * earlier[:, None, :], axis=2)


def row_work(row_inputs, row_grads, gate_up, down_matrix):
    hidden_units = down_matrix.shape[0]
    preact = jnp.dot(row_inputs, gate_up, preferred_element_type=jnp.float32)
    gate_pre = preact[:, :hidden_units]
    up_pre = preact[:, hidden_units:]
    gate_sigmoid = jax.nn.sigmoid(gate_pre)
    hidden = (gate_pre * gate_sigmoid * up_pre).astype(jnp.bfloat16)
    d_hidden = jnp.dot(row_grads, down_matrix.T, preferred_element_type=jnp.float32)
    d_gate_pre = d_hidden * up_pre * gate_sigmoid * (1.0 + gate_pre * (1.0 - gate_sigmoid))
    d_up_pre = d_hidden * gate_pre * gate_sigmoid
    d_preact = jnp.concatenate([d_gate_pre, d_up_pre], axis=1).astype(jnp.bfloat16)
    d_rows = jnp.dot(d_preact, gate_up.T, preferred_element_type=jnp.float32).astype(jnp.bfloat16)
    return (d_rows, hidden, d_preact)


def routed_body(tokens, d_output, combine, routes, gate_weight, up_weight, down_weight):
    experts = lax.axis_size("expert")
    tok_count = tokens.shape[0]
    model_width = tokens.shape[1]
    top_count = routes.shape[1]
    capacity = max(2, (9 * tok_count * top_count + 8 * experts - 1) // (8 * experts))
    slot_count = experts * capacity
    slot_index = route_slots(routes, experts)
    position = (routes * capacity + slot_index).reshape(-1)
    spread_inputs = jnp.repeat(tokens, top_count, axis=0)
    scaled = (
        (combine[:, :, None] * d_output[:, None, :].astype(jnp.float32))
        .astype(jnp.bfloat16)
        .reshape(-1, model_width)
    )
    send_inputs = (
        jnp.zeros((slot_count, model_width), jnp.bfloat16)
        .at[position]
        .set(spread_inputs)
        .reshape(experts, capacity, model_width)
    )
    send_grads = (
        jnp.zeros((slot_count, model_width), jnp.bfloat16)
        .at[position]
        .set(scaled)
        .reshape(experts, capacity, model_width)
    )
    whole_gate, whole_up, whole_down = (
        lax.all_gather(gate_weight, "dp", axis=1, tiled=True),
        lax.all_gather(up_weight, "dp", axis=1, tiled=True),
        lax.all_gather(down_weight, "dp", axis=2, tiled=True),
    )
    gate_up = jnp.concatenate([whole_gate[0], whole_up[0]], axis=1)
    down_matrix = whole_down[0]
    hidden_units = down_matrix.shape[0]
    recv_inputs, recv_grads = (
        lax.all_to_all(send_inputs, "expert", split_axis=0, concat_axis=0, tiled=True),
        lax.all_to_all(send_grads, "expert", split_axis=0, concat_axis=0, tiled=True),
    )
    flat_inputs = recv_inputs.reshape(-1, model_width)
    flat_grads = recv_grads.reshape(-1, model_width)
    d_rows, hidden, d_preact = row_work(flat_inputs, flat_grads, gate_up, down_matrix)
    returned = lax.all_to_all(
        d_rows.reshape(experts, capacity, model_width),
        "expert",
        split_axis=0,
        concat_axis=0,
        tiled=True,
    )
    route_rows = returned.reshape(-1, model_width)[position].reshape(
        tok_count, top_count, model_width
    )
    d_tokens = jnp.sum(route_rows.astype(jnp.float32), axis=1).astype(jnp.bfloat16)
    gate_up_grad = jnp.dot(flat_inputs.T, d_preact, preferred_element_type=jnp.float32)
    down_grad = jnp.dot(flat_grads.T, hidden, preferred_element_type=jnp.float32)
    stacked = jnp.concatenate([gate_up_grad, down_grad], axis=1)
    summed = lax.psum_scatter(
        stacked.astype(jnp.bfloat16), "dp", scatter_dimension=0, tiled=True
    ).astype(jnp.float32)
    d_gate_weight = summed[:, :hidden_units][None]
    d_up_weight = summed[:, hidden_units : 2 * hidden_units][None]
    d_down_weight = summed[:, 2 * hidden_units :].T[None]
    return (d_tokens, d_gate_weight, d_up_weight, d_down_weight)


def solution(mesh):
    placed = (
        P(("dp", "expert"), None),
        P(("dp", "expert"), None),
        P(("dp", "expert"), None),
        P(("dp", "expert"), None),
        P("expert", "dp", None),
        P("expert", "dp", None),
        P("expert", None, "dp"),
    )
    dense = mesh.shape["expert"] == Z * Y * CORES and mesh.shape["dp"] == 2
    return jax.shard_map(
        dense_body if dense else routed_body,
        mesh=mesh,
        in_specs=placed,
        out_specs=(
            P(("dp", "expert"), None),
            P("expert", "dp", None),
            P("expert", "dp", None),
            P("expert", None, "dp"),
        ),
        check_vma=False,
    )
```

```python
import functools

import jax
import jax.numpy as jnp
from jax import lax
from jax.experimental import pallas as pl
from jax.experimental.pallas import tpu as pltpu
from jax.sharding import PartitionSpec as P

F32 = jnp.float32
BF16 = jnp.bfloat16
LANES = 128
VMEM_BYTES = 56 * 1024 * 1024


def vmem():
    return pl.BlockSpec(memory_space=pltpu.VMEM)


def smem():
    return pl.BlockSpec(memory_space=pltpu.SMEM)


def hbm():
    return pl.BlockSpec(memory_space=pl.ANY)


def params():
    return pltpu.CompilerParams(vmem_limit_bytes=VMEM_BYTES)


def cost():
    return pl.CostEstimate(flops=1024, bytes_accessed=1024, transcendentals=0)


def dot(a, b, dims):
    return lax.dot_general(a, b, (dims, ((), ())), preferred_element_type=F32)


def pack_kernel(experts, tokens, d_output, combine, routes, out):
    rows, width = tokens.shape
    out[:, :width] = tokens[...]
    out[:, width : 2 * width] = d_output[...]
    line = lax.broadcasted_iota(jnp.int32, (LANES, rows), 0)
    expert = lax.rem(line, experts)
    dense = jnp.zeros((LANES, rows), F32)
    for k in range(routes.shape[0]):
        dense = dense + jnp.where(expert == routes[k : k + 1, :], combine[k : k + 1, :], 0.0)
    high = dense.astype(BF16).astype(F32)
    rest = dense - high
    middle = rest.astype(BF16).astype(F32)
    low = rest - middle
    parts = jnp.where(
        line < experts,
        high,
        jnp.where(line < 2 * experts, middle, jnp.where(line < 3 * experts, low, 0.0)),
    )
    out[:, 2 * width :] = parts.T.astype(BF16)


def pack(experts, tokens, d_output, combine, routes):
    rows, width = tokens.shape
    return pl.pallas_call(
        functools.partial(pack_kernel, experts),
        out_shape=jax.ShapeDtypeStruct((rows, 2 * width + LANES), BF16),
        in_specs=[vmem()] * 4,
        out_specs=vmem(),
        cost_estimate=cost(),
        compiler_params=params(),
    )(tokens, d_output, combine.T, routes.T)


def pack_weights_kernel(gate, up, down, out):
    hidden_units = gate.shape[1]
    out[:, :hidden_units] = gate[...]
    out[:, hidden_units : 2 * hidden_units] = up[...]
    out[:, 2 * hidden_units :] = down[...].T


def pack_weights(gate, up, down):
    size, hidden_units = gate.shape
    return pl.pallas_call(
        pack_weights_kernel,
        out_shape=jax.ShapeDtypeStruct((size, 3 * hidden_units), BF16),
        in_specs=[vmem()] * 3,
        out_specs=vmem(),
        cost_estimate=cost(),
        compiler_params=params(),
    )(gate, up, down)


def rows_kernel(experts, count, scal, *refs):
    refs = list(refs)
    blocks = [refs.pop(0) for _ in range(count)]
    weights = [refs.pop(0) for _ in range(4)]
    out_rows = [refs.pop(0) for _ in range(count)]
    kept = [refs.pop(0) for _ in range(4)]
    held, total, sems = refs
    part, expert = scal[0], scal[1]
    size = weights[0].shape[0]
    hidden_units = weights[0].shape[1] // 3
    width = 2 * size
    rows = blocks[0].shape[0]
    copies = [pltpu.make_async_copy(weights[i], held.at[i], sems.at[i]) for i in range(4)]
    for c in copies:
        c.start()
    sides = [pl.multiple_of(part * size, size), pl.multiple_of((1 - part) * size, size)]
    both = 2 * hidden_units
    for which in range(2):
        scaled_out, grads_out = kept[2 * which], kept[2 * which + 1]
        copies[2 * which].wait()
        copies[2 * which + 1].wait()
        for i in range(0, count, 2):
            group = blocks[i : i + 2]
            span = slice(i * rows, (i + len(group)) * rows)
            parts = jnp.concatenate([b[:, 2 * width :] for b in group], axis=0).astype(F32)
            lane = lax.broadcasted_iota(jnp.int32, parts.shape, 1)
            wanted = expert if which == 0 else expert + 1 - 2 * lax.rem(expert, 2)
            mine = (lax.rem(lane, experts) == wanted) & (lane < 3 * experts)
            weight = jnp.sum(jnp.where(mine, parts, 0.0), axis=1, keepdims=True)
            preact = None
            d_hidden = None
            for side in range(2):
                at = sides[side]
                tok = jnp.concatenate([b[:, pl.ds(at, size)] for b in group], axis=0)
                grad = jnp.concatenate([b[:, pl.ds(pl.multiple_of(width + at, size), size)] for b in group], axis=0)
                scaled = (weight * grad.astype(F32)).astype(BF16)
                scaled_out[span, pl.ds(at, size)] = scaled
                half = held.at[2 * which + side]
                p = dot(tok, half[:, :both], ((1,), (0,)))
                h = dot(scaled, half[:, both:], ((1,), (0,)))
                preact = p if side == 0 else preact + p
                d_hidden = h if side == 0 else d_hidden + h
            gate_pre = preact[:, :hidden_units]
            up_pre = preact[:, hidden_units:]
            sig = jax.nn.sigmoid(gate_pre)
            silu = gate_pre * sig
            d_gate = (d_hidden * up_pre * sig * (1.0 + gate_pre * (1.0 - sig))).astype(BF16)
            d_up = (d_hidden * silu).astype(BF16)
            grads_out[span, :hidden_units] = d_gate
            grads_out[span, hidden_units:both] = d_up
            grads_out[span, both:] = (silu * up_pre).astype(BF16)
            d_preact = jnp.concatenate([d_gate, d_up], axis=1)
            for side in range(2):
                at = sides[side]
                d_rows = dot(d_preact, held[2 * which + side, :, :both], ((1,), (1,)))
                if which == 0:
                    total[span, pl.ds(at, size)] = d_rows
                else:
                    d_rows = (d_rows + total[span, pl.ds(at, size)]).astype(BF16)
                    for j in range(len(group)):
                        out_rows[i + j][:, pl.ds(at, size)] = d_rows[j * rows : (j + 1) * rows]


def rows_call(experts, scal, blocks, weights):
    count = len(blocks)
    rows = blocks[0].shape[0]
    size, stacked = weights[0].shape
    total = count * rows
    sds = jax.ShapeDtypeStruct
    out = [sds((rows, 2 * size), BF16)] * count + [sds((total, 2 * size), BF16), sds((total, stacked), BF16)] * 2
    return pl.pallas_call(
        functools.partial(rows_kernel, experts, count),
        out_shape=out,
        in_specs=[smem()] + [vmem()] * count + [hbm()] * 4,
        out_specs=[vmem()] * len(out),
        scratch_shapes=[
            pltpu.VMEM((4, size, stacked), BF16),
            pltpu.VMEM((total, 2 * size), F32),
            pltpu.SemaphoreType.DMA((4,)),
        ],
        cost_estimate=cost(),
        compiler_params=params(),
    )(scal, *blocks, *weights)


def half_kernel(count, groups, side, *refs):
    blocks = refs[:count]
    scaled = refs[count : count + groups]
    grads = refs[count + groups : count + 2 * groups]
    out = refs[-1]
    both = 2 * (out.shape[1] // 3)
    tok = jnp.concatenate([b[...] for b in blocks], axis=0)
    grad = jnp.concatenate([s[...] for s in scaled], axis=0)
    made = jnp.concatenate([g[...] for g in grads], axis=0)
    out[:, :both] = dot(tok, made[:, :both], ((0,), (0,))).astype(BF16)
    out[:, both:] = dot(grad, made[:, both:], ((0,), (0,))).astype(BF16)


def half_call(side, blocks, scaled, grads):
    size = scaled[0].shape[1] // 2
    stacked = grads[0].shape[1]
    half = lambda a: pl.BlockSpec((a.shape[0], size), lambda i, s: (0, s[0]))
    whole = lambda a: pl.BlockSpec(a.shape, lambda i, s: (0, 0))
    return pl.pallas_call(
        functools.partial(half_kernel, len(blocks), len(scaled)),
        out_shape=jax.ShapeDtypeStruct((size, stacked), BF16),
        grid_spec=pltpu.PrefetchScalarGridSpec(
            num_scalar_prefetch=1,
            grid=(1,),
            in_specs=[half(b) for b in blocks] + [half(s) for s in scaled] + [whole(g) for g in grads],
            out_specs=pl.BlockSpec((size, stacked), lambda i, s: (0, 0)),
        ),
        cost_estimate=cost(),
        compiler_params=params(),
    )(side, *blocks, *scaled, *grads)


def finish_kernel(keep, from_core, from_part, d_gate, d_up, d_down):
    hidden_units = d_gate.shape[1]
    group = (keep[...].astype(F32) + from_core[...].astype(F32)).astype(BF16).astype(F32)
    whole = group + from_part[...].astype(F32)
    d_gate[...] = whole[:, :hidden_units]
    d_up[...] = whole[:, hidden_units : 2 * hidden_units]
    d_down[...] = whole[:, 2 * hidden_units :].T


def finish(keep, from_core, from_part):
    size, stacked = keep.shape
    hidden_units = stacked // 3
    sds = jax.ShapeDtypeStruct
    return pl.pallas_call(
        finish_kernel,
        out_shape=[sds((size, hidden_units), F32), sds((size, hidden_units), F32), sds((hidden_units, size), F32)],
        in_specs=[vmem()] * 3,
        out_specs=[vmem()] * 3,
        cost_estimate=cost(),
        compiler_params=params(),
    )(keep, from_core, from_part)


Z, Y, CORES = 4, 2, 2


def pairs_of(move):
    out = []
    for z in range(Z):
        for y in range(Y):
            for c in range(CORES):
                to = move(z, y, c)
                if to is not None:
                    out.append(((z * Y + y) * CORES + c, (to[0] * Y + to[1]) * CORES + to[2]))
    return out


def along_z(table):
    return pairs_of(lambda z, y, c: (table[z], y, c) if z in table else None)


SWAP_CORE = pairs_of(lambda z, y, c: (z, y, 1 - c))
SWAP_Y = pairs_of(lambda z, y, c: (z, 1 - y, c))
OUTER = along_z({0: 1, 1: 0, 2: 3, 3: 2})
INNER = along_z({1: 2, 2: 1})
OUTWARD = along_z({1: 0, 2: 3})
SKIP_TO_INNER = along_z({0: 2, 3: 1})
SKIP_TO_OUTER = along_z({1: 3, 2: 0})
ENDS = along_z({0: 3, 3: 0})


def after(value, *others):
    return lax.optimization_barrier((value,) + others)[0]


def dense_body(tokens, d_output, combine, routes, gate_weight, up_weight, down_weight):
    experts = lax.axis_size("expert")
    part = lax.axis_index("dp")
    expert = lax.axis_index("expert")
    z = expert // (Y * CORES)
    inner = (z == 1) | (z == 2)
    scal = jnp.stack([part, expert]).astype(jnp.int32)
    mine = part[None].astype(jnp.int32)
    other = (1 - part)[None].astype(jnp.int32)

    move = lambda a, pairs: lax.ppermute(a, "expert", pairs)
    across = lambda a: lax.ppermute(a, "dp", [(0, 1), (1, 0)])

    own = pack(experts, tokens, d_output, combine, routes)
    w_own = pack_weights(gate_weight[0], up_weight[0], down_weight[0])
    w_part = across(w_own)
    w_core = move(w_own, SWAP_CORE)
    w_both = move(w_part, SWAP_CORE)
    weights = [w_own, w_part, w_core, w_both]

    b1 = move(own, OUTER)
    f1 = move(own, INNER)
    y0 = move(own, SWAP_Y)
    f2 = move(b1, INNER)
    y1 = move(b1, SWAP_Y)
    g1 = move(f1, OUTWARD)
    b2 = jnp.where(inner, f1, g1)
    y2 = move(b2, SWAP_Y)
    g2 = move(f2, OUTWARD)
    b3 = jnp.where(inner, f2, g2)
    y3 = move(b3, SWAP_Y)

    p0, p1, q0, *kept_a = rows_call(experts, scal, [own, b1, y0], weights)
    p2, q1, p3, q2, *kept_b = rows_call(experts, scal, [b2, y1, b3, y2], weights)
    q3, *kept_c = rows_call(experts, scal, [y3], weights)
    r0, r1, r2, r3 = (move(q, SWAP_Y) for q in (q0, q1, q2, q3))

    blocks = [own, b1, y0, b2, y1, b3, y2, y3]
    kept = [kept_a, kept_b, kept_c]
    half = lambda side, which: half_call(side, blocks, [k[2 * which] for k in kept], [k[2 * which + 1] for k in kept])
    got = move(half(other, 1), SWAP_CORE)
    send = (half(other, 0).astype(F32) + got.astype(F32)).astype(BF16)
    from_part = across(send)
    from_core = move(half(mine, 1), SWAP_CORE)
    keep = half(mine, 0)

    add = lambda *terms: sum(t.astype(F32) for t in terms).astype(BF16)
    s1 = add(p1, r1)
    s2 = add(p2, r2)
    s3 = add(p3, r3)
    d_tokens = add(
        p0,
        r0,
        move(s1, OUTER),
        move(s2, INNER),
        move(s2, SKIP_TO_INNER),
        move(s3, SKIP_TO_OUTER),
        move(s3, ENDS),
    )
    d_gate, d_up, d_down = finish(keep, from_core, from_part)
    return (d_tokens, d_gate[None], d_up[None], d_down[None])


def route_slots(routes, experts):
    matches = (routes[:, :, None] == jnp.arange(experts, dtype=jnp.int32)[None, None, :]).astype(
        jnp.int32
    )
    per_token = jnp.sum(matches, axis=1)
    earlier = jnp.cumsum(per_token, axis=0) - per_token
    return jnp.sum(matches * earlier[:, None, :], axis=2)


def row_work(row_inputs, row_grads, gate_up, down_matrix):
    hidden_units = down_matrix.shape[0]
    preact = jnp.dot(row_inputs, gate_up, preferred_element_type=jnp.float32)
    gate_pre = preact[:, :hidden_units]
    up_pre = preact[:, hidden_units:]
    gate_sigmoid = jax.nn.sigmoid(gate_pre)
    hidden = (gate_pre * gate_sigmoid * up_pre).astype(jnp.bfloat16)
    d_hidden = jnp.dot(row_grads, down_matrix.T, preferred_element_type=jnp.float32)
    d_gate_pre = d_hidden * up_pre * gate_sigmoid * (1.0 + gate_pre * (1.0 - gate_sigmoid))
    d_up_pre = d_hidden * gate_pre * gate_sigmoid
    d_preact = jnp.concatenate([d_gate_pre, d_up_pre], axis=1).astype(jnp.bfloat16)
    d_rows = jnp.dot(d_preact, gate_up.T, preferred_element_type=jnp.float32).astype(jnp.bfloat16)
    return (d_rows, hidden, d_preact)


def routed_body(tokens, d_output, combine, routes, gate_weight, up_weight, down_weight):
    experts = lax.axis_size("expert")
    tok_count = tokens.shape[0]
    model_width = tokens.shape[1]
    top_count = routes.shape[1]
    capacity = max(2, (9 * tok_count * top_count + 8 * experts - 1) // (8 * experts))
    slot_count = experts * capacity
    slot_index = route_slots(routes, experts)
    position = (routes * capacity + slot_index).reshape(-1)
    spread_inputs = jnp.repeat(tokens, top_count, axis=0)
    scaled = (
        (combine[:, :, None] * d_output[:, None, :].astype(jnp.float32))
        .astype(jnp.bfloat16)
        .reshape(-1, model_width)
    )
    send_inputs = (
        jnp.zeros((slot_count, model_width), jnp.bfloat16)
        .at[position]
        .set(spread_inputs)
        .reshape(experts, capacity, model_width)
    )
    send_grads = (
        jnp.zeros((slot_count, model_width), jnp.bfloat16)
        .at[position]
        .set(scaled)
        .reshape(experts, capacity, model_width)
    )
    whole_gate, whole_up, whole_down = (
        lax.all_gather(gate_weight, "dp", axis=1, tiled=True),
        lax.all_gather(up_weight, "dp", axis=1, tiled=True),
        lax.all_gather(down_weight, "dp", axis=2, tiled=True),
    )
    gate_up = jnp.concatenate([whole_gate[0], whole_up[0]], axis=1)
    down_matrix = whole_down[0]
    hidden_units = down_matrix.shape[0]
    recv_inputs, recv_grads = (
        lax.all_to_all(send_inputs, "expert", split_axis=0, concat_axis=0, tiled=True),
        lax.all_to_all(send_grads, "expert", split_axis=0, concat_axis=0, tiled=True),
    )
    flat_inputs = recv_inputs.reshape(-1, model_width)
    flat_grads = recv_grads.reshape(-1, model_width)
    d_rows, hidden, d_preact = row_work(flat_inputs, flat_grads, gate_up, down_matrix)
    returned = lax.all_to_all(
        d_rows.reshape(experts, capacity, model_width),
        "expert",
        split_axis=0,
        concat_axis=0,
        tiled=True,
    )
    route_rows = returned.reshape(-1, model_width)[position].reshape(
        tok_count, top_count, model_width
    )
    d_tokens = jnp.sum(route_rows.astype(jnp.float32), axis=1).astype(jnp.bfloat16)
    gate_up_grad = jnp.dot(flat_inputs.T, d_preact, preferred_element_type=jnp.float32)
    down_grad = jnp.dot(flat_grads.T, hidden, preferred_element_type=jnp.float32)
    stacked = jnp.concatenate([gate_up_grad, down_grad], axis=1)
    summed = lax.psum_scatter(
        stacked.astype(jnp.bfloat16), "dp", scatter_dimension=0, tiled=True
    ).astype(jnp.float32)
    d_gate_weight = summed[:, :hidden_units][None]
    d_up_weight = summed[:, hidden_units : 2 * hidden_units][None]
    d_down_weight = summed[:, 2 * hidden_units :].T[None]
    return (d_tokens, d_gate_weight, d_up_weight, d_down_weight)


def solution(mesh):
    placed = (
        P(("dp", "expert"), None),
        P(("dp", "expert"), None),
        P(("dp", "expert"), None),
        P(("dp", "expert"), None),
        P("expert", "dp", None),
        P("expert", "dp", None),
        P("expert", None, "dp"),
    )
    dense = mesh.shape["expert"] == Z * Y * CORES and mesh.shape["dp"] == 2
    return jax.shard_map(
        dense_body if dense else routed_body,
        mesh=mesh,
        in_specs=placed,
        out_specs=(
            P(("dp", "expert"), None),
            P("expert", "dp", None),
            P("expert", "dp", None),
            P("expert", None, "dp"),
        ),
        check_vma=False,
    )
```

```python
import functools

import jax
import jax.numpy as jnp
from jax import lax
from jax.experimental import pallas as pl
from jax.experimental.pallas import tpu as pltpu
from jax.sharding import PartitionSpec as P

F32 = jnp.float32
BF16 = jnp.bfloat16
LANES = 128
VMEM_BYTES = 56 * 1024 * 1024


def vmem():
    return pl.BlockSpec(memory_space=pltpu.VMEM)


def smem():
    return pl.BlockSpec(memory_space=pltpu.SMEM)


def hbm():
    return pl.BlockSpec(memory_space=pl.ANY)


def params():
    return pltpu.CompilerParams(vmem_limit_bytes=VMEM_BYTES)


def cost():
    return pl.CostEstimate(flops=1024, bytes_accessed=1024, transcendentals=0)


def dot(a, b, dims):
    return lax.dot_general(a, b, (dims, ((), ())), preferred_element_type=F32)


def pack_kernel(experts, tokens, d_output, combine, routes, out):
    rows, width = tokens.shape
    out[:, :width] = tokens[...]
    out[:, width : 2 * width] = d_output[...]
    line = lax.broadcasted_iota(jnp.int32, (LANES, rows), 0)
    expert = lax.rem(line, experts)
    dense = jnp.zeros((LANES, rows), F32)
    for k in range(routes.shape[0]):
        dense = dense + jnp.where(expert == routes[k : k + 1, :], combine[k : k + 1, :], 0.0)
    high = dense.astype(BF16).astype(F32)
    rest = dense - high
    middle = rest.astype(BF16).astype(F32)
    low = rest - middle
    parts = jnp.where(
        line < experts,
        high,
        jnp.where(line < 2 * experts, middle, jnp.where(line < 3 * experts, low, 0.0)),
    )
    out[:, 2 * width :] = parts.T.astype(BF16)


def pack(experts, tokens, d_output, combine, routes):
    rows, width = tokens.shape
    return pl.pallas_call(
        functools.partial(pack_kernel, experts),
        out_shape=jax.ShapeDtypeStruct((rows, 2 * width + LANES), BF16),
        in_specs=[vmem()] * 4,
        out_specs=vmem(),
        cost_estimate=cost(),
        compiler_params=params(),
    )(tokens, d_output, combine.T, routes.T)


def pack_weights_kernel(gate, up, down, out):
    hidden_units = gate.shape[1]
    out[:, :hidden_units] = gate[...]
    out[:, hidden_units : 2 * hidden_units] = up[...]
    out[:, 2 * hidden_units :] = down[...].T


def pack_weights(gate, up, down):
    size, hidden_units = gate.shape
    return pl.pallas_call(
        pack_weights_kernel,
        out_shape=jax.ShapeDtypeStruct((size, 3 * hidden_units), BF16),
        in_specs=[vmem()] * 3,
        out_specs=vmem(),
        cost_estimate=cost(),
        compiler_params=params(),
    )(gate, up, down)


def rows_kernel(experts, count, merged, scal, *refs):
    refs = list(refs)
    blocks = [refs.pop(0) for _ in range(count)]
    sets = (len(refs) - 3 - merged) // 2
    raw = [refs.pop(0) for _ in range(sets)]
    out_rows = [refs.pop(0) for _ in range(merged)]
    kept = [refs.pop(0) for _ in range(sets)]
    held, total, sems = refs
    part, expert = scal[0], scal[1]
    size = raw[0].shape[0]
    hidden_units = raw[0].shape[1] // 3
    both = 2 * hidden_units
    width = 2 * size
    rows = blocks[0].shape[0]
    copies = [pltpu.make_async_copy(raw[i], held.at[i], sems.at[i]) for i in range(sets)]
    for c in copies:
        c.start()
    sides = [pl.multiple_of(part * size, size), pl.multiple_of((1 - part) * size, size)]
    parts = jnp.concatenate([b[:, 2 * width :] for b in blocks], axis=0).astype(F32)
    lane = lax.broadcasted_iota(jnp.int32, parts.shape, 1)
    toks = [jnp.concatenate([b[:, pl.ds(at, size)] for b in blocks], axis=0) for at in sides]
    for which in range(sets // 2):
        scaled_out, grads_out = kept[2 * which], kept[2 * which + 1]
        for c in copies[2 * which : 2 * which + 2]:
            c.wait()
        wanted = expert if which == 0 else expert + 1 - 2 * lax.rem(expert, 2)
        mine = (lax.rem(lane, experts) == wanted) & (lane < 3 * experts)
        weight = jnp.sum(jnp.where(mine, parts, 0.0), axis=1, keepdims=True)
        preact = None
        d_hidden = None
        for side in range(2):
            at = sides[side]
            grad_at = pl.multiple_of(width + at, size)
            grad = jnp.concatenate([b[:, pl.ds(grad_at, size)] for b in blocks], axis=0)
            scaled = (weight * grad.astype(F32)).astype(BF16)
            scaled_out[:, pl.ds(at, size)] = scaled
            p = dot(toks[side], held[2 * which + side, :, :both], ((1,), (0,)))
            h = dot(scaled, held[2 * which + side, :, both:], ((1,), (0,)))
            preact = p if side == 0 else preact + p
            d_hidden = h if side == 0 else d_hidden + h
        gate_pre = preact[:, :hidden_units]
        up_pre = preact[:, hidden_units:]
        sig = jax.nn.sigmoid(gate_pre)
        silu = gate_pre * sig
        d_gate = (d_hidden * up_pre * sig * (1.0 + gate_pre * (1.0 - sig))).astype(BF16)
        d_up = (d_hidden * silu).astype(BF16)
        grads_out[:, :hidden_units] = d_gate
        grads_out[:, hidden_units:both] = d_up
        grads_out[:, both:] = (silu * up_pre).astype(BF16)
        d_preact = jnp.concatenate([d_gate, d_up], axis=1)
        for side in range(2):
            at = sides[side]
            d_rows = dot(d_preact, held[2 * which + side, :, :both], ((1,), (1,)))
            if which > 0:
                d_rows = d_rows + total[:, pl.ds(at, size)]
            if which + 1 < sets // 2:
                total[:, pl.ds(at, size)] = d_rows
            else:
                d_rows = d_rows.astype(BF16)
                row = 0
                for out in out_rows:
                    out[:, pl.ds(at, size)] = d_rows[row : row + out.shape[0]]
                    row += out.shape[0]


def rows_call(experts, scal, groups, weights):
    blocks = [b for group in groups for b in group]
    count, sets = len(blocks), len(weights)
    rows = blocks[0].shape[0]
    size, stacked = weights[0].shape
    total = count * rows
    sds = jax.ShapeDtypeStruct
    out = [sds((len(group) * rows, 2 * size), BF16) for group in groups]
    out += [sds((total, 2 * size), BF16), sds((total, stacked), BF16)] * (sets // 2)
    return pl.pallas_call(
        functools.partial(rows_kernel, experts, count, len(groups)),
        out_shape=out,
        in_specs=[smem()] + [vmem()] * count + [hbm()] * sets,
        out_specs=[vmem()] * len(out),
        scratch_shapes=[
            pltpu.VMEM((sets, size, stacked), BF16),
            pltpu.VMEM((total, 2 * size), F32),
            pltpu.SemaphoreType.DMA((sets,)),
        ],
        cost_estimate=cost(),
        compiler_params=params(),
    )(scal, *blocks, *weights)


def half_kernel(count, groups, adds, side, *refs):
    blocks = refs[:count]
    scaled = refs[count : count + groups]
    grads = refs[count + groups : count + 2 * groups]
    out = refs[-1]
    both = 2 * (out.shape[1] // 3)
    tok = jnp.concatenate([b[...] for b in blocks], axis=0)
    grad = jnp.concatenate([s[...] for s in scaled], axis=0)
    made = jnp.concatenate([g[...] for g in grads], axis=0)
    gate_up = dot(tok, made[:, :both], ((0,), (0,)))
    down = dot(grad, made[:, both:], ((0,), (0,)))
    if adds:
        more = refs[count + 2 * groups]
        gate_up = gate_up + more[:, :both].astype(F32)
        down = down + more[:, both:].astype(F32)
    out[:, :both] = gate_up.astype(BF16)
    out[:, both:] = down.astype(BF16)


def half_call(side, blocks, scaled, grads, more=None):
    size = scaled[0].shape[1] // 2
    stacked = grads[0].shape[1]
    half = lambda a: pl.BlockSpec((a.shape[0], size), lambda i, s: (0, s[0]))
    whole = lambda a: pl.BlockSpec(a.shape, lambda i, s: (0, 0))
    extra = [] if more is None else [more]
    return pl.pallas_call(
        functools.partial(half_kernel, len(blocks), len(scaled), len(extra)),
        out_shape=jax.ShapeDtypeStruct((size, stacked), BF16),
        grid_spec=pltpu.PrefetchScalarGridSpec(
            num_scalar_prefetch=1,
            grid=(1,),
            in_specs=[half(b) for b in blocks] + [half(s) for s in scaled] + [whole(g) for g in [*grads, *extra]],
            out_specs=pl.BlockSpec((size, stacked), lambda i, s: (0, 0)),
        ),
        cost_estimate=cost(),
        compiler_params=params(),
    )(side, *blocks, *scaled, *grads, *extra)


def finish_kernel(keep, from_part, d_gate, d_up, d_down):
    hidden_units = d_gate.shape[1]
    whole = keep[...].astype(F32) + from_part[...].astype(F32)
    d_gate[...] = whole[:, :hidden_units]
    d_up[...] = whole[:, hidden_units : 2 * hidden_units]
    d_down[...] = whole[:, 2 * hidden_units :].T


def finish(keep, from_part):
    size, stacked = keep.shape
    hidden_units = stacked // 3
    sds = jax.ShapeDtypeStruct
    step = size // 4
    piece = lambda n: pl.BlockSpec((step, n), lambda i: (i, 0))
    return pl.pallas_call(
        finish_kernel,
        out_shape=[sds((size, hidden_units), F32), sds((size, hidden_units), F32), sds((hidden_units, size), F32)],
        grid=(size // step,),
        in_specs=[piece(stacked)] * 2,
        out_specs=[piece(hidden_units), piece(hidden_units), pl.BlockSpec((hidden_units, step), lambda i: (0, i))],
        cost_estimate=cost(),
        compiler_params=params(),
    )(keep, from_part)


Z, Y, CORES = 4, 2, 2


def pairs_of(move):
    out = []
    for z in range(Z):
        for y in range(Y):
            for c in range(CORES):
                to = move(z, y, c)
                if to is not None:
                    out.append(((z * Y + y) * CORES + c, (to[0] * Y + to[1]) * CORES + to[2]))
    return out


def along_z(table):
    return pairs_of(lambda z, y, c: (table[z], y, c) if z in table else None)


SWAP_CORE = pairs_of(lambda z, y, c: (z, y, 1 - c))
SWAP_Y = pairs_of(lambda z, y, c: (z, 1 - y, c))
OUTER = along_z({0: 1, 1: 0, 2: 3, 3: 2})
INNER = along_z({1: 2, 2: 1})
OUTWARD = along_z({1: 0, 2: 3})
SKIP_TO_INNER = along_z({0: 2, 3: 1})
SKIP_TO_OUTER = along_z({1: 3, 2: 0})
ENDS = along_z({0: 3, 3: 0})


def after(value, *others):
    return lax.optimization_barrier((value,) + others)[0]


def dense_body(tokens, d_output, combine, routes, gate_weight, up_weight, down_weight):
    experts = lax.axis_size("expert")
    part = lax.axis_index("dp")
    expert = lax.axis_index("expert")
    z = expert // (Y * CORES)
    inner = (z == 1) | (z == 2)
    scal = jnp.stack([part, expert]).astype(jnp.int32)
    mine = part[None].astype(jnp.int32)
    other = (1 - part)[None].astype(jnp.int32)

    move = lambda a, pairs: lax.ppermute(a, "expert", pairs)
    across = lambda a: lax.ppermute(a, "dp", [(0, 1), (1, 0)])

    swap = lambda a: move(a, SWAP_CORE)
    w_own = pack_weights(gate_weight[0], up_weight[0], down_weight[0])
    w_part = across(w_own)
    own = pack(experts, tokens, d_output, combine, routes)

    b1 = move(own, OUTER)
    f1 = move(own, INNER)
    y0 = move(own, SWAP_Y)
    w_core = swap(w_own)
    f2 = move(b1, INNER)
    y1 = move(after(b1, y0), SWAP_Y)
    g1 = move(f1, OUTWARD)
    b2 = jnp.where(inner, f1, g1)
    y2 = move(after(b2, y1, w_part), SWAP_Y)
    w_both = swap(w_part)
    weights = [w_own, w_part, w_core, w_both]
    g2 = move(f2, OUTWARD)
    b3 = jnp.where(inner, f2, g2)

    p0, p1, q0, *kept_a = rows_call(experts, scal, [[own], [b1], [y0]], weights)
    y3 = move(after(b3, y2, p0), SWAP_Y)
    p2, p3, q12, *kept_b = rows_call(experts, scal, [[b2], [b3], [y1, y2]], weights)

    blocks = [own, b1, y0, b2, b3, y1, y2]
    kept = [kept_a, kept_b]
    others = lambda side, first: half_call(side, [first] + blocks[1:], [k[2] for k in kept], [k[3] for k in kept])
    to_core = others(other, own)
    y3 = after(y3, p2, to_core)
    r12 = move(after(q12, y3), SWAP_Y)
    r0 = move(after(q0, y3), SWAP_Y)

    cy3 = swap(y3)
    last, pair, scaled_c, grads_c = rows_call(experts, scal, [[y3], [cy3]], weights[:2])
    q3 = last.astype(F32) + swap(pair).astype(F32)
    all_blocks = blocks + [y3, cy3]
    mine_of = lambda side, more: half_call(
        side, all_blocks, [k[0] for k in kept] + [scaled_c], [k[1] for k in kept] + [grads_c], more
    )
    send = mine_of(other, swap(to_core))
    from_part = across(send)
    keep = mine_of(mine, swap(others(mine, after(own, send))))

    rows = own.shape[0]
    r1, r2 = r12[:rows], r12[rows:]
    r3 = move(after(q3.astype(BF16), r0, r12), SWAP_Y)
    add = lambda *terms: sum(t.astype(F32) for t in terms).astype(BF16)
    s1 = add(p1, r1)
    s2 = add(p2, r2)
    s3 = after(add(p3, r3), keep)
    d_tokens = add(
        p0,
        r0,
        move(s1, OUTER),
        move(s2, INNER),
        move(s2, SKIP_TO_INNER),
        move(s3, SKIP_TO_OUTER),
        move(s3, ENDS),
    )
    d_gate, d_up, d_down = finish(keep, from_part)
    return (d_tokens, d_gate[None], d_up[None], d_down[None])


def route_slots(routes, experts):
    matches = (routes[:, :, None] == jnp.arange(experts, dtype=jnp.int32)[None, None, :]).astype(
        jnp.int32
    )
    per_token = jnp.sum(matches, axis=1)
    earlier = jnp.cumsum(per_token, axis=0) - per_token
    return jnp.sum(matches * earlier[:, None, :], axis=2)


def row_work(row_inputs, row_grads, gate_up, down_matrix):
    hidden_units = down_matrix.shape[0]
    preact = jnp.dot(row_inputs, gate_up, preferred_element_type=jnp.float32)
    gate_pre = preact[:, :hidden_units]
    up_pre = preact[:, hidden_units:]
    gate_sigmoid = jax.nn.sigmoid(gate_pre)
    hidden = (gate_pre * gate_sigmoid * up_pre).astype(jnp.bfloat16)
    d_hidden = jnp.dot(row_grads, down_matrix.T, preferred_element_type=jnp.float32)
    d_gate_pre = d_hidden * up_pre * gate_sigmoid * (1.0 + gate_pre * (1.0 - gate_sigmoid))
    d_up_pre = d_hidden * gate_pre * gate_sigmoid
    d_preact = jnp.concatenate([d_gate_pre, d_up_pre], axis=1).astype(jnp.bfloat16)
    d_rows = jnp.dot(d_preact, gate_up.T, preferred_element_type=jnp.float32).astype(jnp.bfloat16)
    return (d_rows, hidden, d_preact)


def routed_body(tokens, d_output, combine, routes, gate_weight, up_weight, down_weight):
    experts = lax.axis_size("expert")
    tok_count = tokens.shape[0]
    model_width = tokens.shape[1]
    top_count = routes.shape[1]
    capacity = max(2, (9 * tok_count * top_count + 8 * experts - 1) // (8 * experts))
    slot_count = experts * capacity
    slot_index = route_slots(routes, experts)
    position = (routes * capacity + slot_index).reshape(-1)
    spread_inputs = jnp.repeat(tokens, top_count, axis=0)
    scaled = (
        (combine[:, :, None] * d_output[:, None, :].astype(jnp.float32))
        .astype(jnp.bfloat16)
        .reshape(-1, model_width)
    )
    send_inputs = (
        jnp.zeros((slot_count, model_width), jnp.bfloat16)
        .at[position]
        .set(spread_inputs)
        .reshape(experts, capacity, model_width)
    )
    send_grads = (
        jnp.zeros((slot_count, model_width), jnp.bfloat16)
        .at[position]
        .set(scaled)
        .reshape(experts, capacity, model_width)
    )
    whole_gate, whole_up, whole_down = (
        lax.all_gather(gate_weight, "dp", axis=1, tiled=True),
        lax.all_gather(up_weight, "dp", axis=1, tiled=True),
        lax.all_gather(down_weight, "dp", axis=2, tiled=True),
    )
    gate_up = jnp.concatenate([whole_gate[0], whole_up[0]], axis=1)
    down_matrix = whole_down[0]
    hidden_units = down_matrix.shape[0]
    recv_inputs, recv_grads = (
        lax.all_to_all(send_inputs, "expert", split_axis=0, concat_axis=0, tiled=True),
        lax.all_to_all(send_grads, "expert", split_axis=0, concat_axis=0, tiled=True),
    )
    flat_inputs = recv_inputs.reshape(-1, model_width)
    flat_grads = recv_grads.reshape(-1, model_width)
    d_rows, hidden, d_preact = row_work(flat_inputs, flat_grads, gate_up, down_matrix)
    returned = lax.all_to_all(
        d_rows.reshape(experts, capacity, model_width),
        "expert",
        split_axis=0,
        concat_axis=0,
        tiled=True,
    )
    route_rows = returned.reshape(-1, model_width)[position].reshape(
        tok_count, top_count, model_width
    )
    d_tokens = jnp.sum(route_rows.astype(jnp.float32), axis=1).astype(jnp.bfloat16)
    gate_up_grad = jnp.dot(flat_inputs.T, d_preact, preferred_element_type=jnp.float32)
    down_grad = jnp.dot(flat_grads.T, hidden, preferred_element_type=jnp.float32)
    stacked = jnp.concatenate([gate_up_grad, down_grad], axis=1)
    summed = lax.psum_scatter(
        stacked.astype(jnp.bfloat16), "dp", scatter_dimension=0, tiled=True
    ).astype(jnp.float32)
    d_gate_weight = summed[:, :hidden_units][None]
    d_up_weight = summed[:, hidden_units : 2 * hidden_units][None]
    d_down_weight = summed[:, 2 * hidden_units :].T[None]
    return (d_tokens, d_gate_weight, d_up_weight, d_down_weight)


def solution(mesh):
    placed = (
        P(("dp", "expert"), None),
        P(("dp", "expert"), None),
        P(("dp", "expert"), None),
        P(("dp", "expert"), None),
        P("expert", "dp", None),
        P("expert", "dp", None),
        P("expert", None, "dp"),
    )
    dense = mesh.shape["expert"] == Z * Y * CORES and mesh.shape["dp"] == 2
    return jax.shard_map(
        dense_body if dense else routed_body,
        mesh=mesh,
        in_specs=placed,
        out_specs=(
            P(("dp", "expert"), None),
            P("expert", "dp", None),
            P("expert", "dp", None),
            P("expert", None, "dp"),
        ),
        check_vma=False,
    )
```

```python
import functools

import jax
import jax.numpy as jnp
from jax import lax
from jax.experimental import pallas as pl
from jax.experimental.pallas import tpu as pltpu
from jax.sharding import PartitionSpec as P

F32 = jnp.float32
BF16 = jnp.bfloat16
LANES = 128
VMEM_BYTES = 56 * 1024 * 1024


def vmem():
    return pl.BlockSpec(memory_space=pltpu.VMEM)


def smem():
    return pl.BlockSpec(memory_space=pltpu.SMEM)


def hbm():
    return pl.BlockSpec(memory_space=pl.ANY)


def params():
    return pltpu.CompilerParams(vmem_limit_bytes=VMEM_BYTES)


def cost(flops, moved):
    return pl.CostEstimate(flops=int(flops), bytes_accessed=int(moved), transcendentals=0)


def dot(a, b, dims):
    return lax.dot_general(a, b, (dims, ((), ())), preferred_element_type=F32)


def pack_kernel(experts, tokens, d_output, combine, routes, out):
    rows, width = tokens.shape
    out[:, :width] = tokens[...]
    out[:, width : 2 * width] = d_output[...]
    line = lax.broadcasted_iota(jnp.int32, (LANES, rows), 0)
    expert = lax.rem(line, experts)
    dense = jnp.zeros((LANES, rows), F32)
    for k in range(routes.shape[0]):
        dense = dense + jnp.where(expert == routes[k : k + 1, :], combine[k : k + 1, :], 0.0)
    high = dense.astype(BF16).astype(F32)
    rest = dense - high
    middle = rest.astype(BF16).astype(F32)
    low = rest - middle
    parts = jnp.where(
        line < experts,
        high,
        jnp.where(line < 2 * experts, middle, jnp.where(line < 3 * experts, low, 0.0)),
    )
    out[:, 2 * width :] = parts.T.astype(BF16)


def pack(experts, tokens, d_output, combine, routes):
    rows, width = tokens.shape
    return pl.pallas_call(
        functools.partial(pack_kernel, experts),
        out_shape=jax.ShapeDtypeStruct((rows, 2 * width + LANES), BF16),
        in_specs=[vmem()] * 4,
        out_specs=vmem(),
        cost_estimate=cost(0, 3 * rows * width * 2 * 2),
        compiler_params=params(),
    )(tokens, d_output, combine.T, routes.T)


def pack_weights_kernel(gate, up, down, out):
    hidden_units = gate.shape[1]
    out[:, :hidden_units] = gate[...]
    out[:, hidden_units : 2 * hidden_units] = up[...]
    out[:, 2 * hidden_units :] = down[...].T


def pack_weights(gate, up, down):
    size, hidden_units = gate.shape
    return pl.pallas_call(
        pack_weights_kernel,
        out_shape=jax.ShapeDtypeStruct((size, 3 * hidden_units), BF16),
        in_specs=[vmem()] * 3,
        out_specs=vmem(),
        cost_estimate=cost(0, 6 * size * hidden_units * 4),
        compiler_params=params(),
    )(gate, up, down)


def rows_kernel(experts, count, merged, scal, *refs):
    refs = list(refs)
    blocks = [refs.pop(0) for _ in range(count)]
    sets = (len(refs) - 3 - merged) // 2
    raw = [refs.pop(0) for _ in range(sets)]
    out_rows = [refs.pop(0) for _ in range(merged)]
    kept = [refs.pop(0) for _ in range(sets)]
    held, total, sems = refs
    part, expert = scal[0], scal[1]
    size = raw[0].shape[0]
    hidden_units = raw[0].shape[1] // 3
    both = 2 * hidden_units
    width = 2 * size
    rows = blocks[0].shape[0]
    copies = [pltpu.make_async_copy(raw[i], held.at[i], sems.at[i]) for i in range(sets)]
    for c in copies:
        c.start()
    sides = [pl.multiple_of(part * size, size), pl.multiple_of((1 - part) * size, size)]
    parts = jnp.concatenate([b[:, 2 * width :] for b in blocks], axis=0).astype(F32)
    lane = lax.broadcasted_iota(jnp.int32, parts.shape, 1)
    toks = [jnp.concatenate([b[:, pl.ds(at, size)] for b in blocks], axis=0) for at in sides]
    for which in range(sets // 2):
        scaled_out, grads_out = kept[2 * which], kept[2 * which + 1]
        for c in copies[2 * which : 2 * which + 2]:
            c.wait()
        wanted = expert if which == 0 else expert + 1 - 2 * lax.rem(expert, 2)
        mine = (lax.rem(lane, experts) == wanted) & (lane < 3 * experts)
        weight = jnp.sum(jnp.where(mine, parts, 0.0), axis=1, keepdims=True)
        preact = None
        d_hidden = None
        for side in range(2):
            at = sides[side]
            grad_at = pl.multiple_of(width + at, size)
            grad = jnp.concatenate([b[:, pl.ds(grad_at, size)] for b in blocks], axis=0)
            scaled = (weight * grad.astype(F32)).astype(BF16)
            scaled_out[:, pl.ds(at, size)] = scaled
            p = dot(toks[side], held[2 * which + side, :, :both], ((1,), (0,)))
            h = dot(scaled, held[2 * which + side, :, both:], ((1,), (0,)))
            preact = p if side == 0 else preact + p
            d_hidden = h if side == 0 else d_hidden + h
        gate_pre = preact[:, :hidden_units]
        up_pre = preact[:, hidden_units:]
        sig = jax.nn.sigmoid(gate_pre)
        silu = gate_pre * sig
        d_gate = (d_hidden * up_pre * sig * (1.0 + gate_pre * (1.0 - sig))).astype(BF16)
        d_up = (d_hidden * silu).astype(BF16)
        grads_out[:, :hidden_units] = d_gate
        grads_out[:, hidden_units:both] = d_up
        grads_out[:, both:] = (silu * up_pre).astype(BF16)
        d_preact = jnp.concatenate([d_gate, d_up], axis=1)
        for side in range(2):
            at = sides[side]
            d_rows = dot(d_preact, held[2 * which + side, :, :both], ((1,), (1,)))
            if which > 0:
                d_rows = d_rows + total[:, pl.ds(at, size)]
            if which + 1 < sets // 2:
                total[:, pl.ds(at, size)] = d_rows
            else:
                d_rows = d_rows.astype(BF16)
                row = 0
                for out in out_rows:
                    out[:, pl.ds(at, size)] = d_rows[row : row + out.shape[0]]
                    row += out.shape[0]


def rows_call(experts, scal, groups, weights):
    blocks = [b for group in groups for b in group]
    count, sets = len(blocks), len(weights)
    rows = blocks[0].shape[0]
    size, stacked = weights[0].shape
    total = count * rows
    sds = jax.ShapeDtypeStruct
    out = [sds((len(group) * rows, 2 * size), BF16) for group in groups]
    out += [sds((total, 2 * size), BF16), sds((total, stacked), BF16)] * (sets // 2)
    return pl.pallas_call(
        functools.partial(rows_kernel, experts, count, len(groups)),
        out_shape=out,
        in_specs=[smem()] + [vmem()] * count + [hbm()] * sets,
        out_specs=[vmem()] * len(out),
        scratch_shapes=[
            pltpu.VMEM((sets, size, stacked), BF16),
            pltpu.VMEM((total, 2 * size), F32),
            pltpu.SemaphoreType.DMA((sets,)),
        ],
        cost_estimate=cost(24 * total * size * stacked * sets // 2, 1 << 20),
        compiler_params=params(),
    )(scal, *blocks, *weights)


def half_kernel(count, groups, adds, side, *refs):
    blocks = refs[:count]
    scaled = refs[count : count + groups]
    grads = refs[count + groups : count + 2 * groups]
    out = refs[-1]
    both = 2 * (out.shape[1] // 3)
    tok = jnp.concatenate([b[...] for b in blocks], axis=0)
    grad = jnp.concatenate([s[...] for s in scaled], axis=0)
    made = jnp.concatenate([g[...] for g in grads], axis=0)
    gate_up = dot(tok, made[:, :both], ((0,), (0,)))
    down = dot(grad, made[:, both:], ((0,), (0,)))
    if adds:
        more = refs[count + 2 * groups]
        gate_up = gate_up + more[:, :both].astype(F32)
        down = down + more[:, both:].astype(F32)
    out[:, :both] = gate_up.astype(BF16)
    out[:, both:] = down.astype(BF16)


def half_call(side, blocks, scaled, grads, more=None):
    size = scaled[0].shape[1] // 2
    stacked = grads[0].shape[1]
    half = lambda a: pl.BlockSpec((a.shape[0], size), lambda i, s: (0, s[0]))
    whole = lambda a: pl.BlockSpec(a.shape, lambda i, s: (0, 0))
    extra = [] if more is None else [more]
    return pl.pallas_call(
        functools.partial(half_kernel, len(blocks), len(scaled), len(extra)),
        out_shape=jax.ShapeDtypeStruct((size, stacked), BF16),
        grid_spec=pltpu.PrefetchScalarGridSpec(
            num_scalar_prefetch=1,
            grid=(1,),
            in_specs=[half(b) for b in blocks] + [half(s) for s in scaled] + [whole(g) for g in [*grads, *extra]],
            out_specs=pl.BlockSpec((size, stacked), lambda i, s: (0, 0)),
        ),
        cost_estimate=cost(1024, 1024),
        compiler_params=params(),
    )(side, *blocks, *scaled, *grads, *extra)


def finish_kernel(keep, from_part, d_gate, d_up, d_down):
    hidden_units = d_gate.shape[1]
    whole = keep[...].astype(F32) + from_part[...].astype(F32)
    d_gate[...] = whole[:, :hidden_units]
    d_up[...] = whole[:, hidden_units : 2 * hidden_units]
    d_down[...] = whole[:, 2 * hidden_units :].T


def finish(keep, from_part):
    size, stacked = keep.shape
    hidden_units = stacked // 3
    sds = jax.ShapeDtypeStruct
    step = size // 4
    piece = lambda n: pl.BlockSpec((step, n), lambda i: (i, 0))
    return pl.pallas_call(
        finish_kernel,
        out_shape=[sds((size, hidden_units), F32), sds((size, hidden_units), F32), sds((hidden_units, size), F32)],
        grid=(size // step,),
        in_specs=[piece(stacked)] * 2,
        out_specs=[piece(hidden_units), piece(hidden_units), pl.BlockSpec((hidden_units, step), lambda i: (0, i))],
        cost_estimate=cost(1024, 1024),
        compiler_params=params(),
    )(keep, from_part)


Z, Y, CORES = 4, 2, 2


def pairs_of(move):
    out = []
    for z in range(Z):
        for y in range(Y):
            for c in range(CORES):
                to = move(z, y, c)
                if to is not None:
                    out.append(((z * Y + y) * CORES + c, (to[0] * Y + to[1]) * CORES + to[2]))
    return out


def along_z(table):
    return pairs_of(lambda z, y, c: (table[z], y, c) if z in table else None)


SWAP_CORE = pairs_of(lambda z, y, c: (z, y, 1 - c))
SWAP_Y = pairs_of(lambda z, y, c: (z, 1 - y, c))
OUTER = along_z({0: 1, 1: 0, 2: 3, 3: 2})
INNER = along_z({1: 2, 2: 1})
OUTWARD = along_z({1: 0, 2: 3})
SKIP_TO_INNER = along_z({0: 2, 3: 1})
SKIP_TO_OUTER = along_z({1: 3, 2: 0})
ENDS = along_z({0: 3, 3: 0})


def after(value, *others):
    return lax.optimization_barrier((value,) + others)[0]


def dense_body(tokens, d_output, combine, routes, gate_weight, up_weight, down_weight):
    experts = lax.axis_size("expert")
    part = lax.axis_index("dp")
    expert = lax.axis_index("expert")
    z = expert // (Y * CORES)
    inner = (z == 1) | (z == 2)
    scal = jnp.stack([part, expert]).astype(jnp.int32)
    mine = part[None].astype(jnp.int32)
    other = (1 - part)[None].astype(jnp.int32)

    move = lambda a, pairs: lax.ppermute(a, "expert", pairs)
    across = lambda a: lax.ppermute(a, "dp", [(0, 1), (1, 0)])

    swap = lambda a: move(a, SWAP_CORE)
    w_own = pack_weights(gate_weight[0], up_weight[0], down_weight[0])
    w_part = across(w_own)
    own = pack(experts, tokens, d_output, combine, routes)

    b1 = move(own, OUTER)
    f1 = move(own, INNER)
    y0 = move(own, SWAP_Y)
    w_core = swap(w_own)
    f2 = move(b1, INNER)
    y1 = move(after(b1, y0), SWAP_Y)
    g1 = move(f1, OUTWARD)
    b2 = jnp.where(inner, f1, g1)
    y2 = move(after(b2, y1, w_part), SWAP_Y)
    w_both = swap(w_part)
    weights = [w_own, w_part, w_core, w_both]
    g2 = move(f2, OUTWARD)
    p0, p1, q0, *kept_a = rows_call(experts, scal, [[own], [b1], [y0]], weights)
    b3 = jnp.where(inner, f2, after(g2, p0))
    y3 = move(after(b3, y2), SWAP_Y)
    p2, p3, q12, *kept_b = rows_call(experts, scal, [[b2], [b3], [y1, y2]], weights)

    blocks = [own, b1, y0, b2, b3, y1, y2]
    kept = [kept_a, kept_b]
    others = lambda side, first: half_call(side, [first] + blocks[1:], [k[2] for k in kept], [k[3] for k in kept])
    to_core = others(other, own)
    y3 = after(y3, p2, to_core)
    r12 = move(after(q12, y3), SWAP_Y)
    r0 = move(after(q0, y3), SWAP_Y)

    cy3 = swap(y3)
    last, pair, scaled_c, grads_c = rows_call(experts, scal, [[y3], [cy3]], weights[:2])
    q3 = last.astype(F32) + swap(pair).astype(F32)
    all_blocks = blocks + [y3, cy3]
    mine_of = lambda side, more: half_call(
        side, all_blocks, [k[0] for k in kept] + [scaled_c], [k[1] for k in kept] + [grads_c], more
    )
    send = mine_of(other, swap(to_core))
    from_part = across(send)
    keep = mine_of(mine, swap(others(mine, after(own, send))))

    rows = own.shape[0]
    r1, r2 = r12[:rows], r12[rows:]
    r3 = move(after(q3.astype(BF16), r0, r12), SWAP_Y)
    add = lambda *terms: sum(t.astype(F32) for t in terms).astype(BF16)
    s1 = add(p1, r1)
    s2 = add(p2, r2)
    s3 = add(p3, r3)
    d_tokens = add(
        p0,
        r0,
        move(s1, OUTER),
        move(s2, INNER),
        move(s2, SKIP_TO_INNER),
        move(s3, SKIP_TO_OUTER),
        move(s3, ENDS),
    )
    d_gate, d_up, d_down = finish(keep, from_part)
    return (d_tokens, d_gate[None], d_up[None], d_down[None])


def route_slots(routes, experts):
    matches = (routes[:, :, None] == jnp.arange(experts, dtype=jnp.int32)[None, None, :]).astype(
        jnp.int32
    )
    per_token = jnp.sum(matches, axis=1)
    earlier = jnp.cumsum(per_token, axis=0) - per_token
    return jnp.sum(matches * earlier[:, None, :], axis=2)


def row_work(row_inputs, row_grads, gate_up, down_matrix):
    hidden_units = down_matrix.shape[0]
    preact = jnp.dot(row_inputs, gate_up, preferred_element_type=jnp.float32)
    gate_pre = preact[:, :hidden_units]
    up_pre = preact[:, hidden_units:]
    gate_sigmoid = jax.nn.sigmoid(gate_pre)
    hidden = (gate_pre * gate_sigmoid * up_pre).astype(jnp.bfloat16)
    d_hidden = jnp.dot(row_grads, down_matrix.T, preferred_element_type=jnp.float32)
    d_gate_pre = d_hidden * up_pre * gate_sigmoid * (1.0 + gate_pre * (1.0 - gate_sigmoid))
    d_up_pre = d_hidden * gate_pre * gate_sigmoid
    d_preact = jnp.concatenate([d_gate_pre, d_up_pre], axis=1).astype(jnp.bfloat16)
    d_rows = jnp.dot(d_preact, gate_up.T, preferred_element_type=jnp.float32).astype(jnp.bfloat16)
    return (d_rows, hidden, d_preact)


def routed_body(tokens, d_output, combine, routes, gate_weight, up_weight, down_weight):
    experts = lax.axis_size("expert")
    tok_count = tokens.shape[0]
    model_width = tokens.shape[1]
    top_count = routes.shape[1]
    capacity = max(2, (9 * tok_count * top_count + 8 * experts - 1) // (8 * experts))
    slot_count = experts * capacity
    slot_index = route_slots(routes, experts)
    position = (routes * capacity + slot_index).reshape(-1)
    spread_inputs = jnp.repeat(tokens, top_count, axis=0)
    scaled = (
        (combine[:, :, None] * d_output[:, None, :].astype(jnp.float32))
        .astype(jnp.bfloat16)
        .reshape(-1, model_width)
    )
    send_inputs = (
        jnp.zeros((slot_count, model_width), jnp.bfloat16)
        .at[position]
        .set(spread_inputs)
        .reshape(experts, capacity, model_width)
    )
    send_grads = (
        jnp.zeros((slot_count, model_width), jnp.bfloat16)
        .at[position]
        .set(scaled)
        .reshape(experts, capacity, model_width)
    )
    whole_gate, whole_up, whole_down = (
        lax.all_gather(gate_weight, "dp", axis=1, tiled=True),
        lax.all_gather(up_weight, "dp", axis=1, tiled=True),
        lax.all_gather(down_weight, "dp", axis=2, tiled=True),
    )
    gate_up = jnp.concatenate([whole_gate[0], whole_up[0]], axis=1)
    down_matrix = whole_down[0]
    hidden_units = down_matrix.shape[0]
    recv_inputs, recv_grads = (
        lax.all_to_all(send_inputs, "expert", split_axis=0, concat_axis=0, tiled=True),
        lax.all_to_all(send_grads, "expert", split_axis=0, concat_axis=0, tiled=True),
    )
    flat_inputs = recv_inputs.reshape(-1, model_width)
    flat_grads = recv_grads.reshape(-1, model_width)
    d_rows, hidden, d_preact = row_work(flat_inputs, flat_grads, gate_up, down_matrix)
    returned = lax.all_to_all(
        d_rows.reshape(experts, capacity, model_width),
        "expert",
        split_axis=0,
        concat_axis=0,
        tiled=True,
    )
    route_rows = returned.reshape(-1, model_width)[position].reshape(
        tok_count, top_count, model_width
    )
    d_tokens = jnp.sum(route_rows.astype(jnp.float32), axis=1).astype(jnp.bfloat16)
    gate_up_grad = jnp.dot(flat_inputs.T, d_preact, preferred_element_type=jnp.float32)
    down_grad = jnp.dot(flat_grads.T, hidden, preferred_element_type=jnp.float32)
    stacked = jnp.concatenate([gate_up_grad, down_grad], axis=1)
    summed = lax.psum_scatter(
        stacked.astype(jnp.bfloat16), "dp", scatter_dimension=0, tiled=True
    ).astype(jnp.float32)
    d_gate_weight = summed[:, :hidden_units][None]
    d_up_weight = summed[:, hidden_units : 2 * hidden_units][None]
    d_down_weight = summed[:, 2 * hidden_units :].T[None]
    return (d_tokens, d_gate_weight, d_up_weight, d_down_weight)


def solution(mesh):
    placed = (
        P(("dp", "expert"), None),
        P(("dp", "expert"), None),
        P(("dp", "expert"), None),
        P(("dp", "expert"), None),
        P("expert", "dp", None),
        P("expert", "dp", None),
        P("expert", None, "dp"),
    )
    dense = mesh.shape["expert"] == Z * Y * CORES and mesh.shape["dp"] == 2
    return jax.shard_map(
        dense_body if dense else routed_body,
        mesh=mesh,
        in_specs=placed,
        out_specs=(
            P(("dp", "expert"), None),
            P("expert", "dp", None),
            P("expert", "dp", None),
            P("expert", None, "dp"),
        ),
        check_vma=False,
    )
```

```python
import functools

import jax
import jax.numpy as jnp
from jax import lax
from jax.experimental import pallas as pl
from jax.experimental.pallas import tpu as pltpu
from jax.sharding import PartitionSpec as P

F32 = jnp.float32
BF16 = jnp.bfloat16
LANES = 128
VMEM_BYTES = 56 * 1024 * 1024


def vmem():
    return pl.BlockSpec(memory_space=pltpu.VMEM)


def smem():
    return pl.BlockSpec(memory_space=pltpu.SMEM)


def hbm():
    return pl.BlockSpec(memory_space=pl.ANY)


def params():
    return pltpu.CompilerParams(vmem_limit_bytes=VMEM_BYTES)


def cost(flops, moved):
    return pl.CostEstimate(flops=int(flops), bytes_accessed=int(moved), transcendentals=0)


def dot(a, b, dims):
    return lax.dot_general(a, b, (dims, ((), ())), preferred_element_type=F32)


def pack_kernel(experts, tokens, d_output, combine, routes, out):
    rows, width = tokens.shape
    out[:, :width] = tokens[...]
    out[:, width : 2 * width] = d_output[...]
    line = lax.broadcasted_iota(jnp.int32, (LANES, rows), 0)
    expert = lax.rem(line, experts)
    dense = jnp.zeros((LANES, rows), F32)
    for k in range(routes.shape[0]):
        dense = dense + jnp.where(expert == routes[k : k + 1, :], combine[k : k + 1, :], 0.0)
    high = dense.astype(BF16).astype(F32)
    rest = dense - high
    middle = rest.astype(BF16).astype(F32)
    low = rest - middle
    parts = jnp.where(
        line < experts,
        high,
        jnp.where(line < 2 * experts, middle, jnp.where(line < 3 * experts, low, 0.0)),
    )
    out[:, 2 * width :] = parts.T.astype(BF16)


def pack(experts, tokens, d_output, combine, routes):
    rows, width = tokens.shape
    return pl.pallas_call(
        functools.partial(pack_kernel, experts),
        out_shape=jax.ShapeDtypeStruct((rows, 2 * width + LANES), BF16),
        in_specs=[vmem()] * 4,
        out_specs=vmem(),
        cost_estimate=cost(0, 3 * rows * width * 2 * 2),
        compiler_params=params(),
    )(tokens, d_output, combine.T, routes.T)


def pack_weights_kernel(gate, up, down, out):
    hidden_units = gate.shape[1]
    out[:, :hidden_units] = gate[...]
    out[:, hidden_units : 2 * hidden_units] = up[...]
    out[:, 2 * hidden_units :] = down[...].T


def pack_weights(gate, up, down):
    size, hidden_units = gate.shape
    return pl.pallas_call(
        pack_weights_kernel,
        out_shape=jax.ShapeDtypeStruct((size, 3 * hidden_units), BF16),
        in_specs=[vmem()] * 3,
        out_specs=vmem(),
        cost_estimate=cost(0, 6 * size * hidden_units * 4),
        compiler_params=params(),
    )(gate, up, down)


def rows_kernel(experts, count, merged, joined, scal, *refs):
    refs = list(refs)
    blocks = [refs.pop(0) for _ in range(count)]
    sets = 4
    raw = [refs.pop(0) for _ in range(sets)]
    out_rows = [refs.pop(0) for _ in range(merged)]
    kept = [refs.pop(0) for _ in range(3 if joined else 4)]
    held, total, sems = refs
    part, expert = scal[0], scal[1]
    size = raw[0].shape[0]
    hidden_units = raw[0].shape[1] // 3
    both = 2 * hidden_units
    width = 2 * size
    rows = blocks[0].shape[0]
    copies = [pltpu.make_async_copy(raw[i], held.at[i], sems.at[i]) for i in range(sets)]
    for c in copies:
        c.start()
    sides = [pl.multiple_of(part * size, size), pl.multiple_of((1 - part) * size, size)]
    parts = jnp.concatenate([b[:, 2 * width :] for b in blocks], axis=0).astype(F32)
    lane = lax.broadcasted_iota(jnp.int32, parts.shape, 1)
    toks = [jnp.concatenate([b[:, pl.ds(at, size)] for b in blocks], axis=0) for at in sides]
    for which in range(sets // 2):
        grads_out = kept[2 * which]
        scaled_out, scaled_at = (grads_out, 3 * hidden_units) if joined and which == 1 else (kept[2 * which + 1], 0)
        for c in copies[2 * which : 2 * which + 2]:
            c.wait()
        wanted = expert if which == 0 else expert + 1 - 2 * lax.rem(expert, 2)
        mine = (lax.rem(lane, experts) == wanted) & (lane < 3 * experts)
        weight = jnp.sum(jnp.where(mine, parts, 0.0), axis=1, keepdims=True)
        preact = None
        d_hidden = None
        for side in range(2):
            at = sides[side]
            grad_at = pl.multiple_of(width + at, size)
            grad = jnp.concatenate([b[:, pl.ds(grad_at, size)] for b in blocks], axis=0)
            scaled = (weight * grad.astype(F32)).astype(BF16)
            scaled_out[:, pl.ds(pl.multiple_of(scaled_at + at, LANES), size)] = scaled
            if joined and which == 1:
                grads_out[:, pl.ds(pl.multiple_of(3 * hidden_units + width + at, LANES), size)] = toks[side]
            p = dot(toks[side], held[2 * which + side, :, :both], ((1,), (0,)))
            h = dot(scaled, held[2 * which + side, :, both:], ((1,), (0,)))
            preact = p if side == 0 else preact + p
            d_hidden = h if side == 0 else d_hidden + h
        gate_pre = preact[:, :hidden_units]
        up_pre = preact[:, hidden_units:]
        sig = jax.nn.sigmoid(gate_pre)
        silu = gate_pre * sig
        d_gate = (d_hidden * up_pre * sig * (1.0 + gate_pre * (1.0 - sig))).astype(BF16)
        d_up = (d_hidden * silu).astype(BF16)
        grads_out[:, :hidden_units] = d_gate
        grads_out[:, hidden_units:both] = d_up
        grads_out[:, both : both + hidden_units] = (silu * up_pre).astype(BF16)
        d_preact = jnp.concatenate([d_gate, d_up], axis=1)
        for side in range(2):
            at = sides[side]
            d_rows = dot(d_preact, held[2 * which + side, :, :both], ((1,), (1,)))
            if which > 0:
                d_rows = d_rows + total[:, pl.ds(at, size)]
            if which + 1 < sets // 2:
                total[:, pl.ds(at, size)] = d_rows
            else:
                d_rows = d_rows.astype(BF16)
                row = 0
                for out in out_rows:
                    out[:, pl.ds(at, size)] = d_rows[row : row + out.shape[0]]
                    row += out.shape[0]


def rows_call(experts, scal, groups, weights, joined=False):
    blocks = [b for group in groups for b in group]
    count, sets = len(blocks), len(weights)
    rows = blocks[0].shape[0]
    size, stacked = weights[0].shape
    total = count * rows
    sds = jax.ShapeDtypeStruct
    out = [sds((len(group) * rows, 2 * size), BF16) for group in groups]
    out += [sds((total, stacked), BF16), sds((total, 2 * size), BF16)]
    out += [sds((total, stacked + 4 * size), BF16)] if joined else out[-2:]
    return pl.pallas_call(
        functools.partial(rows_kernel, experts, count, len(groups), joined),
        out_shape=out,
        in_specs=[smem()] + [vmem()] * count + [hbm()] * sets,
        out_specs=[vmem()] * len(out),
        scratch_shapes=[
            pltpu.VMEM((sets, size, stacked), BF16),
            pltpu.VMEM((total, 2 * size), F32),
            pltpu.SemaphoreType.DMA((sets,)),
        ],
        cost_estimate=cost(24 * total * size * stacked * sets // 2 * (10 if joined else 1), 1 << 20),
        compiler_params=params(),
    )(scal, *blocks, *weights)


def half_kernel(count, groups, joined, adds, sides, *refs):
    refs = list(refs)
    side = sides[pl.program_id(0)]
    toks = [refs.pop(0) for _ in range(count)]
    scaled = [refs.pop(0) for _ in range(groups)]
    made = [refs.pop(0) for _ in range(groups)]
    last = refs.pop(0) if joined else None
    more = refs.pop(0) if adds else None
    out = refs.pop(0)
    size, stacked = out.shape
    both = stacked // 3 * 2
    for kind in range(2):
        rows = [r[...] for r in (toks if kind == 0 else scaled)]
        span = slice(0, both) if kind == 0 else slice(both, stacked)
        cols = [g[:, span] for g in made]
        if joined:
            cols.append(last[:, span])
            first = stacked + (2 * size if kind == 0 else 0)
            rows.append(last[:, pl.ds(pl.multiple_of(first + side * size, LANES), size)])
        new = dot(jnp.concatenate(rows, axis=0), jnp.concatenate(cols, axis=0), ((0,), (0,)))
        if adds:
            new = new + more[:, span].astype(F32)
        out[:, span] = new.astype(BF16)


def half_call(sides, blocks, kept, last=None, more=None):
    grads, scaled = [k[0] for k in kept], [k[1] for k in kept]
    size = scaled[0].shape[1] // 2
    stacked = grads[0].shape[1]
    half = lambda a: pl.BlockSpec((a.shape[0], size), lambda i, s: (0, s[i]))
    whole = lambda a: pl.BlockSpec(a.shape, lambda i, s: (0, 0))
    operands = [*blocks, *scaled, *grads]
    specs = [half(a) for a in (*blocks, *scaled)] + [whole(g) for g in grads]
    if last is not None:
        operands.append(last)
        specs.append(whole(last))
    if more is not None:
        operands.append(more)
        specs.append(pl.BlockSpec((size, stacked), lambda i, s: (s[i], 0)))
    count = sides.shape[0]
    return pl.pallas_call(
        functools.partial(half_kernel, len(blocks), len(kept), last is not None, more is not None),
        out_shape=jax.ShapeDtypeStruct((count * size, stacked), BF16),
        grid_spec=pltpu.PrefetchScalarGridSpec(
            num_scalar_prefetch=1,
            grid=(count,),
            in_specs=specs,
            out_specs=pl.BlockSpec((size, stacked), lambda i, s: (i, 0)),
        ),
        cost_estimate=cost(1024, 1024),
        compiler_params=params(),
    )(sides, *operands)


def finish_kernel(keep, from_part, d_gate, d_up, d_down):
    hidden_units = d_gate.shape[1]
    whole = keep[...].astype(F32) + from_part[...].astype(F32)
    d_gate[...] = whole[:, :hidden_units]
    d_up[...] = whole[:, hidden_units : 2 * hidden_units]
    d_down[...] = whole[:, 2 * hidden_units :].T


def finish(keep, from_part):
    size, stacked = keep.shape
    hidden_units = stacked // 3
    sds = jax.ShapeDtypeStruct
    step = size // 4
    piece = lambda n: pl.BlockSpec((step, n), lambda i: (i, 0))
    return pl.pallas_call(
        finish_kernel,
        out_shape=[sds((size, hidden_units), F32), sds((size, hidden_units), F32), sds((hidden_units, size), F32)],
        grid=(size // step,),
        in_specs=[piece(stacked)] * 2,
        out_specs=[piece(hidden_units), piece(hidden_units), pl.BlockSpec((hidden_units, step), lambda i: (0, i))],
        cost_estimate=cost(1024, 1024),
        compiler_params=params(),
    )(keep, from_part)


Z, Y, CORES = 4, 2, 2


def pairs_of(move):
    out = []
    for z in range(Z):
        for y in range(Y):
            for c in range(CORES):
                to = move(z, y, c)
                if to is not None:
                    out.append(((z * Y + y) * CORES + c, (to[0] * Y + to[1]) * CORES + to[2]))
    return out


def along_z(table):
    return pairs_of(lambda z, y, c: (table[z], y, c) if z in table else None)


SWAP_CORE = pairs_of(lambda z, y, c: (z, y, 1 - c))
SWAP_Y = pairs_of(lambda z, y, c: (z, 1 - y, c))
OUTER = along_z({0: 1, 1: 0, 2: 3, 3: 2})
INNER = along_z({1: 2, 2: 1})
OUTWARD = along_z({1: 0, 2: 3})
SKIP_TO_INNER = along_z({0: 2, 3: 1})
SKIP_TO_OUTER = along_z({1: 3, 2: 0})
ENDS = along_z({0: 3, 3: 0})


def after(value, *others):
    return lax.optimization_barrier((value,) + others)[0]


def dense_body(tokens, d_output, combine, routes, gate_weight, up_weight, down_weight):
    experts = lax.axis_size("expert")
    part = lax.axis_index("dp")
    expert = lax.axis_index("expert")
    z = expert // (Y * CORES)
    inner = (z == 1) | (z == 2)
    scal = jnp.stack([part, expert]).astype(jnp.int32)
    mine = part[None].astype(jnp.int32)
    other = (1 - part)[None].astype(jnp.int32)
    sides = jnp.arange(2, dtype=jnp.int32)

    move = lambda a, pairs: lax.ppermute(a, "expert", pairs)
    across = lambda a: lax.ppermute(a, "dp", [(0, 1), (1, 0)])

    swap = lambda a: move(a, SWAP_CORE)
    own = pack(experts, tokens, d_output, combine, routes)
    w_own = pack_weights(after(gate_weight[0], own), up_weight[0], down_weight[0])
    w_part = across(w_own)

    b1 = move(own, OUTER)
    f1 = move(own, INNER)
    y0 = move(own, SWAP_Y)
    f2 = move(b1, INNER)
    y1 = move(after(b1, y0), SWAP_Y)
    g1 = move(f1, OUTWARD)
    b2 = jnp.where(inner, f1, g1)
    y2 = move(after(b2, y1, f2), SWAP_Y)
    g2 = move(f2, OUTWARD)

    w_core = swap(after(w_own, y1, f2))
    w_both = swap(after(w_part, y1, f2))
    weights = [w_own, w_part, w_core, w_both]
    p0, p1, q0, *kept_a = rows_call(experts, scal, [[own], [b1], [y0]], weights)
    b3 = jnp.where(inner, f2, after(g2, p0))
    y3 = move(after(b3, y2), SWAP_Y)
    p2, p3, q1, *kept_b = rows_call(experts, scal, [[b2], [b3], [y1]], weights)
    q2, *kept_c = rows_call(experts, scal, [[after(y2, p2)]], weights)

    blocks = [own, b1, y0, b2, b3, y1, y2]
    kept = [kept_a, kept_b, kept_c]
    to_core = half_call(sides, blocks, [k[2:] for k in kept])
    y3 = after(y3, q2, to_core)
    r0, r1, r2 = (move(after(q, y3), SWAP_Y) for q in (q0, q1, q2))

    q3, *kept_d, joined = rows_call(experts, scal, [[y3]], weights, joined=True)
    last = swap(joined)
    r3 = move(after(q3, r0), SWAP_Y)
    all_blocks = blocks + [y3]
    all_kept = [k[:2] for k in kept] + [kept_d]
    got = swap(to_core)
    send = half_call(other, all_blocks, all_kept, last, got)
    from_part = across(send)
    keep = half_call(after(mine, send), all_blocks, all_kept, last, got)

    add = lambda *terms: sum(t.astype(F32) for t in terms).astype(BF16)
    s1 = add(p1, r1)
    s2 = add(p2, r2)
    s3 = add(p3, r3)
    d_tokens = add(
        p0,
        r0,
        move(s1, OUTER),
        move(s2, INNER),
        move(s2, SKIP_TO_INNER),
        move(s3, SKIP_TO_OUTER),
        move(s3, ENDS),
    )
    d_gate, d_up, d_down = finish(keep, from_part)
    return (d_tokens, d_gate[None], d_up[None], d_down[None])


def route_slots(routes, experts):
    matches = (routes[:, :, None] == jnp.arange(experts, dtype=jnp.int32)[None, None, :]).astype(
        jnp.int32
    )
    per_token = jnp.sum(matches, axis=1)
    earlier = jnp.cumsum(per_token, axis=0) - per_token
    return jnp.sum(matches * earlier[:, None, :], axis=2)


def row_work(row_inputs, row_grads, gate_up, down_matrix):
    hidden_units = down_matrix.shape[0]
    preact = jnp.dot(row_inputs, gate_up, preferred_element_type=jnp.float32)
    gate_pre = preact[:, :hidden_units]
    up_pre = preact[:, hidden_units:]
    gate_sigmoid = jax.nn.sigmoid(gate_pre)
    hidden = (gate_pre * gate_sigmoid * up_pre).astype(jnp.bfloat16)
    d_hidden = jnp.dot(row_grads, down_matrix.T, preferred_element_type=jnp.float32)
    d_gate_pre = d_hidden * up_pre * gate_sigmoid * (1.0 + gate_pre * (1.0 - gate_sigmoid))
    d_up_pre = d_hidden * gate_pre * gate_sigmoid
    d_preact = jnp.concatenate([d_gate_pre, d_up_pre], axis=1).astype(jnp.bfloat16)
    d_rows = jnp.dot(d_preact, gate_up.T, preferred_element_type=jnp.float32).astype(jnp.bfloat16)
    return (d_rows, hidden, d_preact)


def routed_body(tokens, d_output, combine, routes, gate_weight, up_weight, down_weight):
    experts = lax.axis_size("expert")
    tok_count = tokens.shape[0]
    model_width = tokens.shape[1]
    top_count = routes.shape[1]
    capacity = max(2, (9 * tok_count * top_count + 8 * experts - 1) // (8 * experts))
    slot_count = experts * capacity
    slot_index = route_slots(routes, experts)
    position = (routes * capacity + slot_index).reshape(-1)
    spread_inputs = jnp.repeat(tokens, top_count, axis=0)
    scaled = (
        (combine[:, :, None] * d_output[:, None, :].astype(jnp.float32))
        .astype(jnp.bfloat16)
        .reshape(-1, model_width)
    )
    send_inputs = (
        jnp.zeros((slot_count, model_width), jnp.bfloat16)
        .at[position]
        .set(spread_inputs)
        .reshape(experts, capacity, model_width)
    )
    send_grads = (
        jnp.zeros((slot_count, model_width), jnp.bfloat16)
        .at[position]
        .set(scaled)
        .reshape(experts, capacity, model_width)
    )
    whole_gate, whole_up, whole_down = (
        lax.all_gather(gate_weight, "dp", axis=1, tiled=True),
        lax.all_gather(up_weight, "dp", axis=1, tiled=True),
        lax.all_gather(down_weight, "dp", axis=2, tiled=True),
    )
    gate_up = jnp.concatenate([whole_gate[0], whole_up[0]], axis=1)
    down_matrix = whole_down[0]
    hidden_units = down_matrix.shape[0]
    recv_inputs, recv_grads = (
        lax.all_to_all(send_inputs, "expert", split_axis=0, concat_axis=0, tiled=True),
        lax.all_to_all(send_grads, "expert", split_axis=0, concat_axis=0, tiled=True),
    )
    flat_inputs = recv_inputs.reshape(-1, model_width)
    flat_grads = recv_grads.reshape(-1, model_width)
    d_rows, hidden, d_preact = row_work(flat_inputs, flat_grads, gate_up, down_matrix)
    returned = lax.all_to_all(
        d_rows.reshape(experts, capacity, model_width),
        "expert",
        split_axis=0,
        concat_axis=0,
        tiled=True,
    )
    route_rows = returned.reshape(-1, model_width)[position].reshape(
        tok_count, top_count, model_width
    )
    d_tokens = jnp.sum(route_rows.astype(jnp.float32), axis=1).astype(jnp.bfloat16)
    gate_up_grad = jnp.dot(flat_inputs.T, d_preact, preferred_element_type=jnp.float32)
    down_grad = jnp.dot(flat_grads.T, hidden, preferred_element_type=jnp.float32)
    stacked = jnp.concatenate([gate_up_grad, down_grad], axis=1)
    summed = lax.psum_scatter(
        stacked.astype(jnp.bfloat16), "dp", scatter_dimension=0, tiled=True
    ).astype(jnp.float32)
    d_gate_weight = summed[:, :hidden_units][None]
    d_up_weight = summed[:, hidden_units : 2 * hidden_units][None]
    d_down_weight = summed[:, 2 * hidden_units :].T[None]
    return (d_tokens, d_gate_weight, d_up_weight, d_down_weight)


def solution(mesh):
    placed = (
        P(("dp", "expert"), None),
        P(("dp", "expert"), None),
        P(("dp", "expert"), None),
        P(("dp", "expert"), None),
        P("expert", "dp", None),
        P("expert", "dp", None),
        P("expert", None, "dp"),
    )
    dense = mesh.shape["expert"] == Z * Y * CORES and mesh.shape["dp"] == 2
    return jax.shard_map(
        dense_body if dense else routed_body,
        mesh=mesh,
        in_specs=placed,
        out_specs=(
            P(("dp", "expert"), None),
            P("expert", "dp", None),
            P("expert", "dp", None),
            P("expert", None, "dp"),
        ),
        check_vma=False,
    )
```

```python
import functools

import jax
import jax.numpy as jnp
from jax import lax
from jax.experimental import pallas as pl
from jax.experimental.pallas import tpu as pltpu
from jax.sharding import PartitionSpec as P

F32 = jnp.float32
BF16 = jnp.bfloat16
LANES = 128
VMEM_BYTES = 56 * 1024 * 1024


def vmem():
    return pl.BlockSpec(memory_space=pltpu.VMEM)


def smem():
    return pl.BlockSpec(memory_space=pltpu.SMEM)


def hbm():
    return pl.BlockSpec(memory_space=pl.ANY)


def params():
    return pltpu.CompilerParams(vmem_limit_bytes=VMEM_BYTES)


def cost(flops, moved):
    return pl.CostEstimate(flops=int(flops), bytes_accessed=int(moved), transcendentals=0)


def dot(a, b, dims):
    return lax.dot_general(a, b, (dims, ((), ())), preferred_element_type=F32)


def pack_kernel(experts, tokens, d_output, combine, routes, out):
    rows, width = tokens.shape
    out[:, :width] = tokens[...]
    out[:, width : 2 * width] = d_output[...]
    line = lax.broadcasted_iota(jnp.int32, (LANES, rows), 0)
    expert = lax.rem(line, experts)
    dense = jnp.zeros((LANES, rows), F32)
    for k in range(routes.shape[0]):
        dense = dense + jnp.where(expert == routes[k : k + 1, :], combine[k : k + 1, :], 0.0)
    high = dense.astype(BF16).astype(F32)
    rest = dense - high
    middle = rest.astype(BF16).astype(F32)
    low = rest - middle
    parts = jnp.where(
        line < experts,
        high,
        jnp.where(line < 2 * experts, middle, jnp.where(line < 3 * experts, low, 0.0)),
    )
    out[:, 2 * width :] = parts.T.astype(BF16)


def pack(experts, tokens, d_output, combine, routes):
    rows, width = tokens.shape
    return pl.pallas_call(
        functools.partial(pack_kernel, experts),
        out_shape=jax.ShapeDtypeStruct((rows, 2 * width + LANES), BF16),
        in_specs=[vmem()] * 4,
        out_specs=vmem(),
        cost_estimate=cost(0, 3 * rows * width * 2 * 2),
        compiler_params=params(),
    )(tokens, d_output, combine.T, routes.T)


def pack_weights_kernel(gate, up, down, out):
    hidden_units = gate.shape[1]
    out[:, :hidden_units] = gate[...]
    out[:, hidden_units : 2 * hidden_units] = up[...]
    out[:, 2 * hidden_units :] = down[...].T


def pack_weights(gate, up, down):
    size, hidden_units = gate.shape
    return pl.pallas_call(
        pack_weights_kernel,
        out_shape=jax.ShapeDtypeStruct((size, 3 * hidden_units), BF16),
        in_specs=[vmem()] * 3,
        out_specs=vmem(),
        cost_estimate=cost(0, 6 * size * hidden_units * 4),
        compiler_params=params(),
    )(gate, up, down)


def rows_kernel(experts, count, merged, joined, scal, *refs):
    refs = list(refs)
    blocks = [refs.pop(0) for _ in range(count)]
    sets = 4
    raw = [refs.pop(0) for _ in range(sets)]
    out_rows = [refs.pop(0) for _ in range(merged)]
    kept = [refs.pop(0) for _ in range(3 if joined else 4)]
    held, total, sems = refs
    part, expert = scal[0], scal[1]
    size = raw[0].shape[0]
    hidden_units = raw[0].shape[1] // 3
    both = 2 * hidden_units
    width = 2 * size
    rows = blocks[0].shape[0]
    copies = [pltpu.make_async_copy(raw[i], held.at[i], sems.at[i]) for i in range(sets)]
    for c in copies:
        c.start()
    sides = [pl.multiple_of(part * size, size), pl.multiple_of((1 - part) * size, size)]
    parts = jnp.concatenate([b[:, 2 * width :] for b in blocks], axis=0).astype(F32)
    lane = lax.broadcasted_iota(jnp.int32, parts.shape, 1)
    toks = [jnp.concatenate([b[:, pl.ds(at, size)] for b in blocks], axis=0) for at in sides]
    for which in range(sets // 2):
        grads_out = kept[2 * which]
        scaled_out, scaled_at = (grads_out, 3 * hidden_units) if joined and which == 1 else (kept[2 * which + 1], 0)
        for c in copies[2 * which : 2 * which + 2]:
            c.wait()
        wanted = expert if which == 0 else expert + 1 - 2 * lax.rem(expert, 2)
        mine = (lax.rem(lane, experts) == wanted) & (lane < 3 * experts)
        weight = jnp.sum(jnp.where(mine, parts, 0.0), axis=1, keepdims=True)
        preact = None
        d_hidden = None
        for side in range(2):
            at = sides[side]
            grad_at = pl.multiple_of(width + at, size)
            grad = jnp.concatenate([b[:, pl.ds(grad_at, size)] for b in blocks], axis=0)
            scaled = (weight * grad.astype(F32)).astype(BF16)
            scaled_out[:, pl.ds(pl.multiple_of(scaled_at + at, LANES), size)] = scaled
            if joined and which == 1:
                grads_out[:, pl.ds(pl.multiple_of(3 * hidden_units + width + at, LANES), size)] = toks[side]
            p = dot(toks[side], held[2 * which + side, :, :both], ((1,), (0,)))
            h = dot(scaled, held[2 * which + side, :, both:], ((1,), (0,)))
            preact = p if side == 0 else preact + p
            d_hidden = h if side == 0 else d_hidden + h
        gate_pre = preact[:, :hidden_units]
        up_pre = preact[:, hidden_units:]
        sig = jax.nn.sigmoid(gate_pre)
        silu = gate_pre * sig
        d_gate = (d_hidden * up_pre * sig * (1.0 + gate_pre * (1.0 - sig))).astype(BF16)
        d_up = (d_hidden * silu).astype(BF16)
        grads_out[:, :hidden_units] = d_gate
        grads_out[:, hidden_units:both] = d_up
        grads_out[:, both : both + hidden_units] = (silu * up_pre).astype(BF16)
        d_preact = jnp.concatenate([d_gate, d_up], axis=1)
        for side in range(2):
            at = sides[side]
            d_rows = dot(d_preact, held[2 * which + side, :, :both], ((1,), (1,)))
            if which > 0:
                d_rows = d_rows + total[:, pl.ds(at, size)]
            if which + 1 < sets // 2:
                total[:, pl.ds(at, size)] = d_rows
            else:
                d_rows = d_rows.astype(BF16)
                row = 0
                for out in out_rows:
                    out[:, pl.ds(at, size)] = d_rows[row : row + out.shape[0]]
                    row += out.shape[0]


def rows_call(experts, scal, groups, weights, joined=False):
    blocks = [b for group in groups for b in group]
    count, sets = len(blocks), len(weights)
    rows = blocks[0].shape[0]
    size, stacked = weights[0].shape
    total = count * rows
    sds = jax.ShapeDtypeStruct
    out = [sds((len(group) * rows, 2 * size), BF16) for group in groups]
    out += [sds((total, stacked), BF16), sds((total, 2 * size), BF16)]
    out += [sds((total, stacked + 4 * size), BF16)] if joined else out[-2:]
    return pl.pallas_call(
        functools.partial(rows_kernel, experts, count, len(groups), joined),
        out_shape=out,
        in_specs=[smem()] + [vmem()] * count + [hbm()] * sets,
        out_specs=[vmem()] * len(out),
        scratch_shapes=[
            pltpu.VMEM((sets, size, stacked), BF16),
            pltpu.VMEM((total, 2 * size), F32),
            pltpu.SemaphoreType.DMA((sets,)),
        ],
        cost_estimate=cost(24 * total * size * stacked * sets // 2 * (10 if joined else 1), 1 << 20),
        compiler_params=params(),
    )(scal, *blocks, *weights)


def half_kernel(count, groups, joined, adds, sides, *refs):
    refs = list(refs)
    side = sides[pl.program_id(0)]
    toks = [refs.pop(0) for _ in range(count)]
    scaled = [refs.pop(0) for _ in range(groups)]
    made = [refs.pop(0) for _ in range(groups)]
    last = refs.pop(0) if joined else None
    more = refs.pop(0) if adds else None
    out = refs.pop(0)
    size, stacked = out.shape
    both = stacked // 3 * 2
    for kind in range(2):
        rows = [r[...] for r in (toks if kind == 0 else scaled)]
        span = slice(0, both) if kind == 0 else slice(both, stacked)
        cols = [g[:, span] for g in made]
        if joined:
            cols.append(last[:, span])
            first = stacked + (2 * size if kind == 0 else 0)
            rows.append(last[:, pl.ds(pl.multiple_of(first + side * size, LANES), size)])
        new = dot(jnp.concatenate(rows, axis=0), jnp.concatenate(cols, axis=0), ((0,), (0,)))
        if adds:
            new = new + more[:, span].astype(F32)
        out[:, span] = new.astype(BF16)


def half_call(sides, blocks, kept, last=None, more=None, weight=0):
    grads, scaled = [k[0] for k in kept], [k[1] for k in kept]
    size = scaled[0].shape[1] // 2
    stacked = grads[0].shape[1]
    half = lambda a: pl.BlockSpec((a.shape[0], size), lambda i, s: (0, s[i]))
    whole = lambda a: pl.BlockSpec(a.shape, lambda i, s: (0, 0))
    operands = [*blocks, *scaled, *grads]
    specs = [half(a) for a in (*blocks, *scaled)] + [whole(g) for g in grads]
    if last is not None:
        operands.append(last)
        specs.append(whole(last))
    if more is not None:
        operands.append(more)
        specs.append(pl.BlockSpec((size, stacked), lambda i, s: (i, 0)))
    count = sides.shape[0]
    return pl.pallas_call(
        functools.partial(half_kernel, len(blocks), len(kept), last is not None, more is not None),
        out_shape=jax.ShapeDtypeStruct((count * size, stacked), BF16),
        grid_spec=pltpu.PrefetchScalarGridSpec(
            num_scalar_prefetch=1,
            grid=(count,),
            in_specs=specs,
            out_specs=pl.BlockSpec((size, stacked), lambda i, s: (i, 0)),
        ),
        cost_estimate=cost(8 * weight * size * stacked * 1024 + 1024, 1024),
        compiler_params=params(),
    )(sides, *operands)


def finish_kernel(keep, from_part, d_gate, d_up, d_down):
    hidden_units = d_gate.shape[1]
    whole = keep[...].astype(F32) + from_part[...].astype(F32)
    d_gate[...] = whole[:, :hidden_units]
    d_up[...] = whole[:, hidden_units : 2 * hidden_units]
    d_down[...] = whole[:, 2 * hidden_units :].T


def finish(keep, from_part):
    size, stacked = keep.shape
    hidden_units = stacked // 3
    sds = jax.ShapeDtypeStruct
    step = size // 4
    piece = lambda n: pl.BlockSpec((step, n), lambda i: (i, 0))
    return pl.pallas_call(
        finish_kernel,
        out_shape=[sds((size, hidden_units), F32), sds((size, hidden_units), F32), sds((hidden_units, size), F32)],
        grid=(size // step,),
        in_specs=[piece(stacked)] * 2,
        out_specs=[piece(hidden_units), piece(hidden_units), pl.BlockSpec((hidden_units, step), lambda i: (0, i))],
        cost_estimate=cost(1024, 1024),
        compiler_params=params(),
    )(keep, from_part)


Z, Y, CORES = 4, 2, 2


def pairs_of(move):
    out = []
    for z in range(Z):
        for y in range(Y):
            for c in range(CORES):
                to = move(z, y, c)
                if to is not None:
                    out.append(((z * Y + y) * CORES + c, (to[0] * Y + to[1]) * CORES + to[2]))
    return out


def along_z(table):
    return pairs_of(lambda z, y, c: (table[z], y, c) if z in table else None)


SWAP_CORE = pairs_of(lambda z, y, c: (z, y, 1 - c))
SWAP_Y = pairs_of(lambda z, y, c: (z, 1 - y, c))
OUTER = along_z({0: 1, 1: 0, 2: 3, 3: 2})
INNER = along_z({1: 2, 2: 1})
OUTWARD = along_z({1: 0, 2: 3})
SKIP_TO_INNER = along_z({0: 2, 3: 1})
SKIP_TO_OUTER = along_z({1: 3, 2: 0})
ENDS = along_z({0: 3, 3: 0})


def after(value, *others):
    return lax.optimization_barrier((value,) + others)[0]


def dense_body(tokens, d_output, combine, routes, gate_weight, up_weight, down_weight):
    experts = lax.axis_size("expert")
    part = lax.axis_index("dp")
    expert = lax.axis_index("expert")
    z = expert // (Y * CORES)
    inner = (z == 1) | (z == 2)
    scal = jnp.stack([part, expert]).astype(jnp.int32)
    mine = part[None].astype(jnp.int32)
    other = (1 - part)[None].astype(jnp.int32)

    move = lambda a, pairs: lax.ppermute(a, "expert", pairs)
    across = lambda a: lax.ppermute(a, "dp", [(0, 1), (1, 0)])

    swap = lambda a: move(a, SWAP_CORE)
    own = pack(experts, tokens, d_output, combine, routes)
    w_own = pack_weights(after(gate_weight[0], own), up_weight[0], down_weight[0])
    w_part = across(w_own)

    b1 = move(own, OUTER)
    f1 = move(own, INNER)
    y0 = move(own, SWAP_Y)
    f2 = move(b1, INNER)
    y1 = move(after(b1, y0), SWAP_Y)
    g1 = move(f1, OUTWARD)
    b2 = jnp.where(inner, f1, g1)
    y2 = move(after(b2, y1, f2), SWAP_Y)
    g2 = move(f2, OUTWARD)

    w_core = swap(after(w_own, y1, f2))
    w_both = swap(after(w_part, y1, f2))
    weights = [w_own, w_part, w_core, w_both]
    p0, p1, p2, q0, *kept_a = rows_call(experts, scal, [[own], [b1], [b2], [y0]], weights)
    b3 = jnp.where(inner, f2, after(g2, p0))
    y3 = move(after(b3, y2), SWAP_Y)
    p3, q12, *kept_b = rows_call(experts, scal, [[b3], [y1, y2]], weights)

    blocks = [own, b1, b2, y0, b3, y1, y2]
    kept = [kept_a, kept_b]
    others = lambda side, first: half_call(side, [first] + blocks[1:], [k[2:] for k in kept])
    to_core = others(other, own)
    y3 = after(y3, q12, to_core)
    r12 = move(after(q12, y3), SWAP_Y)
    rows = own.shape[0]
    r1, r2 = r12[:rows], r12[rows:]

    q3, *kept_d, joined = rows_call(experts, scal, [[y3]], weights, joined=True)
    last = swap(joined)
    r3 = move(after(q3, r12), SWAP_Y)
    r0 = move(after(q0, r3), SWAP_Y)
    all_blocks = blocks + [y3]
    all_kept = [k[:2] for k in kept] + [kept_d]
    send = half_call(other, all_blocks, all_kept, last, swap(to_core), weight=1)
    from_part = across(send)
    from_core = swap(others(mine, after(own, send, r12)))
    keep = half_call(after(mine, send), all_blocks, all_kept, last, from_core)

    add = lambda *terms: sum(t.astype(F32) for t in terms).astype(BF16)
    s1 = add(p1, r1)
    s2 = add(p2, r2)
    s3 = add(p3, r3)
    d_tokens = add(
        after(p0, keep),
        r0,
        move(s1, OUTER),
        move(s2, INNER),
        move(s2, SKIP_TO_INNER),
        move(s3, SKIP_TO_OUTER),
        move(s3, ENDS),
    )
    d_gate, d_up, d_down = finish(keep, after(from_part, d_tokens))
    return (d_tokens, d_gate[None], d_up[None], d_down[None])


def route_slots(routes, experts):
    matches = (routes[:, :, None] == jnp.arange(experts, dtype=jnp.int32)[None, None, :]).astype(
        jnp.int32
    )
    per_token = jnp.sum(matches, axis=1)
    earlier = jnp.cumsum(per_token, axis=0) - per_token
    return jnp.sum(matches * earlier[:, None, :], axis=2)


def row_work(row_inputs, row_grads, gate_up, down_matrix):
    hidden_units = down_matrix.shape[0]
    preact = jnp.dot(row_inputs, gate_up, preferred_element_type=jnp.float32)
    gate_pre = preact[:, :hidden_units]
    up_pre = preact[:, hidden_units:]
    gate_sigmoid = jax.nn.sigmoid(gate_pre)
    hidden = (gate_pre * gate_sigmoid * up_pre).astype(jnp.bfloat16)
    d_hidden = jnp.dot(row_grads, down_matrix.T, preferred_element_type=jnp.float32)
    d_gate_pre = d_hidden * up_pre * gate_sigmoid * (1.0 + gate_pre * (1.0 - gate_sigmoid))
    d_up_pre = d_hidden * gate_pre * gate_sigmoid
    d_preact = jnp.concatenate([d_gate_pre, d_up_pre], axis=1).astype(jnp.bfloat16)
    d_rows = jnp.dot(d_preact, gate_up.T, preferred_element_type=jnp.float32).astype(jnp.bfloat16)
    return (d_rows, hidden, d_preact)


def routed_body(tokens, d_output, combine, routes, gate_weight, up_weight, down_weight):
    experts = lax.axis_size("expert")
    tok_count = tokens.shape[0]
    model_width = tokens.shape[1]
    top_count = routes.shape[1]
    capacity = max(2, (9 * tok_count * top_count + 8 * experts - 1) // (8 * experts))
    slot_count = experts * capacity
    slot_index = route_slots(routes, experts)
    position = (routes * capacity + slot_index).reshape(-1)
    spread_inputs = jnp.repeat(tokens, top_count, axis=0)
    scaled = (
        (combine[:, :, None] * d_output[:, None, :].astype(jnp.float32))
        .astype(jnp.bfloat16)
        .reshape(-1, model_width)
    )
    send_inputs = (
        jnp.zeros((slot_count, model_width), jnp.bfloat16)
        .at[position]
        .set(spread_inputs)
        .reshape(experts, capacity, model_width)
    )
    send_grads = (
        jnp.zeros((slot_count, model_width), jnp.bfloat16)
        .at[position]
        .set(scaled)
        .reshape(experts, capacity, model_width)
    )
    whole_gate, whole_up, whole_down = (
        lax.all_gather(gate_weight, "dp", axis=1, tiled=True),
        lax.all_gather(up_weight, "dp", axis=1, tiled=True),
        lax.all_gather(down_weight, "dp", axis=2, tiled=True),
    )
    gate_up = jnp.concatenate([whole_gate[0], whole_up[0]], axis=1)
    down_matrix = whole_down[0]
    hidden_units = down_matrix.shape[0]
    recv_inputs, recv_grads = (
        lax.all_to_all(send_inputs, "expert", split_axis=0, concat_axis=0, tiled=True),
        lax.all_to_all(send_grads, "expert", split_axis=0, concat_axis=0, tiled=True),
    )
    flat_inputs = recv_inputs.reshape(-1, model_width)
    flat_grads = recv_grads.reshape(-1, model_width)
    d_rows, hidden, d_preact = row_work(flat_inputs, flat_grads, gate_up, down_matrix)
    returned = lax.all_to_all(
        d_rows.reshape(experts, capacity, model_width),
        "expert",
        split_axis=0,
        concat_axis=0,
        tiled=True,
    )
    route_rows = returned.reshape(-1, model_width)[position].reshape(
        tok_count, top_count, model_width
    )
    d_tokens = jnp.sum(route_rows.astype(jnp.float32), axis=1).astype(jnp.bfloat16)
    gate_up_grad = jnp.dot(flat_inputs.T, d_preact, preferred_element_type=jnp.float32)
    down_grad = jnp.dot(flat_grads.T, hidden, preferred_element_type=jnp.float32)
    stacked = jnp.concatenate([gate_up_grad, down_grad], axis=1)
    summed = lax.psum_scatter(
        stacked.astype(jnp.bfloat16), "dp", scatter_dimension=0, tiled=True
    ).astype(jnp.float32)
    d_gate_weight = summed[:, :hidden_units][None]
    d_up_weight = summed[:, hidden_units : 2 * hidden_units][None]
    d_down_weight = summed[:, 2 * hidden_units :].T[None]
    return (d_tokens, d_gate_weight, d_up_weight, d_down_weight)


def solution(mesh):
    placed = (
        P(("dp", "expert"), None),
        P(("dp", "expert"), None),
        P(("dp", "expert"), None),
        P(("dp", "expert"), None),
        P("expert", "dp", None),
        P("expert", "dp", None),
        P("expert", None, "dp"),
    )
    dense = mesh.shape["expert"] == Z * Y * CORES and mesh.shape["dp"] == 2
    return jax.shard_map(
        dense_body if dense else routed_body,
        mesh=mesh,
        in_specs=placed,
        out_specs=(
            P(("dp", "expert"), None),
            P("expert", "dp", None),
            P("expert", "dp", None),
            P("expert", None, "dp"),
        ),
        check_vma=False,
    )
```

```python
import functools

import jax
import jax.numpy as jnp
from jax import lax
from jax.experimental import pallas as pl
from jax.experimental.pallas import tpu as pltpu
from jax.sharding import PartitionSpec as P

F32 = jnp.float32
BF16 = jnp.bfloat16
LANES = 128
VMEM_BYTES = 56 * 1024 * 1024


def vmem():
    return pl.BlockSpec(memory_space=pltpu.VMEM)


def smem():
    return pl.BlockSpec(memory_space=pltpu.SMEM)


def hbm():
    return pl.BlockSpec(memory_space=pl.ANY)


def params():
    return pltpu.CompilerParams(vmem_limit_bytes=VMEM_BYTES)


def cost(flops, moved):
    return pl.CostEstimate(flops=int(flops), bytes_accessed=int(moved), transcendentals=0)


def dot(a, b, dims):
    return lax.dot_general(a, b, (dims, ((), ())), preferred_element_type=F32)


def pack_kernel(experts, tokens, d_output, combine, routes, out):
    rows, width = tokens.shape
    out[:, :width] = tokens[...]
    out[:, width : 2 * width] = d_output[...]
    line = lax.broadcasted_iota(jnp.int32, (LANES, rows), 0)
    expert = lax.rem(line, experts)
    dense = jnp.zeros((LANES, rows), F32)
    for k in range(routes.shape[0]):
        dense = dense + jnp.where(expert == routes[k : k + 1, :], combine[k : k + 1, :], 0.0)
    high = dense.astype(BF16).astype(F32)
    rest = dense - high
    middle = rest.astype(BF16).astype(F32)
    low = rest - middle
    parts = jnp.where(
        line < experts,
        high,
        jnp.where(line < 2 * experts, middle, jnp.where(line < 3 * experts, low, 0.0)),
    )
    out[:, 2 * width :] = parts.T.astype(BF16)


def pack(experts, tokens, d_output, combine, routes):
    rows, width = tokens.shape
    return pl.pallas_call(
        functools.partial(pack_kernel, experts),
        out_shape=jax.ShapeDtypeStruct((rows, 2 * width + LANES), BF16),
        in_specs=[vmem()] * 4,
        out_specs=vmem(),
        cost_estimate=cost(0, 3 * rows * width * 2 * 2),
        compiler_params=params(),
    )(tokens, d_output, combine.T, routes.T)


def pack_weights_kernel(gate, up, down, out):
    hidden_units = gate.shape[1]
    out[:, :hidden_units] = gate[...]
    out[:, hidden_units : 2 * hidden_units] = up[...]
    out[:, 2 * hidden_units :] = down[...].T


def pack_weights(gate, up, down):
    size, hidden_units = gate.shape
    return pl.pallas_call(
        pack_weights_kernel,
        out_shape=jax.ShapeDtypeStruct((size, 3 * hidden_units), BF16),
        in_specs=[vmem()] * 3,
        out_specs=vmem(),
        cost_estimate=cost(0, 6 * size * hidden_units * 4),
        compiler_params=params(),
    )(gate, up, down)


def rows_kernel(experts, count, merged, joined, scal, *refs):
    refs = list(refs)
    blocks = [refs.pop(0) for _ in range(count)]
    sets = 4
    raw = [refs.pop(0) for _ in range(sets)]
    out_rows = [refs.pop(0) for _ in range(merged)]
    kept = [refs.pop(0) for _ in range(3 if joined else 4)]
    held, total, sems = refs
    part, expert = scal[0], scal[1]
    size = raw[0].shape[0]
    hidden_units = raw[0].shape[1] // 3
    both = 2 * hidden_units
    width = 2 * size
    rows = blocks[0].shape[0]
    copies = [pltpu.make_async_copy(raw[i], held.at[i], sems.at[i]) for i in range(sets)]
    for c in copies:
        c.start()
    sides = [pl.multiple_of(part * size, size), pl.multiple_of((1 - part) * size, size)]
    parts = jnp.concatenate([b[:, 2 * width :] for b in blocks], axis=0).astype(F32)
    lane = lax.broadcasted_iota(jnp.int32, parts.shape, 1)
    toks = [jnp.concatenate([b[:, pl.ds(at, size)] for b in blocks], axis=0) for at in sides]
    for which in range(sets // 2):
        grads_out = kept[2 * which]
        scaled_out, scaled_at = (grads_out, 3 * hidden_units) if joined and which == 1 else (kept[2 * which + 1], 0)
        for c in copies[2 * which : 2 * which + 2]:
            c.wait()
        wanted = expert if which == 0 else expert + 1 - 2 * lax.rem(expert, 2)
        mine = (lax.rem(lane, experts) == wanted) & (lane < 3 * experts)
        weight = jnp.sum(jnp.where(mine, parts, 0.0), axis=1, keepdims=True)
        preact = None
        d_hidden = None
        for side in range(2):
            at = sides[side]
            grad_at = pl.multiple_of(width + at, size)
            grad = jnp.concatenate([b[:, pl.ds(grad_at, size)] for b in blocks], axis=0)
            scaled = (weight * grad.astype(F32)).astype(BF16)
            scaled_out[:, pl.ds(pl.multiple_of(scaled_at + at, LANES), size)] = scaled
            if joined and which == 1:
                grads_out[:, pl.ds(pl.multiple_of(3 * hidden_units + width + at, LANES), size)] = toks[side]
            p = dot(toks[side], held[2 * which + side, :, :both], ((1,), (0,)))
            h = dot(scaled, held[2 * which + side, :, both:], ((1,), (0,)))
            preact = p if side == 0 else preact + p
            d_hidden = h if side == 0 else d_hidden + h
        gate_pre = preact[:, :hidden_units]
        up_pre = preact[:, hidden_units:]
        sig = jax.nn.sigmoid(gate_pre)
        silu = gate_pre * sig
        d_gate = (d_hidden * up_pre * sig * (1.0 + gate_pre * (1.0 - sig))).astype(BF16)
        d_up = (d_hidden * silu).astype(BF16)
        grads_out[:, :hidden_units] = d_gate
        grads_out[:, hidden_units:both] = d_up
        grads_out[:, both : both + hidden_units] = (silu * up_pre).astype(BF16)
        d_preact = jnp.concatenate([d_gate, d_up], axis=1)
        for side in range(2):
            at = sides[side]
            d_rows = dot(d_preact, held[2 * which + side, :, :both], ((1,), (1,)))
            if which > 0:
                d_rows = d_rows + total[:, pl.ds(at, size)]
            if which + 1 < sets // 2:
                total[:, pl.ds(at, size)] = d_rows
            else:
                d_rows = d_rows.astype(BF16)
                row = 0
                for out in out_rows:
                    out[:, pl.ds(at, size)] = d_rows[row : row + out.shape[0]]
                    row += out.shape[0]


def rows_call(experts, scal, groups, weights, joined=False):
    blocks = [b for group in groups for b in group]
    count, sets = len(blocks), len(weights)
    rows = blocks[0].shape[0]
    size, stacked = weights[0].shape
    total = count * rows
    sds = jax.ShapeDtypeStruct
    out = [sds((len(group) * rows, 2 * size), BF16) for group in groups]
    out += [sds((total, stacked), BF16), sds((total, 2 * size), BF16)]
    out += [sds((total, stacked + 4 * size), BF16)] if joined else out[-2:]
    return pl.pallas_call(
        functools.partial(rows_kernel, experts, count, len(groups), joined),
        out_shape=out,
        in_specs=[smem()] + [vmem()] * count + [hbm()] * sets,
        out_specs=[vmem()] * len(out),
        scratch_shapes=[
            pltpu.VMEM((sets, size, stacked), BF16),
            pltpu.VMEM((total, 2 * size), F32),
            pltpu.SemaphoreType.DMA((sets,)),
        ],
        cost_estimate=cost(24 * total * size * stacked * sets // 2 * (10 if joined else 1), 1 << 20),
        compiler_params=params(),
    )(scal, *blocks, *weights)


def half_kernel(count, groups, joined, adds, sides, *refs):
    refs = list(refs)
    side = sides[pl.program_id(0)]
    toks = [refs.pop(0) for _ in range(count)]
    scaled = [refs.pop(0) for _ in range(groups)]
    made = [refs.pop(0) for _ in range(groups)]
    last = refs.pop(0) if joined else None
    more = refs.pop(0) if adds else None
    out = refs.pop(0)
    size, stacked = out.shape
    both = stacked // 3 * 2
    for kind in range(2):
        rows = [r[...] for r in (toks if kind == 0 else scaled)]
        span = slice(0, both) if kind == 0 else slice(both, stacked)
        cols = [g[:, span] for g in made]
        if joined:
            cols.append(last[:, span])
            first = stacked + (2 * size if kind == 0 else 0)
            rows.append(last[:, pl.ds(pl.multiple_of(first + side * size, LANES), size)])
        new = dot(jnp.concatenate(rows, axis=0), jnp.concatenate(cols, axis=0), ((0,), (0,)))
        if adds:
            new = new + more[:, span].astype(F32)
        out[:, span] = new.astype(BF16)


def half_call(sides, blocks, kept, last=None, more=None, at=0, weight=0):
    grads, scaled = [k[0] for k in kept], [k[1] for k in kept]
    size = scaled[0].shape[1] // 2
    stacked = grads[0].shape[1]
    half = lambda a: pl.BlockSpec((a.shape[0], size), lambda i, s: (0, s[i]))
    whole = lambda a: pl.BlockSpec(a.shape, lambda i, s: (0, 0))
    operands = [*blocks, *scaled, *grads]
    specs = [half(a) for a in (*blocks, *scaled)] + [whole(g) for g in grads]
    if last is not None:
        operands.append(last)
        specs.append(whole(last))
    if more is not None:
        operands.append(more)
        specs.append(pl.BlockSpec((size, stacked), lambda i, s: (at, 0)))
    count = sides.shape[0]
    return pl.pallas_call(
        functools.partial(half_kernel, len(blocks), len(kept), last is not None, more is not None),
        out_shape=jax.ShapeDtypeStruct((count * size, stacked), BF16),
        grid_spec=pltpu.PrefetchScalarGridSpec(
            num_scalar_prefetch=1,
            grid=(count,),
            in_specs=specs,
            out_specs=pl.BlockSpec((size, stacked), lambda i, s: (i, 0)),
        ),
        cost_estimate=cost(8 * weight * size * stacked * 1024 + 1024, 1024),
        compiler_params=params(),
    )(sides, *operands)


def finish_kernel(keep, from_part, d_gate, d_up, d_down):
    hidden_units = d_gate.shape[1]
    whole = keep[...].astype(F32) + from_part[...].astype(F32)
    d_gate[...] = whole[:, :hidden_units]
    d_up[...] = whole[:, hidden_units : 2 * hidden_units]
    d_down[...] = whole[:, 2 * hidden_units :].T


def finish(keep, from_part):
    size, stacked = keep.shape
    hidden_units = stacked // 3
    sds = jax.ShapeDtypeStruct
    step = size // 4
    piece = lambda n: pl.BlockSpec((step, n), lambda i: (i, 0))
    return pl.pallas_call(
        finish_kernel,
        out_shape=[sds((size, hidden_units), F32), sds((size, hidden_units), F32), sds((hidden_units, size), F32)],
        grid=(size // step,),
        in_specs=[piece(stacked)] * 2,
        out_specs=[piece(hidden_units), piece(hidden_units), pl.BlockSpec((hidden_units, step), lambda i: (0, i))],
        cost_estimate=cost(1024, 1024),
        compiler_params=params(),
    )(keep, from_part)


Z, Y, CORES = 4, 2, 2


def pairs_of(move):
    out = []
    for z in range(Z):
        for y in range(Y):
            for c in range(CORES):
                to = move(z, y, c)
                if to is not None:
                    out.append(((z * Y + y) * CORES + c, (to[0] * Y + to[1]) * CORES + to[2]))
    return out


def along_z(table):
    return pairs_of(lambda z, y, c: (table[z], y, c) if z in table else None)


SWAP_CORE = pairs_of(lambda z, y, c: (z, y, 1 - c))
SWAP_Y = pairs_of(lambda z, y, c: (z, 1 - y, c))
OUTER = along_z({0: 1, 1: 0, 2: 3, 3: 2})
INNER = along_z({1: 2, 2: 1})
OUTWARD = along_z({1: 0, 2: 3})
SKIP_TO_INNER = along_z({0: 2, 3: 1})
SKIP_TO_OUTER = along_z({1: 3, 2: 0})
ENDS = along_z({0: 3, 3: 0})


def after(value, *others):
    return lax.optimization_barrier((value,) + others)[0]


def dense_body(tokens, d_output, combine, routes, gate_weight, up_weight, down_weight):
    experts = lax.axis_size("expert")
    part = lax.axis_index("dp")
    expert = lax.axis_index("expert")
    z = expert // (Y * CORES)
    inner = (z == 1) | (z == 2)
    scal = jnp.stack([part, expert]).astype(jnp.int32)
    mine = part[None].astype(jnp.int32)
    other = (1 - part)[None].astype(jnp.int32)

    move = lambda a, pairs: lax.ppermute(a, "expert", pairs)
    across = lambda a: lax.ppermute(a, "dp", [(0, 1), (1, 0)])

    swap = lambda a: move(a, SWAP_CORE)
    own = pack(experts, tokens, d_output, combine, routes)
    w_own = pack_weights(after(gate_weight[0], own), up_weight[0], down_weight[0])
    w_part = across(w_own)

    b1 = move(own, OUTER)
    f1 = move(own, INNER)
    y0 = move(own, SWAP_Y)
    f2 = move(b1, INNER)
    y1 = move(after(b1, y0), SWAP_Y)
    g1 = move(f1, OUTWARD)
    b2 = jnp.where(inner, f1, g1)
    y2 = move(after(b2, y1, f2), SWAP_Y)
    g2 = move(f2, OUTWARD)

    w_core = swap(after(w_own, y1, f2))
    w_both = swap(after(w_part, y1, f2))
    weights = [w_own, w_part, w_core, w_both]
    p0, p1, p2, q0, *kept_a = rows_call(experts, scal, [[own], [b1], [b2], [y0]], weights)
    b3 = jnp.where(inner, f2, after(g2, p0))
    y3 = move(after(b3, y2), SWAP_Y)
    p3, q12, *kept_b = rows_call(experts, scal, [[b3], [y1, y2]], weights)

    blocks = [own, b1, b2, y0, b3, y1, y2]
    kept = [kept_a, kept_b]
    to_core = half_call(jnp.concatenate([other, mine]), blocks, [k[2:] for k in kept])
    y3 = after(y3, q12, to_core)
    r12 = move(after(q12, y3), SWAP_Y)
    rows = own.shape[0]
    r1, r2 = r12[:rows], r12[rows:]

    q3, *kept_d, joined = rows_call(experts, scal, [[y3]], weights, joined=True)
    last = swap(joined)
    r3 = move(after(q3, r12), SWAP_Y)
    r0 = move(after(q0, r3), SWAP_Y)
    all_blocks = blocks + [y3]
    all_kept = [k[:2] for k in kept] + [kept_d]
    got = swap(to_core)
    send = half_call(other, all_blocks, all_kept, last, got, weight=1)
    from_part = across(send)
    keep = half_call(after(mine, send), all_blocks, all_kept, last, got, at=1)

    add = lambda *terms: sum(t.astype(F32) for t in terms).astype(BF16)
    s1 = add(p1, r1)
    s2 = add(p2, r2)
    s3 = add(p3, r3)
    d_tokens = add(
        after(p0, keep),
        r0,
        move(s1, OUTER),
        move(s2, INNER),
        move(s2, SKIP_TO_INNER),
        move(s3, SKIP_TO_OUTER),
        move(s3, ENDS),
    )
    d_gate, d_up, d_down = finish(keep, after(from_part, d_tokens))
    return (d_tokens, d_gate[None], d_up[None], d_down[None])


def route_slots(routes, experts):
    matches = (routes[:, :, None] == jnp.arange(experts, dtype=jnp.int32)[None, None, :]).astype(
        jnp.int32
    )
    per_token = jnp.sum(matches, axis=1)
    earlier = jnp.cumsum(per_token, axis=0) - per_token
    return jnp.sum(matches * earlier[:, None, :], axis=2)


def row_work(row_inputs, row_grads, gate_up, down_matrix):
    hidden_units = down_matrix.shape[0]
    preact = jnp.dot(row_inputs, gate_up, preferred_element_type=jnp.float32)
    gate_pre = preact[:, :hidden_units]
    up_pre = preact[:, hidden_units:]
    gate_sigmoid = jax.nn.sigmoid(gate_pre)
    hidden = (gate_pre * gate_sigmoid * up_pre).astype(jnp.bfloat16)
    d_hidden = jnp.dot(row_grads, down_matrix.T, preferred_element_type=jnp.float32)
    d_gate_pre = d_hidden * up_pre * gate_sigmoid * (1.0 + gate_pre * (1.0 - gate_sigmoid))
    d_up_pre = d_hidden * gate_pre * gate_sigmoid
    d_preact = jnp.concatenate([d_gate_pre, d_up_pre], axis=1).astype(jnp.bfloat16)
    d_rows = jnp.dot(d_preact, gate_up.T, preferred_element_type=jnp.float32).astype(jnp.bfloat16)
    return (d_rows, hidden, d_preact)


def routed_body(tokens, d_output, combine, routes, gate_weight, up_weight, down_weight):
    experts = lax.axis_size("expert")
    tok_count = tokens.shape[0]
    model_width = tokens.shape[1]
    top_count = routes.shape[1]
    capacity = max(2, (9 * tok_count * top_count + 8 * experts - 1) // (8 * experts))
    slot_count = experts * capacity
    slot_index = route_slots(routes, experts)
    position = (routes * capacity + slot_index).reshape(-1)
    spread_inputs = jnp.repeat(tokens, top_count, axis=0)
    scaled = (
        (combine[:, :, None] * d_output[:, None, :].astype(jnp.float32))
        .astype(jnp.bfloat16)
        .reshape(-1, model_width)
    )
    send_inputs = (
        jnp.zeros((slot_count, model_width), jnp.bfloat16)
        .at[position]
        .set(spread_inputs)
        .reshape(experts, capacity, model_width)
    )
    send_grads = (
        jnp.zeros((slot_count, model_width), jnp.bfloat16)
        .at[position]
        .set(scaled)
        .reshape(experts, capacity, model_width)
    )
    whole_gate, whole_up, whole_down = (
        lax.all_gather(gate_weight, "dp", axis=1, tiled=True),
        lax.all_gather(up_weight, "dp", axis=1, tiled=True),
        lax.all_gather(down_weight, "dp", axis=2, tiled=True),
    )
    gate_up = jnp.concatenate([whole_gate[0], whole_up[0]], axis=1)
    down_matrix = whole_down[0]
    hidden_units = down_matrix.shape[0]
    recv_inputs, recv_grads = (
        lax.all_to_all(send_inputs, "expert", split_axis=0, concat_axis=0, tiled=True),
        lax.all_to_all(send_grads, "expert", split_axis=0, concat_axis=0, tiled=True),
    )
    flat_inputs = recv_inputs.reshape(-1, model_width)
    flat_grads = recv_grads.reshape(-1, model_width)
    d_rows, hidden, d_preact = row_work(flat_inputs, flat_grads, gate_up, down_matrix)
    returned = lax.all_to_all(
        d_rows.reshape(experts, capacity, model_width),
        "expert",
        split_axis=0,
        concat_axis=0,
        tiled=True,
    )
    route_rows = returned.reshape(-1, model_width)[position].reshape(
        tok_count, top_count, model_width
    )
    d_tokens = jnp.sum(route_rows.astype(jnp.float32), axis=1).astype(jnp.bfloat16)
    gate_up_grad = jnp.dot(flat_inputs.T, d_preact, preferred_element_type=jnp.float32)
    down_grad = jnp.dot(flat_grads.T, hidden, preferred_element_type=jnp.float32)
    stacked = jnp.concatenate([gate_up_grad, down_grad], axis=1)
    summed = lax.psum_scatter(
        stacked.astype(jnp.bfloat16), "dp", scatter_dimension=0, tiled=True
    ).astype(jnp.float32)
    d_gate_weight = summed[:, :hidden_units][None]
    d_up_weight = summed[:, hidden_units : 2 * hidden_units][None]
    d_down_weight = summed[:, 2 * hidden_units :].T[None]
    return (d_tokens, d_gate_weight, d_up_weight, d_down_weight)


def solution(mesh):
    placed = (
        P(("dp", "expert"), None),
        P(("dp", "expert"), None),
        P(("dp", "expert"), None),
        P(("dp", "expert"), None),
        P("expert", "dp", None),
        P("expert", "dp", None),
        P("expert", None, "dp"),
    )
    dense = mesh.shape["expert"] == Z * Y * CORES and mesh.shape["dp"] == 2
    return jax.shard_map(
        dense_body if dense else routed_body,
        mesh=mesh,
        in_specs=placed,
        out_specs=(
            P(("dp", "expert"), None),
            P("expert", "dp", None),
            P("expert", "dp", None),
            P("expert", None, "dp"),
        ),
        check_vma=False,
    )
```

```python
import functools

import jax
import jax.numpy as jnp
from jax import lax
from jax.experimental import pallas as pl
from jax.experimental.pallas import tpu as pltpu
from jax.sharding import PartitionSpec as P

F32 = jnp.float32
BF16 = jnp.bfloat16
LANES = 128
VMEM_BYTES = 56 * 1024 * 1024


def vmem():
    return pl.BlockSpec(memory_space=pltpu.VMEM)


def smem():
    return pl.BlockSpec(memory_space=pltpu.SMEM)


def hbm():
    return pl.BlockSpec(memory_space=pl.ANY)


def params():
    return pltpu.CompilerParams(vmem_limit_bytes=VMEM_BYTES)


def cost(flops, moved):
    return pl.CostEstimate(flops=int(flops), bytes_accessed=int(moved), transcendentals=0)


def dot(a, b, dims):
    return lax.dot_general(a, b, (dims, ((), ())), preferred_element_type=F32)


def pack_kernel(experts, tokens, d_output, combine, routes, out):
    rows, width = tokens.shape
    out[:, :width] = tokens[...]
    out[:, width : 2 * width] = d_output[...]
    line = lax.broadcasted_iota(jnp.int32, (LANES, rows), 0)
    expert = lax.rem(line, experts)
    dense = jnp.zeros((LANES, rows), F32)
    for k in range(routes.shape[0]):
        dense = dense + jnp.where(expert == routes[k : k + 1, :], combine[k : k + 1, :], 0.0)
    high = dense.astype(BF16).astype(F32)
    rest = dense - high
    middle = rest.astype(BF16).astype(F32)
    low = rest - middle
    parts = jnp.where(
        line < experts,
        high,
        jnp.where(line < 2 * experts, middle, jnp.where(line < 3 * experts, low, 0.0)),
    )
    out[:, 2 * width :] = parts.T.astype(BF16)


def pack(experts, tokens, d_output, combine, routes):
    rows, width = tokens.shape
    return pl.pallas_call(
        functools.partial(pack_kernel, experts),
        out_shape=jax.ShapeDtypeStruct((rows, 2 * width + LANES), BF16),
        in_specs=[vmem()] * 4,
        out_specs=vmem(),
        cost_estimate=cost(0, 3 * rows * width * 2 * 2),
        compiler_params=params(),
    )(tokens, d_output, combine.T, routes.T)


def pack_weights_kernel(gate, up, down, out):
    hidden_units = gate.shape[1]
    out[:, :hidden_units] = gate[...]
    out[:, hidden_units : 2 * hidden_units] = up[...]
    out[:, 2 * hidden_units :] = down[...].T


def pack_weights(gate, up, down):
    size, hidden_units = gate.shape
    return pl.pallas_call(
        pack_weights_kernel,
        out_shape=jax.ShapeDtypeStruct((size, 3 * hidden_units), BF16),
        in_specs=[vmem()] * 3,
        out_specs=vmem(),
        cost_estimate=cost(0, 6 * size * hidden_units * 40),
        compiler_params=params(),
    )(gate, up, down)


def rows_kernel(experts, count, sizes, joined, scal, *refs):
    refs = list(refs)
    blocks = [refs.pop(0) for _ in range(count)]
    raw = [refs.pop(0) for _ in range(4)]
    out_rows = [refs.pop(0) for _ in sizes]
    kept = [refs.pop(0) for _ in range(3 if joined else 4)]
    block, held, grads, scaled, total, d_rows, in_sems, out_sems = refs
    part, expert = scal[0], scal[1]
    size, stacked = raw[0].shape
    hidden_units = stacked // 3
    both = 2 * hidden_units
    width = 2 * size
    rows = blocks[0].shape[0]
    arrivals = [
        pltpu.make_async_copy(b, block.at[pl.ds(i * rows, rows), :], in_sems.at[i]) for i, b in enumerate(blocks)
    ]
    weights = [pltpu.make_async_copy(raw[i], held.at[i], in_sems.at[count + i]) for i in range(4)]
    for c in arrivals + weights:
        c.start()
    leaving = []

    def leave(source, target):
        copy = pltpu.make_async_copy(source, target, out_sems.at[len(leaving)])
        copy.start()
        leaving.append(copy)

    for c in arrivals:
        c.wait()
    if joined:
        leave(block.at[:, pl.ds(0, width)], kept[2].at[:, pl.ds(stacked + width, width)])
    sides = [pl.multiple_of(part * size, size), pl.multiple_of((1 - part) * size, size)]
    parts = block[:, 2 * width :].astype(F32)
    lane = lax.broadcasted_iota(jnp.int32, parts.shape, 1)
    for which in range(2):
        for c in weights[2 * which : 2 * which + 2]:
            c.wait()
        wanted = expert if which == 0 else expert + 1 - 2 * lax.rem(expert, 2)
        mine = (lax.rem(lane, experts) == wanted) & (lane < 3 * experts)
        weight = jnp.sum(jnp.where(mine, parts, 0.0), axis=1, keepdims=True)
        preact = None
        d_hidden = None
        for side in range(2):
            at = sides[side]
            grad = block[:, pl.ds(pl.multiple_of(width + at, size), size)]
            scaled_half = (weight * grad.astype(F32)).astype(BF16)
            scaled[which, :, pl.ds(at, size)] = scaled_half
            p = dot(block[:, pl.ds(at, size)], held[2 * which + side, :, :both], ((1,), (0,)))
            h = dot(scaled_half, held[2 * which + side, :, both:], ((1,), (0,)))
            preact = p if side == 0 else preact + p
            d_hidden = h if side == 0 else d_hidden + h
        if joined and which == 1:
            leave(scaled.at[1], kept[2].at[:, pl.ds(stacked, width)])
        else:
            leave(scaled.at[which], kept[2 * which + 1])
        gate_pre = preact[:, :hidden_units]
        up_pre = preact[:, hidden_units:]
        sig = jax.nn.sigmoid(gate_pre)
        silu = gate_pre * sig
        d_gate = (d_hidden * up_pre * sig * (1.0 + gate_pre * (1.0 - sig))).astype(BF16)
        d_up = (d_hidden * silu).astype(BF16)
        grads[which, :, :hidden_units] = d_gate
        grads[which, :, hidden_units:both] = d_up
        grads[which, :, both:] = (silu * up_pre).astype(BF16)
        if joined and which == 1:
            leave(grads.at[1], kept[2].at[:, pl.ds(0, stacked)])
        else:
            leave(grads.at[which], kept[2 * which])
        d_preact = jnp.concatenate([d_gate, d_up], axis=1)
        for side in range(2):
            at = sides[side]
            new = dot(d_preact, held[2 * which + side, :, :both], ((1,), (1,)))
            if which == 0:
                total[:, pl.ds(at, size)] = new
            else:
                d_rows[:, pl.ds(at, size)] = (new + total[:, pl.ds(at, size)]).astype(BF16)
    row = 0
    for out, n in zip(out_rows, sizes):
        leave(d_rows.at[pl.ds(row, n), :], out)
        row += n
    for c in leaving:
        c.wait()


def rows_call(experts, scal, groups, weights, joined=False):
    blocks = [b for group in groups for b in group]
    count = len(blocks)
    rows = blocks[0].shape[0]
    size, stacked = weights[0].shape
    total = count * rows
    sizes = [len(group) * rows for group in groups]
    sds = jax.ShapeDtypeStruct
    out = [sds((n, 2 * size), BF16) for n in sizes]
    out += [sds((total, stacked), BF16), sds((total, 2 * size), BF16)]
    out += [sds((total, stacked + 4 * size), BF16)] if joined else out[-2:]
    return pl.pallas_call(
        functools.partial(rows_kernel, experts, count, sizes, joined),
        out_shape=out,
        in_specs=[smem()] + [hbm()] * (count + 4),
        out_specs=[hbm()] * len(out),
        scratch_shapes=[
            pltpu.VMEM((total, blocks[0].shape[1]), BF16),
            pltpu.VMEM((4, size, stacked), BF16),
            pltpu.VMEM((2, total, stacked), BF16),
            pltpu.VMEM((2, total, 2 * size), BF16),
            pltpu.VMEM((total, 2 * size), F32),
            pltpu.VMEM((total, 2 * size), BF16),
            pltpu.SemaphoreType.DMA((count + 4,)),
            pltpu.SemaphoreType.DMA((len(groups) + 5,)),
        ],
        cost_estimate=cost(24 * total * size * stacked * 2 * (10 if joined else 1), 1 << 20),
        compiler_params=params(),
    )(scal, *blocks, *weights)


def half_kernel(count, groups, joined, adds, at, sides, *refs):
    refs = list(refs)
    blocks = [refs.pop(0) for _ in range(count)]
    scaled = [refs.pop(0) for _ in range(groups)]
    grads = [refs.pop(0) for _ in range(groups)]
    last = refs.pop(0) if joined else None
    more = refs.pop(0) if adds else None
    out, lefts, made, extra, done, sems, out_sems = refs
    size, stacked = done.shape[1:]
    both = stacked // 3 * 2
    rows = blocks[0].shape[0]
    steps = done.shape[0]
    started = []

    def start(source, target):
        copy = pltpu.make_async_copy(source, target, sems.at[len(started)])
        copy.start()
        started.append(copy)
        return copy

    loads = [[[], []] for _ in range(steps)]
    offsets = [pl.multiple_of(sides[i] * size, size) for i in range(steps)]
    row = 0
    for i, b in enumerate(blocks):
        loads[0][0].append(start(b.at[:, pl.ds(offsets[0], size)], lefts.at[0, 0, pl.ds(row, rows), :]))
        row += rows
    if joined:
        first = pl.multiple_of(stacked + 2 * size + offsets[0], LANES)
        loads[0][0].append(start(last.at[:, pl.ds(first, size)], lefts.at[0, 0, pl.ds(row, rows), :]))
    row = 0
    for g in grads:
        loads[0][0].append(start(g, made.at[pl.ds(row, g.shape[0]), :]))
        row += g.shape[0]
    if joined:
        loads[0][0].append(start(last.at[:, pl.ds(0, stacked)], made.at[pl.ds(row, rows), :]))
    if adds:
        loads[0][0].append(start(more.at[pl.ds(at * size, size), :], extra))
    for step in range(steps):
        if step > 0:
            for i, b in enumerate(blocks):
                loads[step][0].append(
                    start(b.at[:, pl.ds(offsets[step], size)], lefts.at[step, 0, pl.ds(i * rows, rows), :])
                )
        row = 0
        for x in scaled:
            n = x.shape[0]
            loads[step][1].append(start(x.at[:, pl.ds(offsets[step], size)], lefts.at[step, 1, pl.ds(row, n), :]))
            row += n
        if joined:
            first = pl.multiple_of(stacked + offsets[step], LANES)
            loads[step][1].append(start(last.at[:, pl.ds(first, size)], lefts.at[step, 1, pl.ds(row, rows), :]))
    leaving = []
    for step in range(steps):
        for kind in range(2):
            for c in loads[step][kind]:
                c.wait()
            first, wide = (0, both) if kind == 0 else (both, stacked - both)
            new = dot(lefts[step, kind], made[:, first : first + wide], ((0,), (0,)))
            if adds:
                new = new + extra[:, first : first + wide].astype(F32)
            done[step, :, first : first + wide] = new.astype(BF16)
            copy = pltpu.make_async_copy(
                done.at[step, :, pl.ds(first, wide)],
                out.at[pl.ds(step * size, size), pl.ds(first, wide)],
                out_sems.at[len(leaving)],
            )
            copy.start()
            leaving.append(copy)
    for c in leaving:
        c.wait()


def half_call(sides, blocks, kept, last=None, more=None, at=0, weight=0):
    grads, scaled = [k[0] for k in kept], [k[1] for k in kept]
    size = scaled[0].shape[1] // 2
    stacked = grads[0].shape[1]
    rows = blocks[0].shape[0]
    extra = [a for a in (last, more) if a is not None]
    operands = [*blocks, *scaled, *grads, *extra]
    steps = sides.shape[0]
    total = (len(blocks) + (last is not None)) * rows
    return pl.pallas_call(
        functools.partial(half_kernel, len(blocks), len(kept), last is not None, more is not None, at),
        out_shape=jax.ShapeDtypeStruct((steps * size, stacked), BF16),
        in_specs=[smem()] + [hbm()] * len(operands),
        out_specs=hbm(),
        scratch_shapes=[
            pltpu.VMEM((steps, 2, total, size), BF16),
            pltpu.VMEM((total, stacked), BF16),
            pltpu.VMEM((size, stacked), BF16),
            pltpu.VMEM((steps, size, stacked), BF16),
            pltpu.SemaphoreType.DMA((steps * (len(blocks) + len(kept) + 2) + len(kept) + 2,)),
            pltpu.SemaphoreType.DMA((2 * steps,)),
        ],
        cost_estimate=cost(8 * weight * size * stacked * 1024 + 1024, 1024),
        compiler_params=params(),
    )(sides, *operands)


def finish_kernel(keep, from_part, d_gate, d_up, d_down):
    hidden_units = d_gate.shape[1]
    whole = keep[...].astype(F32) + from_part[...].astype(F32)
    d_gate[...] = whole[:, :hidden_units]
    d_up[...] = whole[:, hidden_units : 2 * hidden_units]
    d_down[...] = whole[:, 2 * hidden_units :].T


def finish(keep, from_part):
    size, stacked = keep.shape
    hidden_units = stacked // 3
    sds = jax.ShapeDtypeStruct
    step = size // 4
    piece = lambda n: pl.BlockSpec((step, n), lambda i: (i, 0))
    return pl.pallas_call(
        finish_kernel,
        out_shape=[sds((size, hidden_units), F32), sds((size, hidden_units), F32), sds((hidden_units, size), F32)],
        grid=(size // step,),
        in_specs=[piece(stacked)] * 2,
        out_specs=[piece(hidden_units), piece(hidden_units), pl.BlockSpec((hidden_units, step), lambda i: (0, i))],
        cost_estimate=cost(1024, 1024),
        compiler_params=params(),
    )(keep, from_part)


Z, Y, CORES = 4, 2, 2


def pairs_of(move):
    out = []
    for z in range(Z):
        for y in range(Y):
            for c in range(CORES):
                to = move(z, y, c)
                if to is not None:
                    out.append(((z * Y + y) * CORES + c, (to[0] * Y + to[1]) * CORES + to[2]))
    return out


def along_z(table):
    return pairs_of(lambda z, y, c: (table[z], y, c) if z in table else None)


SWAP_CORE = pairs_of(lambda z, y, c: (z, y, 1 - c))
SWAP_Y = pairs_of(lambda z, y, c: (z, 1 - y, c))
OUTER = along_z({0: 1, 1: 0, 2: 3, 3: 2})
INNER = along_z({1: 2, 2: 1})
OUTWARD = along_z({1: 0, 2: 3})
SKIP_TO_INNER = along_z({0: 2, 3: 1})
SKIP_TO_OUTER = along_z({1: 3, 2: 0})
ENDS = along_z({0: 3, 3: 0})


def after(value, *others):
    return lax.optimization_barrier((value,) + others)[0]


def dense_body(tokens, d_output, combine, routes, gate_weight, up_weight, down_weight):
    experts = lax.axis_size("expert")
    part = lax.axis_index("dp")
    expert = lax.axis_index("expert")
    z = expert // (Y * CORES)
    inner = (z == 1) | (z == 2)
    scal = jnp.stack([part, expert]).astype(jnp.int32)
    mine = part[None].astype(jnp.int32)
    other = (1 - part)[None].astype(jnp.int32)

    move = lambda a, pairs: lax.ppermute(a, "expert", pairs)
    across = lambda a: lax.ppermute(a, "dp", [(0, 1), (1, 0)])

    swap = lambda a: move(a, SWAP_CORE)
    own = pack(experts, tokens, d_output, combine, routes)

    b1 = move(own, OUTER)
    f1 = move(own, INNER)
    y0 = move(own, SWAP_Y)
    w_own = pack_weights(after(gate_weight[0], own), up_weight[0], down_weight[0])
    w_part = across(w_own)
    f2 = move(b1, INNER)
    y1 = move(after(b1, y0), SWAP_Y)
    g1 = move(f1, OUTWARD)
    b2 = jnp.where(inner, f1, g1)
    y2 = move(after(b2, y1, f2), SWAP_Y)
    g2 = move(f2, OUTWARD)

    w_core = swap(after(w_own, y1, f2))
    w_both = swap(after(w_part, y1, f2))
    weights = [w_own, w_part, w_core, w_both]
    p0, p1, p2, q0, *kept_a = rows_call(experts, scal, [[own], [b1], [b2], [y0]], weights)
    b3 = jnp.where(inner, f2, after(g2, p0))
    y3 = move(after(b3, y2), SWAP_Y)
    p3, q12, *kept_b = rows_call(experts, scal, [[b3], [y1, y2]], weights)

    blocks = [own, b1, b2, y0, b3, y1, y2]
    kept = [kept_a, kept_b]
    to_core = half_call(jnp.concatenate([other, mine]), blocks, [k[2:] for k in kept])
    y3 = after(y3, q12, to_core)
    r12 = move(after(q12, y3), SWAP_Y)
    rows = own.shape[0]
    r1, r2 = r12[:rows], r12[rows:]

    q3, *kept_d, joined = rows_call(experts, scal, [[y3]], weights, joined=True)
    last = swap(joined)
    r3 = move(after(q3, r12), SWAP_Y)
    r0 = move(after(q0, r3), SWAP_Y)
    all_blocks = blocks + [y3]
    all_kept = [k[:2] for k in kept] + [kept_d]
    got = swap(to_core)
    send = half_call(other, all_blocks, all_kept, last, got, weight=1)
    from_part = across(send)
    keep = half_call(after(mine, send), all_blocks, all_kept, last, got, at=1)

    add = lambda *terms: sum(t.astype(F32) for t in terms).astype(BF16)
    s1 = add(p1, r1)
    s2 = add(p2, r2)
    s3 = add(p3, r3)
    d_tokens = add(
        after(p0, keep),
        r0,
        move(s1, OUTER),
        move(s2, INNER),
        move(s2, SKIP_TO_INNER),
        move(s3, SKIP_TO_OUTER),
        move(s3, ENDS),
    )
    d_gate, d_up, d_down = finish(keep, after(from_part, d_tokens))
    return (d_tokens, d_gate[None], d_up[None], d_down[None])


def route_slots(routes, experts):
    matches = (routes[:, :, None] == jnp.arange(experts, dtype=jnp.int32)[None, None, :]).astype(
        jnp.int32
    )
    per_token = jnp.sum(matches, axis=1)
    earlier = jnp.cumsum(per_token, axis=0) - per_token
    return jnp.sum(matches * earlier[:, None, :], axis=2)


def row_work(row_inputs, row_grads, gate_up, down_matrix):
    hidden_units = down_matrix.shape[0]
    preact = jnp.dot(row_inputs, gate_up, preferred_element_type=jnp.float32)
    gate_pre = preact[:, :hidden_units]
    up_pre = preact[:, hidden_units:]
    gate_sigmoid = jax.nn.sigmoid(gate_pre)
    hidden = (gate_pre * gate_sigmoid * up_pre).astype(jnp.bfloat16)
    d_hidden = jnp.dot(row_grads, down_matrix.T, preferred_element_type=jnp.float32)
    d_gate_pre = d_hidden * up_pre * gate_sigmoid * (1.0 + gate_pre * (1.0 - gate_sigmoid))
    d_up_pre = d_hidden * gate_pre * gate_sigmoid
    d_preact = jnp.concatenate([d_gate_pre, d_up_pre], axis=1).astype(jnp.bfloat16)
    d_rows = jnp.dot(d_preact, gate_up.T, preferred_element_type=jnp.float32).astype(jnp.bfloat16)
    return (d_rows, hidden, d_preact)


def routed_body(tokens, d_output, combine, routes, gate_weight, up_weight, down_weight):
    experts = lax.axis_size("expert")
    tok_count = tokens.shape[0]
    model_width = tokens.shape[1]
    top_count = routes.shape[1]
    capacity = max(2, (9 * tok_count * top_count + 8 * experts - 1) // (8 * experts))
    slot_count = experts * capacity
    slot_index = route_slots(routes, experts)
    position = (routes * capacity + slot_index).reshape(-1)
    spread_inputs = jnp.repeat(tokens, top_count, axis=0)
    scaled = (
        (combine[:, :, None] * d_output[:, None, :].astype(jnp.float32))
        .astype(jnp.bfloat16)
        .reshape(-1, model_width)
    )
    send_inputs = (
        jnp.zeros((slot_count, model_width), jnp.bfloat16)
        .at[position]
        .set(spread_inputs)
        .reshape(experts, capacity, model_width)
    )
    send_grads = (
        jnp.zeros((slot_count, model_width), jnp.bfloat16)
        .at[position]
        .set(scaled)
        .reshape(experts, capacity, model_width)
    )
    whole_gate, whole_up, whole_down = (
        lax.all_gather(gate_weight, "dp", axis=1, tiled=True),
        lax.all_gather(up_weight, "dp", axis=1, tiled=True),
        lax.all_gather(down_weight, "dp", axis=2, tiled=True),
    )
    gate_up = jnp.concatenate([whole_gate[0], whole_up[0]], axis=1)
    down_matrix = whole_down[0]
    hidden_units = down_matrix.shape[0]
    recv_inputs, recv_grads = (
        lax.all_to_all(send_inputs, "expert", split_axis=0, concat_axis=0, tiled=True),
        lax.all_to_all(send_grads, "expert", split_axis=0, concat_axis=0, tiled=True),
    )
    flat_inputs = recv_inputs.reshape(-1, model_width)
    flat_grads = recv_grads.reshape(-1, model_width)
    d_rows, hidden, d_preact = row_work(flat_inputs, flat_grads, gate_up, down_matrix)
    returned = lax.all_to_all(
        d_rows.reshape(experts, capacity, model_width),
        "expert",
        split_axis=0,
        concat_axis=0,
        tiled=True,
    )
    route_rows = returned.reshape(-1, model_width)[position].reshape(
        tok_count, top_count, model_width
    )
    d_tokens = jnp.sum(route_rows.astype(jnp.float32), axis=1).astype(jnp.bfloat16)
    gate_up_grad = jnp.dot(flat_inputs.T, d_preact, preferred_element_type=jnp.float32)
    down_grad = jnp.dot(flat_grads.T, hidden, preferred_element_type=jnp.float32)
    stacked = jnp.concatenate([gate_up_grad, down_grad], axis=1)
    summed = lax.psum_scatter(
        stacked.astype(jnp.bfloat16), "dp", scatter_dimension=0, tiled=True
    ).astype(jnp.float32)
    d_gate_weight = summed[:, :hidden_units][None]
    d_up_weight = summed[:, hidden_units : 2 * hidden_units][None]
    d_down_weight = summed[:, 2 * hidden_units :].T[None]
    return (d_tokens, d_gate_weight, d_up_weight, d_down_weight)


def solution(mesh):
    placed = (
        P(("dp", "expert"), None),
        P(("dp", "expert"), None),
        P(("dp", "expert"), None),
        P(("dp", "expert"), None),
        P("expert", "dp", None),
        P("expert", "dp", None),
        P("expert", None, "dp"),
    )
    dense = mesh.shape["expert"] == Z * Y * CORES and mesh.shape["dp"] == 2
    return jax.shard_map(
        dense_body if dense else routed_body,
        mesh=mesh,
        in_specs=placed,
        out_specs=(
            P(("dp", "expert"), None),
            P("expert", "dp", None),
            P("expert", "dp", None),
            P("expert", None, "dp"),
        ),
        check_vma=False,
    )
```

```python
import functools

import jax
import jax.numpy as jnp
from jax import lax
from jax.experimental import pallas as pl
from jax.experimental.pallas import tpu as pltpu
from jax.sharding import PartitionSpec as P

F32 = jnp.float32
BF16 = jnp.bfloat16
LANES = 128
VMEM_BYTES = 56 * 1024 * 1024


def vmem():
    return pl.BlockSpec(memory_space=pltpu.VMEM)


def smem():
    return pl.BlockSpec(memory_space=pltpu.SMEM)


def hbm():
    return pl.BlockSpec(memory_space=pl.ANY)


def params():
    return pltpu.CompilerParams(vmem_limit_bytes=VMEM_BYTES)


def cost(flops, moved):
    return pl.CostEstimate(flops=int(flops), bytes_accessed=int(moved), transcendentals=0)


def dot(a, b, dims):
    return lax.dot_general(a, b, (dims, ((), ())), preferred_element_type=F32)


def pack_kernel(experts, tokens, d_output, combine, routes, out):
    rows, width = tokens.shape
    out[:, :width] = tokens[...]
    out[:, width : 2 * width] = d_output[...]
    line = lax.broadcasted_iota(jnp.int32, (LANES, rows), 0)
    expert = lax.rem(line, experts)
    dense = jnp.zeros((LANES, rows), F32)
    for k in range(routes.shape[0]):
        dense = dense + jnp.where(expert == routes[k : k + 1, :], combine[k : k + 1, :], 0.0)
    high = dense.astype(BF16).astype(F32)
    rest = dense - high
    middle = rest.astype(BF16).astype(F32)
    low = rest - middle
    parts = jnp.where(
        line < experts,
        high,
        jnp.where(line < 2 * experts, middle, jnp.where(line < 3 * experts, low, 0.0)),
    )
    out[:, 2 * width :] = parts.T.astype(BF16)


def pack(experts, tokens, d_output, combine, routes):
    rows, width = tokens.shape
    return pl.pallas_call(
        functools.partial(pack_kernel, experts),
        out_shape=jax.ShapeDtypeStruct((rows, 2 * width + LANES), BF16),
        in_specs=[vmem()] * 4,
        out_specs=vmem(),
        cost_estimate=cost(0, 3 * rows * width * 2 * 2),
        compiler_params=params(),
    )(tokens, d_output, combine.T, routes.T)


def pack_weights_kernel(gate, up, down, out):
    hidden_units = gate.shape[1]
    out[:, :hidden_units] = gate[...]
    out[:, hidden_units : 2 * hidden_units] = up[...]
    out[:, 2 * hidden_units :] = down[...].T


def pack_weights(gate, up, down):
    size, hidden_units = gate.shape
    return pl.pallas_call(
        pack_weights_kernel,
        out_shape=jax.ShapeDtypeStruct((size, 3 * hidden_units), BF16),
        in_specs=[vmem()] * 3,
        out_specs=vmem(),
        cost_estimate=cost(0, 6 * size * hidden_units * 40),
        compiler_params=params(),
    )(gate, up, down)


def rows_kernel(experts, count, sizes, joined, scal, *refs):
    refs = list(refs)
    blocks = [refs.pop(0) for _ in range(count)]
    raw = [refs.pop(0) for _ in range(4)]
    out_rows = [refs.pop(0) for _ in sizes]
    kept = [refs.pop(0) for _ in range(3 if joined else 4)]
    block, held, grads, scaled, d_rows, in_sems, out_sems = refs
    part, expert = scal[0], scal[1]
    size, stacked = raw[0].shape
    hidden_units = stacked // 3
    both = 2 * hidden_units
    width = 2 * size
    rows = blocks[0].shape[0]
    arrivals = [
        pltpu.make_async_copy(b, block.at[pl.ds(i * rows, rows), :], in_sems.at[i]) for i, b in enumerate(blocks)
    ]
    weights = [pltpu.make_async_copy(raw[i], held.at[i], in_sems.at[count + i]) for i in range(4)]
    for c in arrivals + weights:
        c.start()
    leaving = []

    def leave(source, target):
        copy = pltpu.make_async_copy(source, target, out_sems.at[len(leaving)])
        copy.start()
        leaving.append(copy)

    for c in arrivals:
        c.wait()
    if joined:
        leave(block.at[:, pl.ds(0, width)], kept[2].at[:, pl.ds(stacked + width, width)])
    sides = [pl.multiple_of(part * size, size), pl.multiple_of((1 - part) * size, size)]
    parts = block[:, 2 * width :].astype(F32)
    lane = lax.broadcasted_iota(jnp.int32, parts.shape, 1)
    first = []
    for which in range(2):
        for c in weights[2 * which : 2 * which + 2]:
            c.wait()
        wanted = expert if which == 0 else expert + 1 - 2 * lax.rem(expert, 2)
        mine = (lax.rem(lane, experts) == wanted) & (lane < 3 * experts)
        weight = jnp.sum(jnp.where(mine, parts, 0.0), axis=1, keepdims=True)
        preact = None
        d_hidden = None
        for side in range(2):
            at = sides[side]
            grad = block[:, pl.ds(pl.multiple_of(width + at, size), size)]
            scaled_half = (weight * grad.astype(F32)).astype(BF16)
            scaled[which, :, pl.ds(at, size)] = scaled_half
            p = dot(block[:, pl.ds(at, size)], held[2 * which + side, :, :both], ((1,), (0,)))
            h = dot(scaled_half, held[2 * which + side, :, both:], ((1,), (0,)))
            preact = p if side == 0 else preact + p
            d_hidden = h if side == 0 else d_hidden + h
        first.append((preact, d_hidden))
    leave(scaled.at[0], kept[1])
    leave(scaled.at[1], kept[2].at[:, pl.ds(stacked, width)] if joined else kept[3])
    second = []
    for which in range(2):
        preact, d_hidden = first[which]
        gate_pre = preact[:, :hidden_units]
        up_pre = preact[:, hidden_units:]
        sig = jax.nn.sigmoid(gate_pre)
        silu = gate_pre * sig
        d_gate = (d_hidden * up_pre * sig * (1.0 + gate_pre * (1.0 - sig))).astype(BF16)
        d_up = (d_hidden * silu).astype(BF16)
        grads[which, :, :hidden_units] = d_gate
        grads[which, :, hidden_units:both] = d_up
        grads[which, :, both:] = (silu * up_pre).astype(BF16)
        d_preact = jnp.concatenate([d_gate, d_up], axis=1)
        second.append([dot(d_preact, held[2 * which + side, :, :both], ((1,), (1,))) for side in range(2)])
    leave(grads.at[0], kept[0])
    leave(grads.at[1], kept[2].at[:, pl.ds(0, stacked)] if joined else kept[2])
    for side in range(2):
        d_rows[:, pl.ds(sides[side], size)] = (second[0][side] + second[1][side]).astype(BF16)
    row = 0
    for out, n in zip(out_rows, sizes):
        leave(d_rows.at[pl.ds(row, n), :], out)
        row += n
    for c in leaving:
        c.wait()


def rows_call(experts, scal, groups, weights, joined=False):
    blocks = [b for group in groups for b in group]
    count = len(blocks)
    rows = blocks[0].shape[0]
    size, stacked = weights[0].shape
    total = count * rows
    sizes = [len(group) * rows for group in groups]
    sds = jax.ShapeDtypeStruct
    out = [sds((n, 2 * size), BF16) for n in sizes]
    out += [sds((total, stacked), BF16), sds((total, 2 * size), BF16)]
    out += [sds((total, stacked + 4 * size), BF16)] if joined else out[-2:]
    return pl.pallas_call(
        functools.partial(rows_kernel, experts, count, sizes, joined),
        out_shape=out,
        in_specs=[smem()] + [hbm()] * (count + 4),
        out_specs=[hbm()] * len(out),
        scratch_shapes=[
            pltpu.VMEM((total, blocks[0].shape[1]), BF16),
            pltpu.VMEM((4, size, stacked), BF16),
            pltpu.VMEM((2, total, stacked), BF16),
            pltpu.VMEM((2, total, 2 * size), BF16),
            pltpu.VMEM((total, 2 * size), BF16),
            pltpu.SemaphoreType.DMA((count + 4,)),
            pltpu.SemaphoreType.DMA((len(groups) + 5,)),
        ],
        cost_estimate=cost(24 * total * size * stacked * 2 * (10 if joined else 1), 1 << 20),
        compiler_params=params(),
    )(scal, *blocks, *weights)


def half_kernel(count, groups, joined, adds, at, sides, *refs):
    refs = list(refs)
    blocks = [refs.pop(0) for _ in range(count)]
    scaled = [refs.pop(0) for _ in range(groups)]
    grads = [refs.pop(0) for _ in range(groups)]
    last = refs.pop(0) if joined else None
    more = refs.pop(0) if adds else None
    out, lefts, made, extra, done, sems, out_sems = refs
    size, stacked = done.shape[1:]
    both = stacked // 3 * 2
    rows = blocks[0].shape[0]
    steps = done.shape[0]
    started = []

    def start(source, target):
        copy = pltpu.make_async_copy(source, target, sems.at[len(started)])
        copy.start()
        started.append(copy)
        return copy

    loads = [[[], []] for _ in range(steps)]
    offsets = [pl.multiple_of(sides[i] * size, size) for i in range(steps)]
    row = 0
    for i, b in enumerate(blocks):
        loads[0][0].append(start(b.at[:, pl.ds(offsets[0], size)], lefts.at[0, 0, pl.ds(row, rows), :]))
        row += rows
    if joined:
        first = pl.multiple_of(stacked + 2 * size + offsets[0], LANES)
        loads[0][0].append(start(last.at[:, pl.ds(first, size)], lefts.at[0, 0, pl.ds(row, rows), :]))
    row = 0
    for g in grads:
        loads[0][0].append(start(g, made.at[pl.ds(row, g.shape[0]), :]))
        row += g.shape[0]
    if joined:
        loads[0][0].append(start(last.at[:, pl.ds(0, stacked)], made.at[pl.ds(row, rows), :]))
    if adds:
        loads[0][0].append(start(more.at[pl.ds(at * size, size), :], extra))
    for step in range(steps):
        if step > 0:
            for i, b in enumerate(blocks):
                loads[step][0].append(
                    start(b.at[:, pl.ds(offsets[step], size)], lefts.at[step, 0, pl.ds(i * rows, rows), :])
                )
        row = 0
        for x in scaled:
            n = x.shape[0]
            loads[step][1].append(start(x.at[:, pl.ds(offsets[step], size)], lefts.at[step, 1, pl.ds(row, n), :]))
            row += n
        if joined:
            first = pl.multiple_of(stacked + offsets[step], LANES)
            loads[step][1].append(start(last.at[:, pl.ds(first, size)], lefts.at[step, 1, pl.ds(row, rows), :]))
    leaving = []
    for step in range(steps):
        for kind in range(2):
            for c in loads[step][kind]:
                c.wait()
            first, wide = (0, both) if kind == 0 else (both, stacked - both)
            new = dot(lefts[step, kind], made[:, first : first + wide], ((0,), (0,)))
            if adds:
                new = new + extra[:, first : first + wide].astype(F32)
            done[step, :, first : first + wide] = new.astype(BF16)
            copy = pltpu.make_async_copy(
                done.at[step, :, pl.ds(first, wide)],
                out.at[pl.ds(step * size, size), pl.ds(first, wide)],
                out_sems.at[len(leaving)],
            )
            copy.start()
            leaving.append(copy)
    for c in leaving:
        c.wait()


def half_call(sides, blocks, kept, last=None, more=None, at=0, weight=0):
    grads, scaled = [k[0] for k in kept], [k[1] for k in kept]
    size = scaled[0].shape[1] // 2
    stacked = grads[0].shape[1]
    rows = blocks[0].shape[0]
    extra = [a for a in (last, more) if a is not None]
    operands = [*blocks, *scaled, *grads, *extra]
    steps = sides.shape[0]
    total = (len(blocks) + (last is not None)) * rows
    return pl.pallas_call(
        functools.partial(half_kernel, len(blocks), len(kept), last is not None, more is not None, at),
        out_shape=jax.ShapeDtypeStruct((steps * size, stacked), BF16),
        in_specs=[smem()] + [hbm()] * len(operands),
        out_specs=hbm(),
        scratch_shapes=[
            pltpu.VMEM((steps, 2, total, size), BF16),
            pltpu.VMEM((total, stacked), BF16),
            pltpu.VMEM((size, stacked), BF16),
            pltpu.VMEM((steps, size, stacked), BF16),
            pltpu.SemaphoreType.DMA((steps * (len(blocks) + len(kept) + 2) + len(kept) + 2,)),
            pltpu.SemaphoreType.DMA((2 * steps,)),
        ],
        cost_estimate=cost(8 * weight * size * stacked * 1024 + 1024, 1024),
        compiler_params=params(),
    )(sides, *operands)


def finish_kernel(keep, from_part, d_gate, d_up, d_down):
    hidden_units = d_gate.shape[1]
    whole = keep[...].astype(F32) + from_part[...].astype(F32)
    d_gate[...] = whole[:, :hidden_units]
    d_up[...] = whole[:, hidden_units : 2 * hidden_units]
    d_down[...] = whole[:, 2 * hidden_units :].T


def finish(keep, from_part):
    size, stacked = keep.shape
    hidden_units = stacked // 3
    sds = jax.ShapeDtypeStruct
    step = size // 4
    piece = lambda n: pl.BlockSpec((step, n), lambda i: (i, 0))
    return pl.pallas_call(
        finish_kernel,
        out_shape=[sds((size, hidden_units), F32), sds((size, hidden_units), F32), sds((hidden_units, size), F32)],
        grid=(size // step,),
        in_specs=[piece(stacked)] * 2,
        out_specs=[piece(hidden_units), piece(hidden_units), pl.BlockSpec((hidden_units, step), lambda i: (0, i))],
        cost_estimate=cost(1024, 1024),
        compiler_params=params(),
    )(keep, from_part)


Z, Y, CORES = 4, 2, 2


def pairs_of(move):
    out = []
    for z in range(Z):
        for y in range(Y):
            for c in range(CORES):
                to = move(z, y, c)
                if to is not None:
                    out.append(((z * Y + y) * CORES + c, (to[0] * Y + to[1]) * CORES + to[2]))
    return out


def along_z(table):
    return pairs_of(lambda z, y, c: (table[z], y, c) if z in table else None)


SWAP_CORE = pairs_of(lambda z, y, c: (z, y, 1 - c))
SWAP_Y = pairs_of(lambda z, y, c: (z, 1 - y, c))
OUTER = along_z({0: 1, 1: 0, 2: 3, 3: 2})
INNER = along_z({1: 2, 2: 1})
OUTWARD = along_z({1: 0, 2: 3})
INWARD = along_z({0: 1, 3: 2})
SKIP_TO_OUTER = along_z({1: 3, 2: 0})


def after(value, *others):
    return lax.optimization_barrier((value,) + others)[0]


def dense_body(tokens, d_output, combine, routes, gate_weight, up_weight, down_weight):
    experts = lax.axis_size("expert")
    part = lax.axis_index("dp")
    expert = lax.axis_index("expert")
    z = expert // (Y * CORES)
    inner = (z == 1) | (z == 2)
    scal = jnp.stack([part, expert]).astype(jnp.int32)
    mine = part[None].astype(jnp.int32)
    other = (1 - part)[None].astype(jnp.int32)

    move = lambda a, pairs: lax.ppermute(a, "expert", pairs)
    across = lambda a: lax.ppermute(a, "dp", [(0, 1), (1, 0)])

    swap = lambda a: move(a, SWAP_CORE)
    own = pack(experts, tokens, d_output, combine, routes)

    b1 = move(own, OUTER)
    f1 = move(own, INNER)
    y0 = move(own, SWAP_Y)
    w_own = pack_weights(after(gate_weight[0], own), up_weight[0], down_weight[0])
    w_part = across(w_own)
    f2 = move(b1, INNER)
    y1 = move(after(b1, y0), SWAP_Y)
    g1 = move(f1, OUTWARD)
    b2 = jnp.where(inner, f1, g1)
    y2 = move(after(b2, y1, f2), SWAP_Y)
    g2 = move(f2, OUTWARD)

    w_core = swap(after(w_own, y1, f2))
    w_both = swap(after(w_part, y1, f2))
    weights = [w_own, w_part, w_core, w_both]
    p0, p1, p2, q0, *kept_a = rows_call(experts, scal, [[own], [b1], [b2], [y0]], weights)
    b3 = jnp.where(inner, f2, after(g2, p0))
    y3 = move(after(b3, y2), SWAP_Y)
    p3, q12, *kept_b = rows_call(experts, scal, [[b3], [y1, y2]], weights)

    blocks = [own, b1, b2, y0, b3, y1, y2]
    kept = [kept_a, kept_b]
    to_core = half_call(jnp.concatenate([other, mine]), blocks, [k[2:] for k in kept])
    y3 = after(y3, q12, to_core)
    r12 = move(after(q12, y3), SWAP_Y)
    rows = own.shape[0]
    r1, r2 = r12[:rows], r12[rows:]

    q3, *kept_d, joined = rows_call(experts, scal, [[y3]], weights, joined=True)
    last = swap(joined)
    all_blocks = blocks + [y3]
    all_kept = [k[:2] for k in kept] + [kept_d]
    got = swap(to_core)
    send = half_call(other, all_blocks, all_kept, last, got, weight=1)
    from_part = across(send)
    r3 = move(after(q3, send), SWAP_Y)
    r0 = move(after(q0, r3), SWAP_Y)
    keep = half_call(after(mine, send), all_blocks, all_kept, last, got, at=1)

    add = lambda *terms: sum(t.astype(F32) for t in terms).astype(BF16)
    s1 = add(p1, r1)
    s2 = add(p2, r2)
    s2 = add(s2, move(s2, INWARD))
    s3 = add(p3, r3)
    s3 = add(s3, move(s3, INWARD))
    d_gate, d_up, d_down = finish(keep, after(from_part, s2))
    d_tokens = add(after(p0, d_gate), r0, move(s1, OUTER), move(s2, INNER), move(s3, SKIP_TO_OUTER))
    return (d_tokens, d_gate[None], d_up[None], d_down[None])


def route_slots(routes, experts):
    matches = (routes[:, :, None] == jnp.arange(experts, dtype=jnp.int32)[None, None, :]).astype(
        jnp.int32
    )
    per_token = jnp.sum(matches, axis=1)
    earlier = jnp.cumsum(per_token, axis=0) - per_token
    return jnp.sum(matches * earlier[:, None, :], axis=2)


def row_work(row_inputs, row_grads, gate_up, down_matrix):
    hidden_units = down_matrix.shape[0]
    preact = jnp.dot(row_inputs, gate_up, preferred_element_type=jnp.float32)
    gate_pre = preact[:, :hidden_units]
    up_pre = preact[:, hidden_units:]
    gate_sigmoid = jax.nn.sigmoid(gate_pre)
    hidden = (gate_pre * gate_sigmoid * up_pre).astype(jnp.bfloat16)
    d_hidden = jnp.dot(row_grads, down_matrix.T, preferred_element_type=jnp.float32)
    d_gate_pre = d_hidden * up_pre * gate_sigmoid * (1.0 + gate_pre * (1.0 - gate_sigmoid))
    d_up_pre = d_hidden * gate_pre * gate_sigmoid
    d_preact = jnp.concatenate([d_gate_pre, d_up_pre], axis=1).astype(jnp.bfloat16)
    d_rows = jnp.dot(d_preact, gate_up.T, preferred_element_type=jnp.float32).astype(jnp.bfloat16)
    return (d_rows, hidden, d_preact)


def routed_body(tokens, d_output, combine, routes, gate_weight, up_weight, down_weight):
    experts = lax.axis_size("expert")
    tok_count = tokens.shape[0]
    model_width = tokens.shape[1]
    top_count = routes.shape[1]
    capacity = max(2, (9 * tok_count * top_count + 8 * experts - 1) // (8 * experts))
    slot_count = experts * capacity
    slot_index = route_slots(routes, experts)
    position = (routes * capacity + slot_index).reshape(-1)
    spread_inputs = jnp.repeat(tokens, top_count, axis=0)
    scaled = (
        (combine[:, :, None] * d_output[:, None, :].astype(jnp.float32))
        .astype(jnp.bfloat16)
        .reshape(-1, model_width)
    )
    send_inputs = (
        jnp.zeros((slot_count, model_width), jnp.bfloat16)
        .at[position]
        .set(spread_inputs)
        .reshape(experts, capacity, model_width)
    )
    send_grads = (
        jnp.zeros((slot_count, model_width), jnp.bfloat16)
        .at[position]
        .set(scaled)
        .reshape(experts, capacity, model_width)
    )
    whole_gate, whole_up, whole_down = (
        lax.all_gather(gate_weight, "dp", axis=1, tiled=True),
        lax.all_gather(up_weight, "dp", axis=1, tiled=True),
        lax.all_gather(down_weight, "dp", axis=2, tiled=True),
    )
    gate_up = jnp.concatenate([whole_gate[0], whole_up[0]], axis=1)
    down_matrix = whole_down[0]
    hidden_units = down_matrix.shape[0]
    recv_inputs, recv_grads = (
        lax.all_to_all(send_inputs, "expert", split_axis=0, concat_axis=0, tiled=True),
        lax.all_to_all(send_grads, "expert", split_axis=0, concat_axis=0, tiled=True),
    )
    flat_inputs = recv_inputs.reshape(-1, model_width)
    flat_grads = recv_grads.reshape(-1, model_width)
    d_rows, hidden, d_preact = row_work(flat_inputs, flat_grads, gate_up, down_matrix)
    returned = lax.all_to_all(
        d_rows.reshape(experts, capacity, model_width),
        "expert",
        split_axis=0,
        concat_axis=0,
        tiled=True,
    )
    route_rows = returned.reshape(-1, model_width)[position].reshape(
        tok_count, top_count, model_width
    )
    d_tokens = jnp.sum(route_rows.astype(jnp.float32), axis=1).astype(jnp.bfloat16)
    gate_up_grad = jnp.dot(flat_inputs.T, d_preact, preferred_element_type=jnp.float32)
    down_grad = jnp.dot(flat_grads.T, hidden, preferred_element_type=jnp.float32)
    stacked = jnp.concatenate([gate_up_grad, down_grad], axis=1)
    summed = lax.psum_scatter(
        stacked.astype(jnp.bfloat16), "dp", scatter_dimension=0, tiled=True
    ).astype(jnp.float32)
    d_gate_weight = summed[:, :hidden_units][None]
    d_up_weight = summed[:, hidden_units : 2 * hidden_units][None]
    d_down_weight = summed[:, 2 * hidden_units :].T[None]
    return (d_tokens, d_gate_weight, d_up_weight, d_down_weight)


def solution(mesh):
    placed = (
        P(("dp", "expert"), None),
        P(("dp", "expert"), None),
        P(("dp", "expert"), None),
        P(("dp", "expert"), None),
        P("expert", "dp", None),
        P("expert", "dp", None),
        P("expert", None, "dp"),
    )
    dense = mesh.shape["expert"] == Z * Y * CORES and mesh.shape["dp"] == 2
    return jax.shard_map(
        dense_body if dense else routed_body,
        mesh=mesh,
        in_specs=placed,
        out_specs=(
            P(("dp", "expert"), None),
            P("expert", "dp", None),
            P("expert", "dp", None),
            P("expert", None, "dp"),
        ),
        check_vma=False,
    )
```

```python
import functools

import jax
import jax.numpy as jnp
from jax import lax
from jax.experimental import pallas as pl
from jax.experimental.pallas import tpu as pltpu
from jax.sharding import PartitionSpec as P

F32 = jnp.float32
BF16 = jnp.bfloat16
LANES = 128
VMEM_BYTES = 56 * 1024 * 1024


def vmem():
    return pl.BlockSpec(memory_space=pltpu.VMEM)


def smem():
    return pl.BlockSpec(memory_space=pltpu.SMEM)


def hbm():
    return pl.BlockSpec(memory_space=pl.ANY)


def params():
    return pltpu.CompilerParams(vmem_limit_bytes=VMEM_BYTES)


def cost(flops, moved):
    return pl.CostEstimate(flops=int(flops), bytes_accessed=int(moved), transcendentals=0)


def dot(a, b, dims):
    return lax.dot_general(a, b, (dims, ((), ())), preferred_element_type=F32)


def pack_kernel(experts, tokens, d_output, combine, routes, gate, up, down, out, w_out, parts, turned, sems):
    rows, width = tokens.shape
    hidden_units = gate.shape[1]
    copies = []

    def start(source, target):
        copy = pltpu.make_async_copy(source, target, sems.at[len(copies)])
        copy.start()
        copies.append(copy)

    start(tokens, out.at[:, pl.ds(0, width)])
    start(d_output, out.at[:, pl.ds(width, width)])
    start(gate, w_out.at[:, pl.ds(0, hidden_units)])
    start(up, w_out.at[:, pl.ds(hidden_units, hidden_units)])
    turned[...] = down[...].T
    start(turned, w_out.at[:, pl.ds(2 * hidden_units, hidden_units)])
    line = lax.broadcasted_iota(jnp.int32, (LANES, rows), 0)
    expert = lax.rem(line, experts)
    dense = jnp.zeros((LANES, rows), F32)
    for k in range(routes.shape[0]):
        dense = dense + jnp.where(expert == routes[k : k + 1, :], combine[k : k + 1, :], 0.0)
    high = dense.astype(BF16).astype(F32)
    rest = dense - high
    middle = rest.astype(BF16).astype(F32)
    low = rest - middle
    whole = jnp.where(
        line < experts,
        high,
        jnp.where(line < 2 * experts, middle, jnp.where(line < 3 * experts, low, 0.0)),
    )
    parts[...] = whole.T.astype(BF16)
    start(parts, out.at[:, pl.ds(2 * width, LANES)])
    for c in copies:
        c.wait()


def pack(experts, tokens, d_output, combine, routes, gate, up, down):
    rows, width = tokens.shape
    size, hidden_units = gate.shape
    return pl.pallas_call(
        functools.partial(pack_kernel, experts),
        out_shape=[
            jax.ShapeDtypeStruct((rows, 2 * width + LANES), BF16),
            jax.ShapeDtypeStruct((size, 3 * hidden_units), BF16),
        ],
        in_specs=[hbm(), hbm(), vmem(), vmem(), hbm(), hbm(), vmem()],
        out_specs=[hbm(), hbm()],
        scratch_shapes=[
            pltpu.VMEM((rows, LANES), BF16),
            pltpu.VMEM((size, hidden_units), BF16),
            pltpu.SemaphoreType.DMA((6,)),
        ],
        cost_estimate=cost(0, 1 << 20),
        compiler_params=params(),
    )(tokens, d_output, combine.T, routes.T, gate, up, down)


def rows_kernel(experts, count, sizes, joined, scal, *refs):
    refs = list(refs)
    blocks = [refs.pop(0) for _ in range(count)]
    raw = [refs.pop(0) for _ in range(4)]
    out_rows = [refs.pop(0) for _ in sizes]
    kept = [refs.pop(0) for _ in range(3 if joined else 4)]
    block, held, grads, scaled, d_rows, in_sems, out_sems = refs
    part, expert = scal[0], scal[1]
    size, stacked = raw[0].shape
    hidden_units = stacked // 3
    both = 2 * hidden_units
    width = 2 * size
    rows = blocks[0].shape[0]
    arrivals = [
        pltpu.make_async_copy(b, block.at[pl.ds(i * rows, rows), :], in_sems.at[i]) for i, b in enumerate(blocks)
    ]
    weights = [pltpu.make_async_copy(raw[i], held.at[i], in_sems.at[count + i]) for i in range(4)]
    for c in arrivals + weights:
        c.start()
    leaving = []

    def leave(source, target):
        copy = pltpu.make_async_copy(source, target, out_sems.at[len(leaving)])
        copy.start()
        leaving.append(copy)

    for c in arrivals:
        c.wait()
    if joined:
        leave(block.at[:, pl.ds(0, width)], kept[2].at[:, pl.ds(stacked + width, width)])
    sides = [pl.multiple_of(part * size, size), pl.multiple_of((1 - part) * size, size)]
    parts = block[:, 2 * width :].astype(F32)
    lane = lax.broadcasted_iota(jnp.int32, parts.shape, 1)
    first = []
    for which in range(2):
        for c in weights[2 * which : 2 * which + 2]:
            c.wait()
        wanted = expert if which == 0 else expert + 1 - 2 * lax.rem(expert, 2)
        mine = (lax.rem(lane, experts) == wanted) & (lane < 3 * experts)
        weight = jnp.sum(jnp.where(mine, parts, 0.0), axis=1, keepdims=True)
        preact = None
        d_hidden = None
        for side in range(2):
            at = sides[side]
            grad = block[:, pl.ds(pl.multiple_of(width + at, size), size)]
            scaled_half = (weight * grad.astype(F32)).astype(BF16)
            scaled[which, :, pl.ds(at, size)] = scaled_half
            p = dot(block[:, pl.ds(at, size)], held[2 * which + side, :, :both], ((1,), (0,)))
            h = dot(scaled_half, held[2 * which + side, :, both:], ((1,), (0,)))
            preact = p if side == 0 else preact + p
            d_hidden = h if side == 0 else d_hidden + h
        first.append((preact, d_hidden))
    leave(scaled.at[0], kept[1])
    leave(scaled.at[1], kept[2].at[:, pl.ds(stacked, width)] if joined else kept[3])
    second = []
    for which in range(2):
        preact, d_hidden = first[which]
        gate_pre = preact[:, :hidden_units]
        up_pre = preact[:, hidden_units:]
        sig = jax.nn.sigmoid(gate_pre)
        silu = gate_pre * sig
        d_gate = (d_hidden * up_pre * sig * (1.0 + gate_pre * (1.0 - sig))).astype(BF16)
        d_up = (d_hidden * silu).astype(BF16)
        grads[which, :, :hidden_units] = d_gate
        grads[which, :, hidden_units:both] = d_up
        grads[which, :, both:] = (silu * up_pre).astype(BF16)
        d_preact = jnp.concatenate([d_gate, d_up], axis=1)
        second.append([dot(d_preact, held[2 * which + side, :, :both], ((1,), (1,))) for side in range(2)])
    leave(grads.at[0], kept[0])
    leave(grads.at[1], kept[2].at[:, pl.ds(0, stacked)] if joined else kept[2])
    for side in range(2):
        d_rows[:, pl.ds(sides[side], size)] = (second[0][side] + second[1][side]).astype(BF16)
    row = 0
    for out, n in zip(out_rows, sizes):
        leave(d_rows.at[pl.ds(row, n), :], out)
        row += n
    for c in leaving:
        c.wait()


def rows_call(experts, scal, groups, weights, joined=False):
    blocks = [b for group in groups for b in group]
    count = len(blocks)
    rows = blocks[0].shape[0]
    size, stacked = weights[0].shape
    total = count * rows
    sizes = [len(group) * rows for group in groups]
    sds = jax.ShapeDtypeStruct
    out = [sds((n, 2 * size), BF16) for n in sizes]
    out += [sds((total, stacked), BF16), sds((total, 2 * size), BF16)]
    out += [sds((total, stacked + 4 * size), BF16)] if joined else out[-2:]
    return pl.pallas_call(
        functools.partial(rows_kernel, experts, count, sizes, joined),
        out_shape=out,
        in_specs=[smem()] + [hbm()] * (count + 4),
        out_specs=[hbm()] * len(out),
        scratch_shapes=[
            pltpu.VMEM((total, blocks[0].shape[1]), BF16),
            pltpu.VMEM((4, size, stacked), BF16),
            pltpu.VMEM((2, total, stacked), BF16),
            pltpu.VMEM((2, total, 2 * size), BF16),
            pltpu.VMEM((total, 2 * size), BF16),
            pltpu.SemaphoreType.DMA((count + 4,)),
            pltpu.SemaphoreType.DMA((len(groups) + 5,)),
        ],
        cost_estimate=cost(24 * total * size * stacked * 2 * (10 if joined else 1), 1 << 20),
        compiler_params=params(),
    )(scal, *blocks, *weights)


def half_kernel(count, groups, joined, adds, at, sides, *refs):
    refs = list(refs)
    blocks = [refs.pop(0) for _ in range(count)]
    scaled = [refs.pop(0) for _ in range(groups)]
    grads = [refs.pop(0) for _ in range(groups)]
    last = refs.pop(0) if joined else None
    more = refs.pop(0) if adds else None
    out, lefts, made, extra, done, sems, out_sems = refs
    size, stacked = done.shape[1:]
    both = stacked // 3 * 2
    rows = blocks[0].shape[0]
    steps = done.shape[0]
    started = []

    def start(source, target):
        copy = pltpu.make_async_copy(source, target, sems.at[len(started)])
        copy.start()
        started.append(copy)
        return copy

    loads = [[[], []] for _ in range(steps)]
    offsets = [pl.multiple_of(sides[i] * size, size) for i in range(steps)]
    row = 0
    for i, b in enumerate(blocks):
        loads[0][0].append(start(b.at[:, pl.ds(offsets[0], size)], lefts.at[0, 0, pl.ds(row, rows), :]))
        row += rows
    if joined:
        first = pl.multiple_of(stacked + 2 * size + offsets[0], LANES)
        loads[0][0].append(start(last.at[:, pl.ds(first, size)], lefts.at[0, 0, pl.ds(row, rows), :]))
    row = 0
    for g in grads:
        loads[0][0].append(start(g, made.at[pl.ds(row, g.shape[0]), :]))
        row += g.shape[0]
    if joined:
        loads[0][0].append(start(last.at[:, pl.ds(0, stacked)], made.at[pl.ds(row, rows), :]))
    if adds:
        loads[0][0].append(start(more.at[pl.ds(at * size, size), :], extra))
    for step in range(steps):
        if step > 0:
            for i, b in enumerate(blocks):
                loads[step][0].append(
                    start(b.at[:, pl.ds(offsets[step], size)], lefts.at[step, 0, pl.ds(i * rows, rows), :])
                )
        row = 0
        for x in scaled:
            n = x.shape[0]
            loads[step][1].append(start(x.at[:, pl.ds(offsets[step], size)], lefts.at[step, 1, pl.ds(row, n), :]))
            row += n
        if joined:
            first = pl.multiple_of(stacked + offsets[step], LANES)
            loads[step][1].append(start(last.at[:, pl.ds(first, size)], lefts.at[step, 1, pl.ds(row, rows), :]))
    leaving = []
    for step in range(steps):
        for kind in range(2):
            for c in loads[step][kind]:
                c.wait()
            first, wide = (0, both) if kind == 0 else (both, stacked - both)
            new = dot(lefts[step, kind], made[:, first : first + wide], ((0,), (0,)))
            if adds:
                new = new + extra[:, first : first + wide].astype(F32)
            done[step, :, first : first + wide] = new.astype(BF16)
            copy = pltpu.make_async_copy(
                done.at[step, :, pl.ds(first, wide)],
                out.at[pl.ds(step * size, size), pl.ds(first, wide)],
                out_sems.at[len(leaving)],
            )
            copy.start()
            leaving.append(copy)
    for c in leaving:
        c.wait()


def half_call(sides, blocks, kept, last=None, more=None, at=0, weight=0):
    grads, scaled = [k[0] for k in kept], [k[1] for k in kept]
    size = scaled[0].shape[1] // 2
    stacked = grads[0].shape[1]
    rows = blocks[0].shape[0]
    extra = [a for a in (last, more) if a is not None]
    operands = [*blocks, *scaled, *grads, *extra]
    steps = sides.shape[0]
    total = (len(blocks) + (last is not None)) * rows
    return pl.pallas_call(
        functools.partial(half_kernel, len(blocks), len(kept), last is not None, more is not None, at),
        out_shape=jax.ShapeDtypeStruct((steps * size, stacked), BF16),
        in_specs=[smem()] + [hbm()] * len(operands),
        out_specs=hbm(),
        scratch_shapes=[
            pltpu.VMEM((steps, 2, total, size), BF16),
            pltpu.VMEM((total, stacked), BF16),
            pltpu.VMEM((size, stacked), BF16),
            pltpu.VMEM((steps, size, stacked), BF16),
            pltpu.SemaphoreType.DMA((steps * (len(blocks) + len(kept) + 2) + len(kept) + 2,)),
            pltpu.SemaphoreType.DMA((2 * steps,)),
        ],
        cost_estimate=cost(8 * weight * size * stacked * 1024 + 1024, 1024),
        compiler_params=params(),
    )(sides, *operands)


Z, Y, CORES = 4, 2, 2


def pairs_of(move):
    out = []
    for z in range(Z):
        for y in range(Y):
            for c in range(CORES):
                to = move(z, y, c)
                if to is not None:
                    out.append(((z * Y + y) * CORES + c, (to[0] * Y + to[1]) * CORES + to[2]))
    return out


def along_z(table):
    return pairs_of(lambda z, y, c: (table[z], y, c) if z in table else None)


SWAP_CORE = pairs_of(lambda z, y, c: (z, y, 1 - c))
SWAP_Y = pairs_of(lambda z, y, c: (z, 1 - y, c))
OUTER = along_z({0: 1, 1: 0, 2: 3, 3: 2})
INNER = along_z({1: 2, 2: 1})
OUTWARD = along_z({1: 0, 2: 3})
INWARD = along_z({0: 1, 3: 2})
SKIP_TO_OUTER = along_z({1: 3, 2: 0})


def after(value, *others):
    return lax.optimization_barrier((value,) + others)[0]


def dense_body(tokens, d_output, combine, routes, gate_weight, up_weight, down_weight):
    experts = lax.axis_size("expert")
    part = lax.axis_index("dp")
    expert = lax.axis_index("expert")
    z = expert // (Y * CORES)
    inner = (z == 1) | (z == 2)
    scal = jnp.stack([part, expert]).astype(jnp.int32)
    mine = part[None].astype(jnp.int32)
    other = (1 - part)[None].astype(jnp.int32)

    move = lambda a, pairs: lax.ppermute(a, "expert", pairs)
    across = lambda a: lax.ppermute(a, "dp", [(0, 1), (1, 0)])

    swap = lambda a: move(a, SWAP_CORE)
    own, w_own = pack(experts, tokens, d_output, combine, routes, gate_weight[0], up_weight[0], down_weight[0])
    w_part = across(w_own)

    b1 = move(own, OUTER)
    f1 = move(own, INNER)
    y0 = move(own, SWAP_Y)
    f2 = move(b1, INNER)
    y1 = move(after(b1, y0), SWAP_Y)
    g1 = move(f1, OUTWARD)
    b2 = jnp.where(inner, f1, g1)
    y2 = move(after(b2, y1, f2), SWAP_Y)
    g2 = move(f2, OUTWARD)

    w_core = swap(after(w_own, y1, f2))
    w_both = swap(after(w_part, y1, f2))
    weights = [w_own, w_part, w_core, w_both]
    p0, p1, p2, q0, *kept_a = rows_call(experts, scal, [[own], [b1], [b2], [y0]], weights)
    b3 = jnp.where(inner, f2, after(g2, p0))
    y3 = move(after(b3, y2), SWAP_Y)
    p3, q12, *kept_b = rows_call(experts, scal, [[b3], [y1, y2]], weights)

    blocks = [own, b1, b2, y0, b3, y1, y2]
    kept = [kept_a, kept_b]
    to_core = half_call(jnp.concatenate([other, mine]), blocks, [k[2:] for k in kept])
    y3 = after(y3, q12, to_core)
    r12 = move(after(q12, y3), SWAP_Y)
    rows = own.shape[0]
    r1, r2 = r12[:rows], r12[rows:]

    q3, *kept_d, joined = rows_call(experts, scal, [[y3]], weights, joined=True)
    last = swap(joined)
    all_blocks = blocks + [y3]
    all_kept = [k[:2] for k in kept] + [kept_d]
    got = swap(to_core)
    send = half_call(other, all_blocks, all_kept, last, got, weight=1)
    from_part = across(send)
    r3 = move(after(q3, send), SWAP_Y)
    r0 = move(after(q0, r3), SWAP_Y)
    keep = half_call(after(mine, send), all_blocks, all_kept, last, got, at=1)

    add = lambda *terms: sum(t.astype(F32) for t in terms).astype(BF16)
    s1 = add(p1, r1)
    s2 = add(p2, r2)
    s2 = add(s2, move(s2, INWARD))
    s3 = add(p3, r3)
    s3 = add(s3, move(s3, INWARD))
    d_weights = keep.astype(F32) + after(from_part, s2).astype(F32)
    hidden_units = gate_weight.shape[2]
    d_gate, d_up = d_weights[:, :hidden_units], d_weights[:, hidden_units : 2 * hidden_units]
    d_down = d_weights[:, 2 * hidden_units :].T
    d_tokens = add(after(p0, d_weights), r0, move(s1, OUTER), move(s2, INNER), move(s3, SKIP_TO_OUTER))
    return (d_tokens, d_gate[None], d_up[None], d_down[None])


def route_slots(routes, experts):
    matches = (routes[:, :, None] == jnp.arange(experts, dtype=jnp.int32)[None, None, :]).astype(
        jnp.int32
    )
    per_token = jnp.sum(matches, axis=1)
    earlier = jnp.cumsum(per_token, axis=0) - per_token
    return jnp.sum(matches * earlier[:, None, :], axis=2)


def row_work(row_inputs, row_grads, gate_up, down_matrix):
    hidden_units = down_matrix.shape[0]
    preact = jnp.dot(row_inputs, gate_up, preferred_element_type=jnp.float32)
    gate_pre = preact[:, :hidden_units]
    up_pre = preact[:, hidden_units:]
    gate_sigmoid = jax.nn.sigmoid(gate_pre)
    hidden = (gate_pre * gate_sigmoid * up_pre).astype(jnp.bfloat16)
    d_hidden = jnp.dot(row_grads, down_matrix.T, preferred_element_type=jnp.float32)
    d_gate_pre = d_hidden * up_pre * gate_sigmoid * (1.0 + gate_pre * (1.0 - gate_sigmoid))
    d_up_pre = d_hidden * gate_pre * gate_sigmoid
    d_preact = jnp.concatenate([d_gate_pre, d_up_pre], axis=1).astype(jnp.bfloat16)
    d_rows = jnp.dot(d_preact, gate_up.T, preferred_element_type=jnp.float32).astype(jnp.bfloat16)
    return (d_rows, hidden, d_preact)


def routed_body(tokens, d_output, combine, routes, gate_weight, up_weight, down_weight):
    experts = lax.axis_size("expert")
    tok_count = tokens.shape[0]
    model_width = tokens.shape[1]
    top_count = routes.shape[1]
    capacity = max(2, (9 * tok_count * top_count + 8 * experts - 1) // (8 * experts))
    slot_count = experts * capacity
    slot_index = route_slots(routes, experts)
    position = (routes * capacity + slot_index).reshape(-1)
    spread_inputs = jnp.repeat(tokens, top_count, axis=0)
    scaled = (
        (combine[:, :, None] * d_output[:, None, :].astype(jnp.float32))
        .astype(jnp.bfloat16)
        .reshape(-1, model_width)
    )
    send_inputs = (
        jnp.zeros((slot_count, model_width), jnp.bfloat16)
        .at[position]
        .set(spread_inputs)
        .reshape(experts, capacity, model_width)
    )
    send_grads = (
        jnp.zeros((slot_count, model_width), jnp.bfloat16)
        .at[position]
        .set(scaled)
        .reshape(experts, capacity, model_width)
    )
    whole_gate, whole_up, whole_down = (
        lax.all_gather(gate_weight, "dp", axis=1, tiled=True),
        lax.all_gather(up_weight, "dp", axis=1, tiled=True),
        lax.all_gather(down_weight, "dp", axis=2, tiled=True),
    )
    gate_up = jnp.concatenate([whole_gate[0], whole_up[0]], axis=1)
    down_matrix = whole_down[0]
    hidden_units = down_matrix.shape[0]
    recv_inputs, recv_grads = (
        lax.all_to_all(send_inputs, "expert", split_axis=0, concat_axis=0, tiled=True),
        lax.all_to_all(send_grads, "expert", split_axis=0, concat_axis=0, tiled=True),
    )
    flat_inputs = recv_inputs.reshape(-1, model_width)
    flat_grads = recv_grads.reshape(-1, model_width)
    d_rows, hidden, d_preact = row_work(flat_inputs, flat_grads, gate_up, down_matrix)
    returned = lax.all_to_all(
        d_rows.reshape(experts, capacity, model_width),
        "expert",
        split_axis=0,
        concat_axis=0,
        tiled=True,
    )
    route_rows = returned.reshape(-1, model_width)[position].reshape(
        tok_count, top_count, model_width
    )
    d_tokens = jnp.sum(route_rows.astype(jnp.float32), axis=1).astype(jnp.bfloat16)
    gate_up_grad = jnp.dot(flat_inputs.T, d_preact, preferred_element_type=jnp.float32)
    down_grad = jnp.dot(flat_grads.T, hidden, preferred_element_type=jnp.float32)
    stacked = jnp.concatenate([gate_up_grad, down_grad], axis=1)
    summed = lax.psum_scatter(
        stacked.astype(jnp.bfloat16), "dp", scatter_dimension=0, tiled=True
    ).astype(jnp.float32)
    d_gate_weight = summed[:, :hidden_units][None]
    d_up_weight = summed[:, hidden_units : 2 * hidden_units][None]
    d_down_weight = summed[:, 2 * hidden_units :].T[None]
    return (d_tokens, d_gate_weight, d_up_weight, d_down_weight)


def solution(mesh):
    placed = (
        P(("dp", "expert"), None),
        P(("dp", "expert"), None),
        P(("dp", "expert"), None),
        P(("dp", "expert"), None),
        P("expert", "dp", None),
        P("expert", "dp", None),
        P("expert", None, "dp"),
    )
    dense = mesh.shape["expert"] == Z * Y * CORES and mesh.shape["dp"] == 2
    return jax.shard_map(
        dense_body if dense else routed_body,
        mesh=mesh,
        in_specs=placed,
        out_specs=(
            P(("dp", "expert"), None),
            P("expert", "dp", None),
            P("expert", "dp", None),
            P("expert", None, "dp"),
        ),
        check_vma=False,
    )
```

```python
import functools

import jax
import jax.numpy as jnp
from jax import lax
from jax.experimental import pallas as pl
from jax.experimental.pallas import tpu as pltpu
from jax.sharding import PartitionSpec as P

F32 = jnp.float32
BF16 = jnp.bfloat16
LANES = 128
VMEM_BYTES = 56 * 1024 * 1024


def vmem():
    return pl.BlockSpec(memory_space=pltpu.VMEM)


def smem():
    return pl.BlockSpec(memory_space=pltpu.SMEM)


def hbm():
    return pl.BlockSpec(memory_space=pl.ANY)


def params():
    return pltpu.CompilerParams(vmem_limit_bytes=VMEM_BYTES)


def cost(flops, moved):
    return pl.CostEstimate(flops=int(flops), bytes_accessed=int(moved), transcendentals=0)


def dot(a, b, dims):
    return lax.dot_general(a, b, (dims, ((), ())), preferred_element_type=F32)


def pack_kernel(experts, tokens, d_output, combine, routes, gate, up, down, out, w_out, parts, turned, sems):
    rows, width = tokens.shape
    hidden_units = gate.shape[1]
    copies = []

    def start(source, target):
        copy = pltpu.make_async_copy(source, target, sems.at[len(copies)])
        copy.start()
        copies.append(copy)

    start(tokens, out.at[:, pl.ds(0, width)])
    start(d_output, out.at[:, pl.ds(width, width)])
    start(gate, w_out.at[:, pl.ds(0, hidden_units)])
    start(up, w_out.at[:, pl.ds(hidden_units, hidden_units)])
    turned[...] = down[...].T
    start(turned, w_out.at[:, pl.ds(2 * hidden_units, hidden_units)])
    line = lax.broadcasted_iota(jnp.int32, (LANES, rows), 0)
    expert = lax.rem(line, experts)
    dense = jnp.zeros((LANES, rows), F32)
    for k in range(routes.shape[0]):
        dense = dense + jnp.where(expert == routes[k : k + 1, :], combine[k : k + 1, :], 0.0)
    high = dense.astype(BF16).astype(F32)
    rest = dense - high
    middle = rest.astype(BF16).astype(F32)
    low = rest - middle
    whole = jnp.where(
        line < experts,
        high,
        jnp.where(line < 2 * experts, middle, jnp.where(line < 3 * experts, low, 0.0)),
    )
    parts[...] = whole.T.astype(BF16)
    start(parts, out.at[:, pl.ds(2 * width, LANES)])
    for c in copies:
        c.wait()


def pack(experts, tokens, d_output, combine, routes, gate, up, down):
    rows, width = tokens.shape
    size, hidden_units = gate.shape
    return pl.pallas_call(
        functools.partial(pack_kernel, experts),
        out_shape=[
            jax.ShapeDtypeStruct((rows, 2 * width + LANES), BF16),
            jax.ShapeDtypeStruct((size, 3 * hidden_units), BF16),
        ],
        in_specs=[vmem()] * 7,
        out_specs=[hbm(), hbm()],
        scratch_shapes=[
            pltpu.VMEM((rows, LANES), BF16),
            pltpu.VMEM((size, hidden_units), BF16),
            pltpu.SemaphoreType.DMA((6,)),
        ],
        cost_estimate=cost(0, 1 << 20),
        compiler_params=params(),
    )(tokens, d_output, combine.T, routes.T, gate, up, down)


def rows_kernel(experts, count, sizes, joined, scal, *refs):
    refs = list(refs)
    blocks = [refs.pop(0) for _ in range(count)]
    raw = [refs.pop(0) for _ in range(4)]
    out_rows = [refs.pop(0) for _ in sizes]
    kept = [refs.pop(0) for _ in range(3 if joined else 4)]
    block, held, grads, scaled, d_rows, in_sems, out_sems = refs
    part, expert = scal[0], scal[1]
    size, stacked = raw[0].shape
    hidden_units = stacked // 3
    both = 2 * hidden_units
    width = 2 * size
    rows = blocks[0].shape[0]
    arrivals = [
        pltpu.make_async_copy(b, block.at[pl.ds(i * rows, rows), :], in_sems.at[i]) for i, b in enumerate(blocks)
    ]
    weights = [pltpu.make_async_copy(raw[i], held.at[i], in_sems.at[count + i]) for i in range(4)]
    for c in arrivals + weights:
        c.start()
    leaving = []

    def leave(source, target):
        copy = pltpu.make_async_copy(source, target, out_sems.at[len(leaving)])
        copy.start()
        leaving.append(copy)

    for c in arrivals:
        c.wait()
    if joined:
        leave(block.at[:, pl.ds(0, width)], kept[2].at[:, pl.ds(stacked + width, width)])
    sides = [pl.multiple_of(part * size, size), pl.multiple_of((1 - part) * size, size)]
    parts = block[:, 2 * width :].astype(F32)
    lane = lax.broadcasted_iota(jnp.int32, parts.shape, 1)
    first = []
    for which in range(2):
        for c in weights[2 * which : 2 * which + 2]:
            c.wait()
        wanted = expert if which == 0 else expert + 1 - 2 * lax.rem(expert, 2)
        mine = (lax.rem(lane, experts) == wanted) & (lane < 3 * experts)
        weight = jnp.sum(jnp.where(mine, parts, 0.0), axis=1, keepdims=True)
        preact = None
        d_hidden = None
        for side in range(2):
            at = sides[side]
            grad = block[:, pl.ds(pl.multiple_of(width + at, size), size)]
            scaled_half = (weight * grad.astype(F32)).astype(BF16)
            scaled[which, :, pl.ds(at, size)] = scaled_half
            p = dot(block[:, pl.ds(at, size)], held[2 * which + side, :, :both], ((1,), (0,)))
            h = dot(scaled_half, held[2 * which + side, :, both:], ((1,), (0,)))
            preact = p if side == 0 else preact + p
            d_hidden = h if side == 0 else d_hidden + h
        first.append((preact, d_hidden))
    leave(scaled.at[0], kept[1])
    leave(scaled.at[1], kept[2].at[:, pl.ds(stacked, width)] if joined else kept[3])
    second = []
    for which in range(2):
        preact, d_hidden = first[which]
        gate_pre = preact[:, :hidden_units]
        up_pre = preact[:, hidden_units:]
        sig = jax.nn.sigmoid(gate_pre)
        silu = gate_pre * sig
        d_gate = (d_hidden * up_pre * sig * (1.0 + gate_pre * (1.0 - sig))).astype(BF16)
        d_up = (d_hidden * silu).astype(BF16)
        grads[which, :, :hidden_units] = d_gate
        grads[which, :, hidden_units:both] = d_up
        grads[which, :, both:] = (silu * up_pre).astype(BF16)
        d_preact = jnp.concatenate([d_gate, d_up], axis=1)
        second.append([dot(d_preact, held[2 * which + side, :, :both], ((1,), (1,))) for side in range(2)])
    leave(grads.at[0], kept[0])
    leave(grads.at[1], kept[2].at[:, pl.ds(0, stacked)] if joined else kept[2])
    for side in range(2):
        d_rows[:, pl.ds(sides[side], size)] = (second[0][side] + second[1][side]).astype(BF16)
    row = 0
    for out, n in zip(out_rows, sizes):
        leave(d_rows.at[pl.ds(row, n), :], out)
        row += n
    for c in leaving:
        c.wait()


def rows_call(experts, scal, groups, weights, joined=False):
    blocks = [b for group in groups for b in group]
    count = len(blocks)
    rows = blocks[0].shape[0]
    size, stacked = weights[0].shape
    total = count * rows
    sizes = [len(group) * rows for group in groups]
    sds = jax.ShapeDtypeStruct
    out = [sds((n, 2 * size), BF16) for n in sizes]
    out += [sds((total, stacked), BF16), sds((total, 2 * size), BF16)]
    out += [sds((total, stacked + 4 * size), BF16)] if joined else out[-2:]
    return pl.pallas_call(
        functools.partial(rows_kernel, experts, count, sizes, joined),
        out_shape=out,
        in_specs=[smem()] + [hbm()] * (count + 4),
        out_specs=[hbm()] * len(out),
        scratch_shapes=[
            pltpu.VMEM((total, blocks[0].shape[1]), BF16),
            pltpu.VMEM((4, size, stacked), BF16),
            pltpu.VMEM((2, total, stacked), BF16),
            pltpu.VMEM((2, total, 2 * size), BF16),
            pltpu.VMEM((total, 2 * size), BF16),
            pltpu.SemaphoreType.DMA((count + 4,)),
            pltpu.SemaphoreType.DMA((len(groups) + 5,)),
        ],
        cost_estimate=cost(24 * total * size * stacked * 2 * (10 if joined else 1), 1 << 20),
        compiler_params=params(),
    )(scal, *blocks, *weights)


def half_kernel(count, groups, joined, adds, at, sides, *refs):
    refs = list(refs)
    blocks = [refs.pop(0) for _ in range(count)]
    scaled = [refs.pop(0) for _ in range(groups)]
    grads = [refs.pop(0) for _ in range(groups)]
    last = refs.pop(0) if joined else None
    more = refs.pop(0) if adds else None
    out, lefts, made, extra, done, sems, out_sems = refs
    size, stacked = done.shape[1:]
    both = stacked // 3 * 2
    rows = blocks[0].shape[0]
    steps = done.shape[0]
    started = []

    def start(source, target):
        copy = pltpu.make_async_copy(source, target, sems.at[len(started)])
        copy.start()
        started.append(copy)
        return copy

    loads = [[[], []] for _ in range(steps)]
    offsets = [pl.multiple_of(sides[i] * size, size) for i in range(steps)]
    row = 0
    for i, b in enumerate(blocks):
        loads[0][0].append(start(b.at[:, pl.ds(offsets[0], size)], lefts.at[0, 0, pl.ds(row, rows), :]))
        row += rows
    if joined:
        first = pl.multiple_of(stacked + 2 * size + offsets[0], LANES)
        loads[0][0].append(start(last.at[:, pl.ds(first, size)], lefts.at[0, 0, pl.ds(row, rows), :]))
    row = 0
    for g in grads:
        loads[0][0].append(start(g, made.at[pl.ds(row, g.shape[0]), :]))
        row += g.shape[0]
    if joined:
        loads[0][0].append(start(last.at[:, pl.ds(0, stacked)], made.at[pl.ds(row, rows), :]))
    if adds:
        loads[0][0].append(start(more.at[pl.ds(at * size, size), :], extra))
    for step in range(steps):
        if step > 0:
            for i, b in enumerate(blocks):
                loads[step][0].append(
                    start(b.at[:, pl.ds(offsets[step], size)], lefts.at[step, 0, pl.ds(i * rows, rows), :])
                )
        row = 0
        for x in scaled:
            n = x.shape[0]
            loads[step][1].append(start(x.at[:, pl.ds(offsets[step], size)], lefts.at[step, 1, pl.ds(row, n), :]))
            row += n
        if joined:
            first = pl.multiple_of(stacked + offsets[step], LANES)
            loads[step][1].append(start(last.at[:, pl.ds(first, size)], lefts.at[step, 1, pl.ds(row, rows), :]))
    leaving = []
    for step in range(steps):
        for kind in range(2):
            for c in loads[step][kind]:
                c.wait()
            first, wide = (0, both) if kind == 0 else (both, stacked - both)
            new = dot(lefts[step, kind], made[:, first : first + wide], ((0,), (0,)))
            if adds:
                new = new + extra[:, first : first + wide].astype(F32)
            done[step, :, first : first + wide] = new.astype(BF16)
            copy = pltpu.make_async_copy(
                done.at[step, :, pl.ds(first, wide)],
                out.at[pl.ds(step * size, size), pl.ds(first, wide)],
                out_sems.at[len(leaving)],
            )
            copy.start()
            leaving.append(copy)
    for c in leaving:
        c.wait()


def half_call(sides, blocks, kept, last=None, more=None, at=0, weight=0):
    grads, scaled = [k[0] for k in kept], [k[1] for k in kept]
    size = scaled[0].shape[1] // 2
    stacked = grads[0].shape[1]
    rows = blocks[0].shape[0]
    extra = [a for a in (last, more) if a is not None]
    operands = [*blocks, *scaled, *grads, *extra]
    steps = sides.shape[0]
    total = (len(blocks) + (last is not None)) * rows
    return pl.pallas_call(
        functools.partial(half_kernel, len(blocks), len(kept), last is not None, more is not None, at),
        out_shape=jax.ShapeDtypeStruct((steps * size, stacked), BF16),
        in_specs=[smem()] + [hbm()] * len(operands),
        out_specs=hbm(),
        scratch_shapes=[
            pltpu.VMEM((steps, 2, total, size), BF16),
            pltpu.VMEM((total, stacked), BF16),
            pltpu.VMEM((size, stacked), BF16),
            pltpu.VMEM((steps, size, stacked), BF16),
            pltpu.SemaphoreType.DMA((steps * (len(blocks) + len(kept) + 2) + len(kept) + 2,)),
            pltpu.SemaphoreType.DMA((2 * steps,)),
        ],
        cost_estimate=cost(8 * weight * size * stacked * 1024 + 1024, 1024),
        compiler_params=params(),
    )(sides, *operands)


Z, Y, CORES = 4, 2, 2


def pairs_of(move):
    out = []
    for z in range(Z):
        for y in range(Y):
            for c in range(CORES):
                to = move(z, y, c)
                if to is not None:
                    out.append(((z * Y + y) * CORES + c, (to[0] * Y + to[1]) * CORES + to[2]))
    return out


def along_z(table):
    return pairs_of(lambda z, y, c: (table[z], y, c) if z in table else None)


SWAP_CORE = pairs_of(lambda z, y, c: (z, y, 1 - c))
SWAP_Y = pairs_of(lambda z, y, c: (z, 1 - y, c))
OUTER = along_z({0: 1, 1: 0, 2: 3, 3: 2})
INNER = along_z({1: 2, 2: 1})
OUTWARD = along_z({1: 0, 2: 3})
INWARD = along_z({0: 1, 3: 2})
SKIP_TO_OUTER = along_z({1: 3, 2: 0})


def after(value, *others):
    return lax.optimization_barrier((value,) + others)[0]


def dense_body(tokens, d_output, combine, routes, gate_weight, up_weight, down_weight):
    experts = lax.axis_size("expert")
    part = lax.axis_index("dp")
    expert = lax.axis_index("expert")
    z = expert // (Y * CORES)
    inner = (z == 1) | (z == 2)
    scal = jnp.stack([part, expert]).astype(jnp.int32)
    mine = part[None].astype(jnp.int32)
    other = (1 - part)[None].astype(jnp.int32)

    move = lambda a, pairs: lax.ppermute(a, "expert", pairs)
    across = lambda a: lax.ppermute(a, "dp", [(0, 1), (1, 0)])

    swap = lambda a: move(a, SWAP_CORE)
    own, w_own = pack(experts, tokens, d_output, combine, routes, gate_weight[0], up_weight[0], down_weight[0])
    w_part = across(w_own)

    b1 = move(own, OUTER)
    f1 = move(own, INNER)
    y0 = move(own, SWAP_Y)
    f2 = move(b1, INNER)
    y1 = move(after(b1, y0), SWAP_Y)
    g1 = move(f1, OUTWARD)
    b2 = jnp.where(inner, f1, g1)
    y2 = move(after(b2, y1, f2), SWAP_Y)
    g2 = move(f2, OUTWARD)

    w_core = swap(after(w_own, y1, f2))
    w_both = swap(after(w_part, y1, f2))
    weights = [w_own, w_part, w_core, w_both]
    p0, p1, p2, q01, *kept_a = rows_call(experts, scal, [[own], [b1], [b2], [y0, y1]], weights)
    b3 = jnp.where(inner, f2, after(g2, p0))
    y3 = move(after(b3, y2), SWAP_Y)
    p3, q2, *kept_b = rows_call(experts, scal, [[b3], [y2]], weights)

    blocks = [own, b1, b2, y0, y1, b3, y2]
    kept = [kept_a, kept_b]
    to_core = half_call(jnp.concatenate([other, mine]), blocks, [k[2:] for k in kept])
    y3 = after(y3, q2, to_core)
    r2 = move(after(q2, y3), SWAP_Y)

    q3, *kept_d, joined = rows_call(experts, scal, [[y3]], weights, joined=True)
    last = swap(joined)
    all_blocks = blocks + [y3]
    all_kept = [k[:2] for k in kept] + [kept_d]
    got = swap(to_core)
    send = half_call(other, all_blocks, all_kept, last, got, weight=1)
    from_part = across(send)
    r3 = move(after(q3, send), SWAP_Y)
    r01 = move(after(q01, r3), SWAP_Y)
    rows = own.shape[0]
    r0, r1 = r01[:rows], r01[rows:]
    keep = half_call(after(mine, send), all_blocks, all_kept, last, got, at=1)

    add = lambda *terms: sum(t.astype(F32) for t in terms).astype(BF16)
    s1 = add(p1, r1)
    s2 = add(p2, r2)
    s2 = add(s2, move(s2, INWARD))
    s3 = add(p3, r3)
    s3 = add(s3, move(s3, INWARD))
    d_weights = keep.astype(F32) + after(from_part, s2).astype(F32)
    hidden_units = gate_weight.shape[2]
    d_gate, d_up = d_weights[:, :hidden_units], d_weights[:, hidden_units : 2 * hidden_units]
    d_down = d_weights[:, 2 * hidden_units :].T
    d_tokens = add(after(p0, d_weights), r0, move(s1, OUTER), move(s2, INNER), move(s3, SKIP_TO_OUTER))
    return (d_tokens, d_gate[None], d_up[None], d_down[None])


def route_slots(routes, experts):
    matches = (routes[:, :, None] == jnp.arange(experts, dtype=jnp.int32)[None, None, :]).astype(
        jnp.int32
    )
    per_token = jnp.sum(matches, axis=1)
    earlier = jnp.cumsum(per_token, axis=0) - per_token
    return jnp.sum(matches * earlier[:, None, :], axis=2)


def row_work(row_inputs, row_grads, gate_up, down_matrix):
    hidden_units = down_matrix.shape[0]
    preact = jnp.dot(row_inputs, gate_up, preferred_element_type=jnp.float32)
    gate_pre = preact[:, :hidden_units]
    up_pre = preact[:, hidden_units:]
    gate_sigmoid = jax.nn.sigmoid(gate_pre)
    hidden = (gate_pre * gate_sigmoid * up_pre).astype(jnp.bfloat16)
    d_hidden = jnp.dot(row_grads, down_matrix.T, preferred_element_type=jnp.float32)
    d_gate_pre = d_hidden * up_pre * gate_sigmoid * (1.0 + gate_pre * (1.0 - gate_sigmoid))
    d_up_pre = d_hidden * gate_pre * gate_sigmoid
    d_preact = jnp.concatenate([d_gate_pre, d_up_pre], axis=1).astype(jnp.bfloat16)
    d_rows = jnp.dot(d_preact, gate_up.T, preferred_element_type=jnp.float32).astype(jnp.bfloat16)
    return (d_rows, hidden, d_preact)


def routed_body(tokens, d_output, combine, routes, gate_weight, up_weight, down_weight):
    experts = lax.axis_size("expert")
    tok_count = tokens.shape[0]
    model_width = tokens.shape[1]
    top_count = routes.shape[1]
    capacity = max(2, (9 * tok_count * top_count + 8 * experts - 1) // (8 * experts))
    slot_count = experts * capacity
    slot_index = route_slots(routes, experts)
    position = (routes * capacity + slot_index).reshape(-1)
    spread_inputs = jnp.repeat(tokens, top_count, axis=0)
    scaled = (
        (combine[:, :, None] * d_output[:, None, :].astype(jnp.float32))
        .astype(jnp.bfloat16)
        .reshape(-1, model_width)
    )
    send_inputs = (
        jnp.zeros((slot_count, model_width), jnp.bfloat16)
        .at[position]
        .set(spread_inputs)
        .reshape(experts, capacity, model_width)
    )
    send_grads = (
        jnp.zeros((slot_count, model_width), jnp.bfloat16)
        .at[position]
        .set(scaled)
        .reshape(experts, capacity, model_width)
    )
    whole_gate, whole_up, whole_down = (
        lax.all_gather(gate_weight, "dp", axis=1, tiled=True),
        lax.all_gather(up_weight, "dp", axis=1, tiled=True),
        lax.all_gather(down_weight, "dp", axis=2, tiled=True),
    )
    gate_up = jnp.concatenate([whole_gate[0], whole_up[0]], axis=1)
    down_matrix = whole_down[0]
    hidden_units = down_matrix.shape[0]
    recv_inputs, recv_grads = (
        lax.all_to_all(send_inputs, "expert", split_axis=0, concat_axis=0, tiled=True),
        lax.all_to_all(send_grads, "expert", split_axis=0, concat_axis=0, tiled=True),
    )
    flat_inputs = recv_inputs.reshape(-1, model_width)
    flat_grads = recv_grads.reshape(-1, model_width)
    d_rows, hidden, d_preact = row_work(flat_inputs, flat_grads, gate_up, down_matrix)
    returned = lax.all_to_all(
        d_rows.reshape(experts, capacity, model_width),
        "expert",
        split_axis=0,
        concat_axis=0,
        tiled=True,
    )
    route_rows = returned.reshape(-1, model_width)[position].reshape(
        tok_count, top_count, model_width
    )
    d_tokens = jnp.sum(route_rows.astype(jnp.float32), axis=1).astype(jnp.bfloat16)
    gate_up_grad = jnp.dot(flat_inputs.T, d_preact, preferred_element_type=jnp.float32)
    down_grad = jnp.dot(flat_grads.T, hidden, preferred_element_type=jnp.float32)
    stacked = jnp.concatenate([gate_up_grad, down_grad], axis=1)
    summed = lax.psum_scatter(
        stacked.astype(jnp.bfloat16), "dp", scatter_dimension=0, tiled=True
    ).astype(jnp.float32)
    d_gate_weight = summed[:, :hidden_units][None]
    d_up_weight = summed[:, hidden_units : 2 * hidden_units][None]
    d_down_weight = summed[:, 2 * hidden_units :].T[None]
    return (d_tokens, d_gate_weight, d_up_weight, d_down_weight)


def solution(mesh):
    placed = (
        P(("dp", "expert"), None),
        P(("dp", "expert"), None),
        P(("dp", "expert"), None),
        P(("dp", "expert"), None),
        P("expert", "dp", None),
        P("expert", "dp", None),
        P("expert", None, "dp"),
    )
    dense = mesh.shape["expert"] == Z * Y * CORES and mesh.shape["dp"] == 2
    return jax.shard_map(
        dense_body if dense else routed_body,
        mesh=mesh,
        in_specs=placed,
        out_specs=(
            P(("dp", "expert"), None),
            P("expert", "dp", None),
            P("expert", "dp", None),
            P("expert", None, "dp"),
        ),
        check_vma=False,
    )
```

```python
import functools

import jax
import jax.numpy as jnp
from jax import lax
from jax.experimental import pallas as pl
from jax.experimental.pallas import tpu as pltpu
from jax.sharding import PartitionSpec as P

F32 = jnp.float32
BF16 = jnp.bfloat16
LANES = 128
VMEM_BYTES = 56 * 1024 * 1024


def vmem():
    return pl.BlockSpec(memory_space=pltpu.VMEM)


def smem():
    return pl.BlockSpec(memory_space=pltpu.SMEM)


def hbm():
    return pl.BlockSpec(memory_space=pl.ANY)


def params():
    return pltpu.CompilerParams(vmem_limit_bytes=VMEM_BYTES)


def cost(flops, moved):
    return pl.CostEstimate(flops=int(flops), bytes_accessed=int(moved), transcendentals=0)


def dot(a, b, dims):
    return lax.dot_general(a, b, (dims, ((), ())), preferred_element_type=F32)


def pack_kernel(experts, tokens, d_output, combine, routes, gate, up, down, out, w_out, parts, turned, sems):
    rows, width = tokens.shape
    hidden_units = gate.shape[1]
    copies = []

    def start(source, target):
        copy = pltpu.make_async_copy(source, target, sems.at[len(copies)])
        copy.start()
        copies.append(copy)

    start(tokens, out.at[:, pl.ds(0, width)])
    start(d_output, out.at[:, pl.ds(width, width)])
    start(gate, w_out.at[:, pl.ds(0, hidden_units)])
    start(up, w_out.at[:, pl.ds(hidden_units, hidden_units)])
    turned[...] = down[...].T
    start(turned, w_out.at[:, pl.ds(2 * hidden_units, hidden_units)])
    line = lax.broadcasted_iota(jnp.int32, (LANES, rows), 0)
    expert = lax.rem(line, experts)
    dense = jnp.zeros((LANES, rows), F32)
    for k in range(routes.shape[0]):
        dense = dense + jnp.where(expert == routes[k : k + 1, :], combine[k : k + 1, :], 0.0)
    high = dense.astype(BF16).astype(F32)
    rest = dense - high
    middle = rest.astype(BF16).astype(F32)
    low = rest - middle
    whole = jnp.where(
        line < experts,
        high,
        jnp.where(line < 2 * experts, middle, jnp.where(line < 3 * experts, low, 0.0)),
    )
    parts[...] = whole.T.astype(BF16)
    start(parts, out.at[:, pl.ds(2 * width, LANES)])
    for c in copies:
        c.wait()


def pack(experts, tokens, d_output, combine, routes, gate, up, down):
    rows, width = tokens.shape
    size, hidden_units = gate.shape
    return pl.pallas_call(
        functools.partial(pack_kernel, experts),
        out_shape=[
            jax.ShapeDtypeStruct((rows, 2 * width + LANES), BF16),
            jax.ShapeDtypeStruct((size, 3 * hidden_units), BF16),
        ],
        in_specs=[vmem()] * 7,
        out_specs=[hbm(), hbm()],
        scratch_shapes=[
            pltpu.VMEM((rows, LANES), BF16),
            pltpu.VMEM((size, hidden_units), BF16),
            pltpu.SemaphoreType.DMA((6,)),
        ],
        cost_estimate=cost(0, 1 << 20),
        compiler_params=params(),
    )(tokens, d_output, combine.T, routes.T, gate, up, down)


def rows_kernel(experts, count, sizes, which, scal, *refs):
    refs = list(refs)
    joined, closing = which == (1,), which == (0,)
    blocks = [refs.pop(0) for _ in range(count)]
    raw = [refs.pop(0) for _ in range(2 * len(which))]
    partial = refs.pop(0) if closing else None
    out_rows = [refs.pop(0) for _ in sizes]
    kept = [refs.pop(0) for _ in range(1 if joined else 2 * len(which))]
    block, held, grads, scaled, d_rows, in_sems, out_sems = refs[:7]
    before = refs[7] if closing else None
    part, expert = scal[0], scal[1]
    size, stacked = raw[0].shape
    hidden_units = stacked // 3
    both = 2 * hidden_units
    width = 2 * size
    rows = blocks[0].shape[0]
    arrivals = [
        pltpu.make_async_copy(b, block.at[pl.ds(i * rows, rows), :], in_sems.at[i]) for i, b in enumerate(blocks)
    ]
    weights = [pltpu.make_async_copy(w, held.at[i], in_sems.at[count + i]) for i, w in enumerate(raw)]
    for c in arrivals + weights:
        c.start()
    if closing:
        earlier = pltpu.make_async_copy(partial, before, in_sems.at[count + len(raw)])
        earlier.start()
    leaving = []

    def leave(source, target):
        copy = pltpu.make_async_copy(source, target, out_sems.at[len(leaving)])
        copy.start()
        leaving.append(copy)

    for c in arrivals:
        c.wait()
    if joined:
        leave(block.at[:, pl.ds(0, width)], kept[0].at[:, pl.ds(stacked + width, width)])
    sides = [pl.multiple_of(part * size, size), pl.multiple_of((1 - part) * size, size)]
    parts = block[:, 2 * width :].astype(F32)
    lane = lax.broadcasted_iota(jnp.int32, parts.shape, 1)
    first = []
    for i, one in enumerate(which):
        for c in weights[2 * i : 2 * i + 2]:
            c.wait()
        wanted = expert if one == 0 else expert + 1 - 2 * lax.rem(expert, 2)
        mine = (lax.rem(lane, experts) == wanted) & (lane < 3 * experts)
        weight = jnp.sum(jnp.where(mine, parts, 0.0), axis=1, keepdims=True)
        preact = None
        d_hidden = None
        for side in range(2):
            at = sides[side]
            grad = block[:, pl.ds(pl.multiple_of(width + at, size), size)]
            scaled_half = (weight * grad.astype(F32)).astype(BF16)
            scaled[i, :, pl.ds(at, size)] = scaled_half
            p = dot(block[:, pl.ds(at, size)], held[2 * i + side, :, :both], ((1,), (0,)))
            h = dot(scaled_half, held[2 * i + side, :, both:], ((1,), (0,)))
            preact = p if side == 0 else preact + p
            d_hidden = h if side == 0 else d_hidden + h
        first.append((preact, d_hidden))
    for i in range(len(which)):
        leave(scaled.at[i], kept[0].at[:, pl.ds(stacked, width)] if joined else kept[2 * i + 1])
    second = []
    for i in range(len(which)):
        preact, d_hidden = first[i]
        gate_pre = preact[:, :hidden_units]
        up_pre = preact[:, hidden_units:]
        sig = jax.nn.sigmoid(gate_pre)
        silu = gate_pre * sig
        d_gate = (d_hidden * up_pre * sig * (1.0 + gate_pre * (1.0 - sig))).astype(BF16)
        d_up = (d_hidden * silu).astype(BF16)
        grads[i, :, :hidden_units] = d_gate
        grads[i, :, hidden_units:both] = d_up
        grads[i, :, both:] = (silu * up_pre).astype(BF16)
        d_preact = jnp.concatenate([d_gate, d_up], axis=1)
        second.append([dot(d_preact, held[2 * i + side, :, :both], ((1,), (1,))) for side in range(2)])
    for i in range(len(which)):
        leave(grads.at[i], kept[0].at[:, pl.ds(0, stacked)] if joined else kept[2 * i])
    if closing:
        earlier.wait()
        second.append([before[:, pl.ds(at, size)] for at in sides])
    for side in range(2):
        d_rows[:, pl.ds(sides[side], size)] = sum(x[side] for x in second).astype(d_rows.dtype)
    row = 0
    for out, n in zip(out_rows, sizes):
        leave(d_rows.at[pl.ds(row, n), :], out)
        row += n
    for c in leaving:
        c.wait()


def rows_call(experts, scal, groups, weights, which=(0, 1), partial=None):
    blocks = [b for group in groups for b in group]
    count = len(blocks)
    rows = blocks[0].shape[0]
    size, stacked = weights[0].shape
    total = count * rows
    sizes = [len(group) * rows for group in groups]
    joined = which == (1,)
    kind = F32 if joined else BF16
    sds = jax.ShapeDtypeStruct
    out = [sds((n, 2 * size), kind) for n in sizes]
    if joined:
        out += [sds((total, stacked + 4 * size), BF16)]
    else:
        out += [sds((total, stacked), BF16), sds((total, 2 * size), BF16)] * len(which)
    operands = [*blocks, *weights] + ([] if partial is None else [partial])
    scratch = [
        pltpu.VMEM((total, blocks[0].shape[1]), BF16),
        pltpu.VMEM((len(weights), size, stacked), BF16),
        pltpu.VMEM((len(which), total, stacked), BF16),
        pltpu.VMEM((len(which), total, 2 * size), BF16),
        pltpu.VMEM((total, 2 * size), kind),
        pltpu.SemaphoreType.DMA((len(operands),)),
        pltpu.SemaphoreType.DMA((len(groups) + 5,)),
    ]
    if partial is not None:
        scratch.append(pltpu.VMEM(partial.shape, F32))
    return pl.pallas_call(
        functools.partial(rows_kernel, experts, count, sizes, which),
        out_shape=out,
        in_specs=[smem()] + [hbm()] * len(operands),
        out_specs=[hbm()] * len(out),
        scratch_shapes=scratch,
        cost_estimate=cost(24 * total * size * stacked * len(which) * (1 if len(which) == 2 else 10), 1 << 20),
        compiler_params=params(),
    )(scal, *operands)


def half_kernel(count, groups, joined, adds, at, sides, *refs):
    refs = list(refs)
    blocks = [refs.pop(0) for _ in range(count)]
    scaled = [refs.pop(0) for _ in range(groups)]
    grads = [refs.pop(0) for _ in range(groups)]
    last = refs.pop(0) if joined else None
    more = refs.pop(0) if adds else None
    out, lefts, made, extra, done, sems, out_sems = refs
    size, stacked = done.shape[1:]
    both = stacked // 3 * 2
    rows = blocks[0].shape[0]
    steps = done.shape[0]
    started = []

    def start(source, target):
        copy = pltpu.make_async_copy(source, target, sems.at[len(started)])
        copy.start()
        started.append(copy)
        return copy

    loads = [[[], []] for _ in range(steps)]
    offsets = [pl.multiple_of(sides[i] * size, size) for i in range(steps)]
    row = 0
    for i, b in enumerate(blocks):
        loads[0][0].append(start(b.at[:, pl.ds(offsets[0], size)], lefts.at[0, 0, pl.ds(row, rows), :]))
        row += rows
    if joined:
        first = pl.multiple_of(stacked + 2 * size + offsets[0], LANES)
        loads[0][0].append(start(last.at[:, pl.ds(first, size)], lefts.at[0, 0, pl.ds(row, rows), :]))
    row = 0
    for g in grads:
        loads[0][0].append(start(g, made.at[pl.ds(row, g.shape[0]), :]))
        row += g.shape[0]
    if joined:
        loads[0][0].append(start(last.at[:, pl.ds(0, stacked)], made.at[pl.ds(row, rows), :]))
    if adds:
        loads[0][0].append(start(more.at[pl.ds(at * size, size), :], extra))
    for step in range(steps):
        if step > 0:
            for i, b in enumerate(blocks):
                loads[step][0].append(
                    start(b.at[:, pl.ds(offsets[step], size)], lefts.at[step, 0, pl.ds(i * rows, rows), :])
                )
        row = 0
        for x in scaled:
            n = x.shape[0]
            loads[step][1].append(start(x.at[:, pl.ds(offsets[step], size)], lefts.at[step, 1, pl.ds(row, n), :]))
            row += n
        if joined:
            first = pl.multiple_of(stacked + offsets[step], LANES)
            loads[step][1].append(start(last.at[:, pl.ds(first, size)], lefts.at[step, 1, pl.ds(row, rows), :]))
    leaving = []
    for step in range(steps):
        for kind in range(2):
            for c in loads[step][kind]:
                c.wait()
            first, wide = (0, both) if kind == 0 else (both, stacked - both)
            new = dot(lefts[step, kind], made[:, first : first + wide], ((0,), (0,)))
            if adds:
                new = new + extra[:, first : first + wide].astype(F32)
            done[step, :, first : first + wide] = new.astype(BF16)
            copy = pltpu.make_async_copy(
                done.at[step, :, pl.ds(first, wide)],
                out.at[pl.ds(step * size, size), pl.ds(first, wide)],
                out_sems.at[len(leaving)],
            )
            copy.start()
            leaving.append(copy)
    for c in leaving:
        c.wait()


def half_call(sides, blocks, kept, last=None, more=None, at=0, weight=0):
    grads, scaled = [k[0] for k in kept], [k[1] for k in kept]
    size = scaled[0].shape[1] // 2
    stacked = grads[0].shape[1]
    rows = blocks[0].shape[0]
    extra = [a for a in (last, more) if a is not None]
    operands = [*blocks, *scaled, *grads, *extra]
    steps = sides.shape[0]
    total = (len(blocks) + (last is not None)) * rows
    return pl.pallas_call(
        functools.partial(half_kernel, len(blocks), len(kept), last is not None, more is not None, at),
        out_shape=jax.ShapeDtypeStruct((steps * size, stacked), BF16),
        in_specs=[smem()] + [hbm()] * len(operands),
        out_specs=hbm(),
        scratch_shapes=[
            pltpu.VMEM((steps, 2, total, size), BF16),
            pltpu.VMEM((total, stacked), BF16),
            pltpu.VMEM((size, stacked), BF16),
            pltpu.VMEM((steps, size, stacked), BF16),
            pltpu.SemaphoreType.DMA((steps * (len(blocks) + len(kept) + 2) + len(kept) + 2,)),
            pltpu.SemaphoreType.DMA((2 * steps,)),
        ],
        cost_estimate=cost(8 * weight * size * stacked * 1024 + 1024, 1024),
        compiler_params=params(),
    )(sides, *operands)


Z, Y, CORES = 4, 2, 2


def pairs_of(move):
    out = []
    for z in range(Z):
        for y in range(Y):
            for c in range(CORES):
                to = move(z, y, c)
                if to is not None:
                    out.append(((z * Y + y) * CORES + c, (to[0] * Y + to[1]) * CORES + to[2]))
    return out


def along_z(table):
    return pairs_of(lambda z, y, c: (table[z], y, c) if z in table else None)


SWAP_CORE = pairs_of(lambda z, y, c: (z, y, 1 - c))
SWAP_Y = pairs_of(lambda z, y, c: (z, 1 - y, c))
OUTER = along_z({0: 1, 1: 0, 2: 3, 3: 2})
INNER = along_z({1: 2, 2: 1})
OUTWARD = along_z({1: 0, 2: 3})
INWARD = along_z({0: 1, 3: 2})
SKIP_TO_OUTER = along_z({1: 3, 2: 0})


def after(value, *others):
    return lax.optimization_barrier((value,) + others)[0]


def dense_body(tokens, d_output, combine, routes, gate_weight, up_weight, down_weight):
    experts = lax.axis_size("expert")
    part = lax.axis_index("dp")
    expert = lax.axis_index("expert")
    z = expert // (Y * CORES)
    inner = (z == 1) | (z == 2)
    scal = jnp.stack([part, expert]).astype(jnp.int32)
    mine = part[None].astype(jnp.int32)
    other = (1 - part)[None].astype(jnp.int32)

    move = lambda a, pairs: lax.ppermute(a, "expert", pairs)
    across = lambda a: lax.ppermute(a, "dp", [(0, 1), (1, 0)])

    swap = lambda a: move(a, SWAP_CORE)
    own, w_own = pack(experts, tokens, d_output, combine, routes, gate_weight[0], up_weight[0], down_weight[0])
    w_part = across(w_own)

    b1 = move(own, OUTER)
    f1 = move(own, INNER)
    y0 = move(own, SWAP_Y)
    f2 = move(b1, INNER)
    y1 = move(after(b1, y0), SWAP_Y)
    g1 = move(f1, OUTWARD)
    b2 = jnp.where(inner, f1, g1)
    y2 = move(after(b2, y1, f2), SWAP_Y)
    g2 = move(f2, OUTWARD)

    w_core = swap(after(w_own, y1, f2))
    w_both = swap(after(w_part, y1, f2))
    weights = [w_own, w_part, w_core, w_both]
    p0, p1, p2, q01, *kept_a = rows_call(experts, scal, [[own], [b1], [b2], [y0, y1]], weights)
    b3 = jnp.where(inner, f2, after(g2, p0))
    y3 = move(after(b3, y2), SWAP_Y)
    p3, q2, *kept_b = rows_call(experts, scal, [[b3], [y2]], weights)

    blocks = [own, b1, b2, y0, y1, b3, y2]
    kept = [kept_a, kept_b]
    to_core = half_call(jnp.concatenate([other, mine]), blocks, [k[2:] for k in kept])
    y3 = after(y3, q2, to_core)
    r2 = move(after(q2, y3), SWAP_Y)

    partial, joined = rows_call(experts, scal, [[y3]], weights[2:], which=(1,))
    q3, *kept_d = rows_call(experts, scal, [[y3]], weights[:2], which=(0,), partial=partial)
    last = swap(joined)
    all_blocks = blocks + [y3]
    all_kept = [k[:2] for k in kept] + [kept_d]
    got = swap(to_core)
    send = half_call(other, all_blocks, all_kept, last, got, weight=1)
    from_part = across(send)
    r3 = move(after(q3, send), SWAP_Y)
    r01 = move(after(q01, r3), SWAP_Y)
    rows = own.shape[0]
    r0, r1 = r01[:rows], r01[rows:]
    keep = half_call(after(mine, send), all_blocks, all_kept, last, got, at=1)

    add = lambda *terms: sum(t.astype(F32) for t in terms).astype(BF16)
    s1 = add(p1, r1)
    s2 = add(p2, r2)
    s2 = add(s2, move(s2, INWARD))
    s3 = add(p3, r3)
    s3 = add(s3, move(s3, INWARD))
    d_weights = keep.astype(F32) + after(from_part, s2).astype(F32)
    hidden_units = gate_weight.shape[2]
    d_gate, d_up = d_weights[:, :hidden_units], d_weights[:, hidden_units : 2 * hidden_units]
    d_down = d_weights[:, 2 * hidden_units :].T
    d_tokens = add(after(p0, d_weights), r0, move(s1, OUTER), move(s2, INNER), move(s3, SKIP_TO_OUTER))
    return (d_tokens, d_gate[None], d_up[None], d_down[None])


def route_slots(routes, experts):
    matches = (routes[:, :, None] == jnp.arange(experts, dtype=jnp.int32)[None, None, :]).astype(
        jnp.int32
    )
    per_token = jnp.sum(matches, axis=1)
    earlier = jnp.cumsum(per_token, axis=0) - per_token
    return jnp.sum(matches * earlier[:, None, :], axis=2)


def row_work(row_inputs, row_grads, gate_up, down_matrix):
    hidden_units = down_matrix.shape[0]
    preact = jnp.dot(row_inputs, gate_up, preferred_element_type=jnp.float32)
    gate_pre = preact[:, :hidden_units]
    up_pre = preact[:, hidden_units:]
    gate_sigmoid = jax.nn.sigmoid(gate_pre)
    hidden = (gate_pre * gate_sigmoid * up_pre).astype(jnp.bfloat16)
    d_hidden = jnp.dot(row_grads, down_matrix.T, preferred_element_type=jnp.float32)
    d_gate_pre = d_hidden * up_pre * gate_sigmoid * (1.0 + gate_pre * (1.0 - gate_sigmoid))
    d_up_pre = d_hidden * gate_pre * gate_sigmoid
    d_preact = jnp.concatenate([d_gate_pre, d_up_pre], axis=1).astype(jnp.bfloat16)
    d_rows = jnp.dot(d_preact, gate_up.T, preferred_element_type=jnp.float32).astype(jnp.bfloat16)
    return (d_rows, hidden, d_preact)


def routed_body(tokens, d_output, combine, routes, gate_weight, up_weight, down_weight):
    experts = lax.axis_size("expert")
    tok_count = tokens.shape[0]
    model_width = tokens.shape[1]
    top_count = routes.shape[1]
    capacity = max(2, (9 * tok_count * top_count + 8 * experts - 1) // (8 * experts))
    slot_count = experts * capacity
    slot_index = route_slots(routes, experts)
    position = (routes * capacity + slot_index).reshape(-1)
    spread_inputs = jnp.repeat(tokens, top_count, axis=0)
    scaled = (
        (combine[:, :, None] * d_output[:, None, :].astype(jnp.float32))
        .astype(jnp.bfloat16)
        .reshape(-1, model_width)
    )
    send_inputs = (
        jnp.zeros((slot_count, model_width), jnp.bfloat16)
        .at[position]
        .set(spread_inputs)
        .reshape(experts, capacity, model_width)
    )
    send_grads = (
        jnp.zeros((slot_count, model_width), jnp.bfloat16)
        .at[position]
        .set(scaled)
        .reshape(experts, capacity, model_width)
    )
    whole_gate, whole_up, whole_down = (
        lax.all_gather(gate_weight, "dp", axis=1, tiled=True),
        lax.all_gather(up_weight, "dp", axis=1, tiled=True),
        lax.all_gather(down_weight, "dp", axis=2, tiled=True),
    )
    gate_up = jnp.concatenate([whole_gate[0], whole_up[0]], axis=1)
    down_matrix = whole_down[0]
    hidden_units = down_matrix.shape[0]
    recv_inputs, recv_grads = (
        lax.all_to_all(send_inputs, "expert", split_axis=0, concat_axis=0, tiled=True),
        lax.all_to_all(send_grads, "expert", split_axis=0, concat_axis=0, tiled=True),
    )
    flat_inputs = recv_inputs.reshape(-1, model_width)
    flat_grads = recv_grads.reshape(-1, model_width)
    d_rows, hidden, d_preact = row_work(flat_inputs, flat_grads, gate_up, down_matrix)
    returned = lax.all_to_all(
        d_rows.reshape(experts, capacity, model_width),
        "expert",
        split_axis=0,
        concat_axis=0,
        tiled=True,
    )
    route_rows = returned.reshape(-1, model_width)[position].reshape(
        tok_count, top_count, model_width
    )
    d_tokens = jnp.sum(route_rows.astype(jnp.float32), axis=1).astype(jnp.bfloat16)
    gate_up_grad = jnp.dot(flat_inputs.T, d_preact, preferred_element_type=jnp.float32)
    down_grad = jnp.dot(flat_grads.T, hidden, preferred_element_type=jnp.float32)
    stacked = jnp.concatenate([gate_up_grad, down_grad], axis=1)
    summed = lax.psum_scatter(
        stacked.astype(jnp.bfloat16), "dp", scatter_dimension=0, tiled=True
    ).astype(jnp.float32)
    d_gate_weight = summed[:, :hidden_units][None]
    d_up_weight = summed[:, hidden_units : 2 * hidden_units][None]
    d_down_weight = summed[:, 2 * hidden_units :].T[None]
    return (d_tokens, d_gate_weight, d_up_weight, d_down_weight)


def solution(mesh):
    placed = (
        P(("dp", "expert"), None),
        P(("dp", "expert"), None),
        P(("dp", "expert"), None),
        P(("dp", "expert"), None),
        P("expert", "dp", None),
        P("expert", "dp", None),
        P("expert", None, "dp"),
    )
    dense = mesh.shape["expert"] == Z * Y * CORES and mesh.shape["dp"] == 2
    return jax.shard_map(
        dense_body if dense else routed_body,
        mesh=mesh,
        in_specs=placed,
        out_specs=(
            P(("dp", "expert"), None),
            P("expert", "dp", None),
            P("expert", "dp", None),
            P("expert", None, "dp"),
        ),
        check_vma=False,
    )
```

```python
import functools

import jax
import jax.numpy as jnp
from jax import lax
from jax.experimental import pallas as pl
from jax.experimental.pallas import tpu as pltpu
from jax.sharding import PartitionSpec as P

F32 = jnp.float32
BF16 = jnp.bfloat16
LANES = 128
VMEM_BYTES = 56 * 1024 * 1024


def vmem():
    return pl.BlockSpec(memory_space=pltpu.VMEM)


def smem():
    return pl.BlockSpec(memory_space=pltpu.SMEM)


def hbm():
    return pl.BlockSpec(memory_space=pl.ANY)


def params():
    return pltpu.CompilerParams(vmem_limit_bytes=VMEM_BYTES)


def cost(flops, moved):
    return pl.CostEstimate(flops=int(flops), bytes_accessed=int(moved), transcendentals=0)


def dot(a, b, dims):
    return lax.dot_general(a, b, (dims, ((), ())), preferred_element_type=F32)


def pack_kernel(experts, tokens, d_output, combine, routes, gate, up, down, out, w_out, parts, turned, sems):
    rows, width = tokens.shape
    hidden_units = gate.shape[1]
    copies = []

    def start(source, target):
        copy = pltpu.make_async_copy(source, target, sems.at[len(copies)])
        copy.start()
        copies.append(copy)

    start(tokens, out.at[:, pl.ds(0, width)])
    start(d_output, out.at[:, pl.ds(width, width)])
    start(gate, w_out.at[:, pl.ds(0, hidden_units)])
    start(up, w_out.at[:, pl.ds(hidden_units, hidden_units)])
    turned[...] = down[...].T
    start(turned, w_out.at[:, pl.ds(2 * hidden_units, hidden_units)])
    line = lax.broadcasted_iota(jnp.int32, (LANES, rows), 0)
    expert = lax.rem(line, experts)
    dense = jnp.zeros((LANES, rows), F32)
    for k in range(routes.shape[0]):
        dense = dense + jnp.where(expert == routes[k : k + 1, :], combine[k : k + 1, :], 0.0)
    high = dense.astype(BF16).astype(F32)
    rest = dense - high
    middle = rest.astype(BF16).astype(F32)
    low = rest - middle
    whole = jnp.where(
        line < experts,
        high,
        jnp.where(line < 2 * experts, middle, jnp.where(line < 3 * experts, low, 0.0)),
    )
    parts[...] = whole.T.astype(BF16)
    start(parts, out.at[:, pl.ds(2 * width, LANES)])
    for c in copies:
        c.wait()


def pack(experts, tokens, d_output, combine, routes, gate, up, down):
    rows, width = tokens.shape
    size, hidden_units = gate.shape
    return pl.pallas_call(
        functools.partial(pack_kernel, experts),
        out_shape=[
            jax.ShapeDtypeStruct((rows, 2 * width + LANES), BF16),
            jax.ShapeDtypeStruct((size, 3 * hidden_units), BF16),
        ],
        in_specs=[vmem()] * 7,
        out_specs=[hbm(), hbm()],
        scratch_shapes=[
            pltpu.VMEM((rows, LANES), BF16),
            pltpu.VMEM((size, hidden_units), BF16),
            pltpu.SemaphoreType.DMA((6,)),
        ],
        cost_estimate=cost(0, 1 << 20),
        compiler_params=params(),
    )(tokens, d_output, combine.T, routes.T, gate, up, down)


def rows_kernel(experts, count, sizes, which, halves, scal, *refs):
    refs = list(refs)
    blocks = [refs.pop(0) for _ in range(count)]
    raw = [refs.pop(0) for _ in range(2 * len(which))]
    past, kinds, wanted_sides, adds = halves
    past_blocks = [refs.pop(0) for _ in range(past)]
    past_grads = [refs.pop(0) for _ in range(kinds)]
    past_scaled = [refs.pop(0) for _ in range(kinds)]
    more = refs.pop(0) if adds else None
    out_rows = [refs.pop(0) for _ in sizes]
    kept = [refs.pop(0) for _ in range(2 * len(which))]
    products = [refs.pop(0) for _ in wanted_sides]
    block, held, grads, scaled, d_rows, in_sems, out_sems = refs[:7]
    part, expert = scal[0], scal[1]
    size, stacked = raw[0].shape
    hidden_units = stacked // 3
    both = 2 * hidden_units
    width = 2 * size
    rows = blocks[0].shape[0]
    sides = [pl.multiple_of(part * size, size), pl.multiple_of((1 - part) * size, size)]
    started, leaving = [], []

    def start(source, target):
        copy = pltpu.make_async_copy(source, target, in_sems.at[len(started)])
        copy.start()
        started.append(copy)
        return copy

    def leave(source, target):
        copy = pltpu.make_async_copy(source, target, out_sems.at[len(leaving)])
        copy.start()
        leaving.append(copy)

    arrivals = [start(b, block.at[pl.ds(i * rows, rows), :]) for i, b in enumerate(blocks)]
    weights = [start(w, held.at[i]) for i, w in enumerate(raw)]
    later = []
    if wanted_sides:
        lefts, made, extra, done = refs[7:]
        row = 0
        for g, x in zip(past_grads, past_scaled):
            n = g.shape[0]
            later.append(start(g, made.at[pl.ds(row, n), :]))
            for k, side in enumerate(wanted_sides):
                later.append(start(x.at[:, pl.ds(sides[side], size)], lefts.at[k, 1, pl.ds(row, n), :]))
            row += n
        for i, b in enumerate(past_blocks):
            for k, side in enumerate(wanted_sides):
                later.append(start(b.at[:, pl.ds(sides[side], size)], lefts.at[k, 0, pl.ds(i * rows, rows), :]))
        if adds:
            later.append(start(more, extra))
    for c in arrivals:
        c.wait()
    parts = block[:, 2 * width :].astype(F32)
    lane = lax.broadcasted_iota(jnp.int32, parts.shape, 1)
    first = []
    for i, one in enumerate(which):
        for c in weights[2 * i : 2 * i + 2]:
            c.wait()
        wanted = expert if one == 0 else expert + 1 - 2 * lax.rem(expert, 2)
        mine = (lax.rem(lane, experts) == wanted) & (lane < 3 * experts)
        weight = jnp.sum(jnp.where(mine, parts, 0.0), axis=1, keepdims=True)
        preact = None
        d_hidden = None
        for side in range(2):
            at = sides[side]
            grad = block[:, pl.ds(pl.multiple_of(width + at, size), size)]
            scaled_half = (weight * grad.astype(F32)).astype(BF16)
            scaled[i, :, pl.ds(at, size)] = scaled_half
            p = dot(block[:, pl.ds(at, size)], held[2 * i + side, :, :both], ((1,), (0,)))
            h = dot(scaled_half, held[2 * i + side, :, both:], ((1,), (0,)))
            preact = p if side == 0 else preact + p
            d_hidden = h if side == 0 else d_hidden + h
        first.append((preact, d_hidden))
    for i in range(len(which)):
        leave(scaled.at[i], kept[2 * i + 1])
    second = []
    for i in range(len(which)):
        preact, d_hidden = first[i]
        gate_pre = preact[:, :hidden_units]
        up_pre = preact[:, hidden_units:]
        sig = jax.nn.sigmoid(gate_pre)
        silu = gate_pre * sig
        d_gate = (d_hidden * up_pre * sig * (1.0 + gate_pre * (1.0 - sig))).astype(BF16)
        d_up = (d_hidden * silu).astype(BF16)
        grads[i, :, :hidden_units] = d_gate
        grads[i, :, hidden_units:both] = d_up
        grads[i, :, both:] = (silu * up_pre).astype(BF16)
        d_preact = jnp.concatenate([d_gate, d_up], axis=1)
        second.append([dot(d_preact, held[2 * i + side, :, :both], ((1,), (1,))) for side in range(2)])
    for i in range(len(which)):
        leave(grads.at[i], kept[2 * i])
    for side in range(2):
        d_rows[:, pl.ds(sides[side], size)] = sum(x[side] for x in second).astype(BF16)
    row = 0
    for out, n in zip(out_rows, sizes):
        leave(d_rows.at[pl.ds(row, n), :], out)
        row += n
    for c in later:
        c.wait()
    end = len(which) - 1
    for k, side in enumerate(wanted_sides):
        at = sides[side]
        for kind, span in enumerate((slice(0, both), slice(both, stacked))):
            now = block[:, pl.ds(at, size)] if kind == 0 else scaled[end, :, pl.ds(at, size)]
            new = dot(lefts[k, kind], made[:, span], ((0,), (0,))) + dot(now, grads[end, :, span], ((0,), (0,)))
            if adds:
                new = new + extra[:, span].astype(F32)
            done[k, :, span] = new.astype(BF16)
        leave(done.at[k], products[k])
    for c in leaving:
        c.wait()


def rows_call(experts, scal, groups, weights, which=(0, 1), past=((), ()), sides=(), more=None):
    blocks = [b for group in groups for b in group]
    count = len(blocks)
    rows = blocks[0].shape[0]
    size, stacked = weights[0].shape
    total = count * rows
    sizes = [len(group) * rows for group in groups]
    sds = jax.ShapeDtypeStruct
    out = [sds((n, 2 * size), BF16) for n in sizes]
    out += [sds((total, stacked), BF16), sds((total, 2 * size), BF16)] * len(which)
    out += [sds((size, stacked), BF16)] * len(sides)
    past_blocks, past_kept = past
    operands = [*blocks, *weights, *past_blocks, *(k[0] for k in past_kept), *(k[1] for k in past_kept)]
    if more is not None:
        operands.append(more)
    scratch = [
        pltpu.VMEM((total, blocks[0].shape[1]), BF16),
        pltpu.VMEM((len(weights), size, stacked), BF16),
        pltpu.VMEM((len(which), total, stacked), BF16),
        pltpu.VMEM((len(which), total, 2 * size), BF16),
        pltpu.VMEM((total, 2 * size), BF16),
        pltpu.SemaphoreType.DMA((len(operands) + len(sides) * (len(past_blocks) + len(past_kept)),)),
        pltpu.SemaphoreType.DMA((len(out),)),
    ]
    if sides:
        earlier = len(past_blocks) * rows
        scratch += [
            pltpu.VMEM((len(sides), 2, earlier, size), BF16),
            pltpu.VMEM((earlier, stacked), BF16),
            pltpu.VMEM((size, stacked), BF16),
            pltpu.VMEM((len(sides), size, stacked), BF16),
        ]
    halves = (len(past_blocks), len(past_kept), sides, more is not None)
    return pl.pallas_call(
        functools.partial(rows_kernel, experts, count, sizes, which, halves),
        out_shape=out,
        in_specs=[smem()] + [hbm()] * len(operands),
        out_specs=[hbm()] * len(out),
        scratch_shapes=scratch,
        cost_estimate=cost(24 * total * size * stacked * len(which) * (1 if len(which) == 2 else 10), 1 << 20),
        compiler_params=params(),
    )(scal, *operands)


def half_kernel(count, groups, sides, *refs):
    refs = list(refs)
    blocks = [refs.pop(0) for _ in range(count)]
    scaled = [refs.pop(0) for _ in range(groups)]
    grads = [refs.pop(0) for _ in range(groups)]
    more, out, lefts, made, extra, done, sems, out_sems = refs
    size, stacked = done.shape
    both = stacked // 3 * 2
    rows = blocks[0].shape[0]
    at = pl.multiple_of(sides[0] * size, size)
    started = []

    def start(source, target):
        copy = pltpu.make_async_copy(source, target, sems.at[len(started)])
        copy.start()
        started.append(copy)

    for i, b in enumerate(blocks):
        start(b.at[:, pl.ds(at, size)], lefts.at[0, pl.ds(i * rows, rows), :])
    row = 0
    for g in grads:
        start(g, made.at[pl.ds(row, g.shape[0]), :])
        row += g.shape[0]
    start(more, extra)
    early = len(started)
    row = 0
    for x in scaled:
        start(x.at[:, pl.ds(at, size)], lefts.at[1, pl.ds(row, x.shape[0]), :])
        row += x.shape[0]
    leaving = []
    for kind, (first, wide) in enumerate(((0, both), (both, stacked - both))):
        for c in started[:early] if kind == 0 else started[early:]:
            c.wait()
        new = dot(lefts[kind], made[:, first : first + wide], ((0,), (0,)))
        done[:, first : first + wide] = (new + extra[:, first : first + wide].astype(F32)).astype(BF16)
        copy = pltpu.make_async_copy(
            done.at[:, pl.ds(first, wide)], out.at[:, pl.ds(first, wide)], out_sems.at[len(leaving)]
        )
        copy.start()
        leaving.append(copy)
    for c in leaving:
        c.wait()


def half_call(sides, blocks, kept, more):
    grads, scaled = [k[0] for k in kept], [k[1] for k in kept]
    size = scaled[0].shape[1] // 2
    stacked = grads[0].shape[1]
    total = len(blocks) * blocks[0].shape[0]
    operands = [*blocks, *scaled, *grads, more]
    return pl.pallas_call(
        functools.partial(half_kernel, len(blocks), len(kept)),
        out_shape=jax.ShapeDtypeStruct((size, stacked), BF16),
        in_specs=[smem()] + [hbm()] * len(operands),
        out_specs=hbm(),
        scratch_shapes=[
            pltpu.VMEM((2, total, size), BF16),
            pltpu.VMEM((total, stacked), BF16),
            pltpu.VMEM((size, stacked), BF16),
            pltpu.VMEM((size, stacked), BF16),
            pltpu.SemaphoreType.DMA((len(operands),)),
            pltpu.SemaphoreType.DMA((2,)),
        ],
        cost_estimate=cost(1024, 1024),
        compiler_params=params(),
    )(sides, *operands)


Z, Y, CORES = 4, 2, 2


def pairs_of(move):
    out = []
    for z in range(Z):
        for y in range(Y):
            for c in range(CORES):
                to = move(z, y, c)
                if to is not None:
                    out.append(((z * Y + y) * CORES + c, (to[0] * Y + to[1]) * CORES + to[2]))
    return out


def along_z(table):
    return pairs_of(lambda z, y, c: (table[z], y, c) if z in table else None)


SWAP_CORE = pairs_of(lambda z, y, c: (z, y, 1 - c))
SWAP_Y = pairs_of(lambda z, y, c: (z, 1 - y, c))
OUTER = along_z({0: 1, 1: 0, 2: 3, 3: 2})
INNER = along_z({1: 2, 2: 1})
OUTWARD = along_z({1: 0, 2: 3})
INWARD = along_z({0: 1, 3: 2})
SKIP_TO_OUTER = along_z({1: 3, 2: 0})


def after(value, *others):
    return lax.optimization_barrier((value,) + others)[0]


def dense_body(tokens, d_output, combine, routes, gate_weight, up_weight, down_weight):
    experts = lax.axis_size("expert")
    part = lax.axis_index("dp")
    expert = lax.axis_index("expert")
    z = expert // (Y * CORES)
    inner = (z == 1) | (z == 2)
    scal = jnp.stack([part, expert]).astype(jnp.int32)
    mine = part[None].astype(jnp.int32)
    other = (1 - part)[None].astype(jnp.int32)

    move = lambda a, pairs: lax.ppermute(a, "expert", pairs)
    across = lambda a: lax.ppermute(a, "dp", [(0, 1), (1, 0)])

    swap = lambda a: move(a, SWAP_CORE)
    own, w_own = pack(experts, tokens, d_output, combine, routes, gate_weight[0], up_weight[0], down_weight[0])
    w_part = across(w_own)

    b1 = move(own, OUTER)
    f1 = move(own, INNER)
    y0 = move(own, SWAP_Y)
    f2 = move(b1, INNER)
    y1 = move(after(b1, y0), SWAP_Y)
    g1 = move(f1, OUTWARD)
    b2 = jnp.where(inner, f1, g1)
    y2 = move(after(b2, y1, f2), SWAP_Y)
    g2 = move(f2, OUTWARD)

    w_core = swap(after(w_own, y1, f2))
    w_both = swap(after(w_part, y1, f2))
    weights = [w_own, w_part, w_core, w_both]
    p0, p1, p2, q0, q1, *kept_a = rows_call(experts, scal, [[own], [b1], [b2], [y0], [y1]], weights)
    b3 = jnp.where(inner, f2, after(g2, p0))
    y3 = move(after(b3, y2), SWAP_Y)
    early = [own, b1, b2, y0, y1]

    p3, q2, *kept_b, to_other, to_mine = rows_call(
        experts, scal, [[b3], [y2]], weights, past=(early, [kept_a[2:]]), sides=(1, 0)
    )
    y3 = after(y3, q2)
    cy3 = swap(y3)
    got_other, got_mine = swap(after(to_other, y3)), swap(after(to_mine, y3, cy3))
    r2 = move(after(q2, y3), SWAP_Y)
    r1 = move(after(q1, y3), SWAP_Y)

    blocks = early + [b3, y2]
    kept = [kept_a[:2], kept_b[:2]]
    last, pair, *kept_c, send = rows_call(
        experts, scal, [[y3], [cy3]], weights[:2], which=(0,), past=(blocks, kept), sides=(1,), more=got_other
    )
    from_part = across(send)
    add = lambda *terms: sum(t.astype(F32) for t in terms).astype(BF16)
    r3 = move(add(last, swap(after(pair, r2, r1, got_mine))), SWAP_Y)
    r0 = move(after(q0, r3), SWAP_Y)
    keep = half_call(after(mine, send), blocks + [y3, cy3], kept + [kept_c], more=got_mine)

    s1 = add(p1, r1)
    s2 = add(p2, r2)
    s2 = add(s2, move(s2, INWARD))
    s3 = add(p3, r3)
    s3 = add(s3, move(s3, INWARD))
    d_weights = keep.astype(F32) + after(from_part, s3).astype(F32)
    hidden_units = gate_weight.shape[2]
    d_gate, d_up = d_weights[:, :hidden_units], d_weights[:, hidden_units : 2 * hidden_units]
    d_down = d_weights[:, 2 * hidden_units :].T
    d_tokens = add(after(p0, d_weights), r0, move(s1, OUTER), move(s2, INNER), move(s3, SKIP_TO_OUTER))
    return (d_tokens, d_gate[None], d_up[None], d_down[None])


def route_slots(routes, experts):
    matches = (routes[:, :, None] == jnp.arange(experts, dtype=jnp.int32)[None, None, :]).astype(
        jnp.int32
    )
    per_token = jnp.sum(matches, axis=1)
    earlier = jnp.cumsum(per_token, axis=0) - per_token
    return jnp.sum(matches * earlier[:, None, :], axis=2)


def row_work(row_inputs, row_grads, gate_up, down_matrix):
    hidden_units = down_matrix.shape[0]
    preact = jnp.dot(row_inputs, gate_up, preferred_element_type=jnp.float32)
    gate_pre = preact[:, :hidden_units]
    up_pre = preact[:, hidden_units:]
    gate_sigmoid = jax.nn.sigmoid(gate_pre)
    hidden = (gate_pre * gate_sigmoid * up_pre).astype(jnp.bfloat16)
    d_hidden = jnp.dot(row_grads, down_matrix.T, preferred_element_type=jnp.float32)
    d_gate_pre = d_hidden * up_pre * gate_sigmoid * (1.0 + gate_pre * (1.0 - gate_sigmoid))
    d_up_pre = d_hidden * gate_pre * gate_sigmoid
    d_preact = jnp.concatenate([d_gate_pre, d_up_pre], axis=1).astype(jnp.bfloat16)
    d_rows = jnp.dot(d_preact, gate_up.T, preferred_element_type=jnp.float32).astype(jnp.bfloat16)
    return (d_rows, hidden, d_preact)


def routed_body(tokens, d_output, combine, routes, gate_weight, up_weight, down_weight):
    experts = lax.axis_size("expert")
    tok_count = tokens.shape[0]
    model_width = tokens.shape[1]
    top_count = routes.shape[1]
    capacity = max(2, (9 * tok_count * top_count + 8 * experts - 1) // (8 * experts))
    slot_count = experts * capacity
    slot_index = route_slots(routes, experts)
    position = (routes * capacity + slot_index).reshape(-1)
    spread_inputs = jnp.repeat(tokens, top_count, axis=0)
    scaled = (
        (combine[:, :, None] * d_output[:, None, :].astype(jnp.float32))
        .astype(jnp.bfloat16)
        .reshape(-1, model_width)
    )
    send_inputs = (
        jnp.zeros((slot_count, model_width), jnp.bfloat16)
        .at[position]
        .set(spread_inputs)
        .reshape(experts, capacity, model_width)
    )
    send_grads = (
        jnp.zeros((slot_count, model_width), jnp.bfloat16)
        .at[position]
        .set(scaled)
        .reshape(experts, capacity, model_width)
    )
    whole_gate, whole_up, whole_down = (
        lax.all_gather(gate_weight, "dp", axis=1, tiled=True),
        lax.all_gather(up_weight, "dp", axis=1, tiled=True),
        lax.all_gather(down_weight, "dp", axis=2, tiled=True),
    )
    gate_up = jnp.concatenate([whole_gate[0], whole_up[0]], axis=1)
    down_matrix = whole_down[0]
    hidden_units = down_matrix.shape[0]
    recv_inputs, recv_grads = (
        lax.all_to_all(send_inputs, "expert", split_axis=0, concat_axis=0, tiled=True),
        lax.all_to_all(send_grads, "expert", split_axis=0, concat_axis=0, tiled=True),
    )
    flat_inputs = recv_inputs.reshape(-1, model_width)
    flat_grads = recv_grads.reshape(-1, model_width)
    d_rows, hidden, d_preact = row_work(flat_inputs, flat_grads, gate_up, down_matrix)
    returned = lax.all_to_all(
        d_rows.reshape(experts, capacity, model_width),
        "expert",
        split_axis=0,
        concat_axis=0,
        tiled=True,
    )
    route_rows = returned.reshape(-1, model_width)[position].reshape(
        tok_count, top_count, model_width
    )
    d_tokens = jnp.sum(route_rows.astype(jnp.float32), axis=1).astype(jnp.bfloat16)
    gate_up_grad = jnp.dot(flat_inputs.T, d_preact, preferred_element_type=jnp.float32)
    down_grad = jnp.dot(flat_grads.T, hidden, preferred_element_type=jnp.float32)
    stacked = jnp.concatenate([gate_up_grad, down_grad], axis=1)
    summed = lax.psum_scatter(
        stacked.astype(jnp.bfloat16), "dp", scatter_dimension=0, tiled=True
    ).astype(jnp.float32)
    d_gate_weight = summed[:, :hidden_units][None]
    d_up_weight = summed[:, hidden_units : 2 * hidden_units][None]
    d_down_weight = summed[:, 2 * hidden_units :].T[None]
    return (d_tokens, d_gate_weight, d_up_weight, d_down_weight)


def solution(mesh):
    placed = (
        P(("dp", "expert"), None),
        P(("dp", "expert"), None),
        P(("dp", "expert"), None),
        P(("dp", "expert"), None),
        P("expert", "dp", None),
        P("expert", "dp", None),
        P("expert", None, "dp"),
    )
    dense = mesh.shape["expert"] == Z * Y * CORES and mesh.shape["dp"] == 2
    return jax.shard_map(
        dense_body if dense else routed_body,
        mesh=mesh,
        in_specs=placed,
        out_specs=(
            P(("dp", "expert"), None),
            P("expert", "dp", None),
            P("expert", "dp", None),
            P("expert", None, "dp"),
        ),
        check_vma=False,
    )
```

```python
import functools

import jax
import jax.numpy as jnp
from jax import lax
from jax.experimental import pallas as pl
from jax.experimental.pallas import tpu as pltpu
from jax.sharding import PartitionSpec as P

F32 = jnp.float32
BF16 = jnp.bfloat16
LANES = 128
VMEM_BYTES = 56 * 1024 * 1024


def vmem():
    return pl.BlockSpec(memory_space=pltpu.VMEM)


def smem():
    return pl.BlockSpec(memory_space=pltpu.SMEM)


def hbm():
    return pl.BlockSpec(memory_space=pl.ANY)


def params():
    return pltpu.CompilerParams(vmem_limit_bytes=VMEM_BYTES)


def cost(flops, moved):
    return pl.CostEstimate(flops=int(flops), bytes_accessed=int(moved), transcendentals=0)


def dot(a, b, dims):
    return lax.dot_general(a, b, (dims, ((), ())), preferred_element_type=F32)


def pack_kernel(experts, tokens, d_output, combine, routes, gate, up, down, out, w_out, parts, turned, sems):
    rows, width = tokens.shape
    hidden_units = gate.shape[1]
    copies = []

    def start(source, target):
        copy = pltpu.make_async_copy(source, target, sems.at[len(copies)])
        copy.start()
        copies.append(copy)

    start(tokens, out.at[:, pl.ds(0, width)])
    start(d_output, out.at[:, pl.ds(width, width)])
    start(gate, w_out.at[:, pl.ds(0, hidden_units)])
    start(up, w_out.at[:, pl.ds(hidden_units, hidden_units)])
    turned[...] = down[...].T
    start(turned, w_out.at[:, pl.ds(2 * hidden_units, hidden_units)])
    line = lax.broadcasted_iota(jnp.int32, (LANES, rows), 0)
    expert = lax.rem(line, experts)
    dense = jnp.zeros((LANES, rows), F32)
    for k in range(routes.shape[0]):
        dense = dense + jnp.where(expert == routes[k : k + 1, :], combine[k : k + 1, :], 0.0)
    high = dense.astype(BF16).astype(F32)
    rest = dense - high
    middle = rest.astype(BF16).astype(F32)
    low = rest - middle
    whole = jnp.where(
        line < experts,
        high,
        jnp.where(line < 2 * experts, middle, jnp.where(line < 3 * experts, low, 0.0)),
    )
    parts[...] = whole.T.astype(BF16)
    start(parts, out.at[:, pl.ds(2 * width, LANES)])
    for c in copies:
        c.wait()


def pack(experts, tokens, d_output, combine, routes, gate, up, down):
    rows, width = tokens.shape
    size, hidden_units = gate.shape
    return pl.pallas_call(
        functools.partial(pack_kernel, experts),
        out_shape=[
            jax.ShapeDtypeStruct((rows, 2 * width + LANES), BF16),
            jax.ShapeDtypeStruct((size, 3 * hidden_units), BF16),
        ],
        in_specs=[vmem()] * 7,
        out_specs=[hbm(), hbm()],
        scratch_shapes=[
            pltpu.VMEM((rows, LANES), BF16),
            pltpu.VMEM((size, hidden_units), BF16),
            pltpu.SemaphoreType.DMA((6,)),
        ],
        cost_estimate=cost(0, 1 << 20),
        compiler_params=params(),
    )(tokens, d_output, combine.T, routes.T, gate, up, down)


def rows_kernel(experts, count, sizes, which, halves, scal, *refs):
    refs = list(refs)
    blocks = [refs.pop(0) for _ in range(count)]
    raw = [refs.pop(0) for _ in range(2 * len(which))]
    past, kinds, wanted_sides, adds = halves
    past_blocks = [refs.pop(0) for _ in range(past)]
    past_grads = [refs.pop(0) for _ in range(kinds)]
    past_scaled = [refs.pop(0) for _ in range(kinds)]
    more = refs.pop(0) if adds else None
    out_rows = [refs.pop(0) for _ in sizes]
    kept = [refs.pop(0) for _ in range(2 * len(which))]
    products = [refs.pop(0) for _ in wanted_sides]
    block, held, grads, scaled, d_rows, in_sems, out_sems = refs[:7]
    part, expert = scal[0], scal[1]
    size, stacked = raw[0].shape
    hidden_units = stacked // 3
    both = 2 * hidden_units
    width = 2 * size
    rows = blocks[0].shape[0]
    sides = [pl.multiple_of(part * size, size), pl.multiple_of((1 - part) * size, size)]
    started, leaving = [], []

    def start(source, target):
        copy = pltpu.make_async_copy(source, target, in_sems.at[len(started)])
        copy.start()
        started.append(copy)
        return copy

    def leave(source, target):
        copy = pltpu.make_async_copy(source, target, out_sems.at[len(leaving)])
        copy.start()
        leaving.append(copy)

    arrivals = [start(b, block.at[pl.ds(i * rows, rows), :]) for i, b in enumerate(blocks)]
    weights = [start(w, held.at[i]) for i, w in enumerate(raw)]
    later = []
    if wanted_sides:
        lefts, made, extra, done = refs[7:]
        row = 0
        for g, x in zip(past_grads, past_scaled):
            n = g.shape[0]
            later.append(start(g, made.at[pl.ds(row, n), :]))
            for k, side in enumerate(wanted_sides):
                later.append(start(x.at[:, pl.ds(sides[side], size)], lefts.at[k, 1, pl.ds(row, n), :]))
            row += n
        for i, b in enumerate(past_blocks):
            for k, side in enumerate(wanted_sides):
                later.append(start(b.at[:, pl.ds(sides[side], size)], lefts.at[k, 0, pl.ds(i * rows, rows), :]))
        if adds:
            later.append(start(more, extra))
    for c in arrivals:
        c.wait()
    parts = block[:, 2 * width :].astype(F32)
    lane = lax.broadcasted_iota(jnp.int32, parts.shape, 1)
    first = []
    for i, one in enumerate(which):
        for c in weights[2 * i : 2 * i + 2]:
            c.wait()
        wanted = expert if one == 0 else expert + 1 - 2 * lax.rem(expert, 2)
        mine = (lax.rem(lane, experts) == wanted) & (lane < 3 * experts)
        weight = jnp.sum(jnp.where(mine, parts, 0.0), axis=1, keepdims=True)
        preact = None
        d_hidden = None
        for side in range(2):
            at = sides[side]
            grad = block[:, pl.ds(pl.multiple_of(width + at, size), size)]
            scaled_half = (weight * grad.astype(F32)).astype(BF16)
            scaled[i, :, pl.ds(at, size)] = scaled_half
            p = dot(block[:, pl.ds(at, size)], held[2 * i + side, :, :both], ((1,), (0,)))
            h = dot(scaled_half, held[2 * i + side, :, both:], ((1,), (0,)))
            preact = p if side == 0 else preact + p
            d_hidden = h if side == 0 else d_hidden + h
        first.append((preact, d_hidden))
    for i in range(len(which)):
        leave(scaled.at[i], kept[2 * i + 1])
    second = []
    for i in range(len(which)):
        preact, d_hidden = first[i]
        gate_pre = preact[:, :hidden_units]
        up_pre = preact[:, hidden_units:]
        sig = jax.nn.sigmoid(gate_pre)
        silu = gate_pre * sig
        d_gate = (d_hidden * up_pre * sig * (1.0 + gate_pre * (1.0 - sig))).astype(BF16)
        d_up = (d_hidden * silu).astype(BF16)
        grads[i, :, :hidden_units] = d_gate
        grads[i, :, hidden_units:both] = d_up
        grads[i, :, both:] = (silu * up_pre).astype(BF16)
        d_preact = jnp.concatenate([d_gate, d_up], axis=1)
        second.append([dot(d_preact, held[2 * i + side, :, :both], ((1,), (1,))) for side in range(2)])
    for i in range(len(which)):
        leave(grads.at[i], kept[2 * i])
    for side in range(2):
        d_rows[:, pl.ds(sides[side], size)] = sum(x[side] for x in second).astype(BF16)
    row = 0
    for out, n in zip(out_rows, sizes):
        leave(d_rows.at[pl.ds(row, n), :], out)
        row += n
    for c in later:
        c.wait()
    end = len(which) - 1
    for k, side in enumerate(wanted_sides):
        at = sides[side]
        for kind, span in enumerate((slice(0, both), slice(both, stacked))):
            now = block[:, pl.ds(at, size)] if kind == 0 else scaled[end, :, pl.ds(at, size)]
            new = dot(lefts[k, kind], made[:, span], ((0,), (0,))) + dot(now, grads[end, :, span], ((0,), (0,)))
            if adds:
                new = new + extra[:, span].astype(F32)
            done[k, :, span] = new.astype(BF16)
        leave(done.at[k], products[k])
    for c in leaving:
        c.wait()


def rows_call(experts, scal, groups, weights, which=(0, 1), past=((), ()), sides=(), more=None):
    blocks = [b for group in groups for b in group]
    count = len(blocks)
    rows = blocks[0].shape[0]
    size, stacked = weights[0].shape
    total = count * rows
    sizes = [len(group) * rows for group in groups]
    sds = jax.ShapeDtypeStruct
    out = [sds((n, 2 * size), BF16) for n in sizes]
    out += [sds((total, stacked), BF16), sds((total, 2 * size), BF16)] * len(which)
    out += [sds((size, stacked), BF16)] * len(sides)
    past_blocks, past_kept = past
    operands = [*blocks, *weights, *past_blocks, *(k[0] for k in past_kept), *(k[1] for k in past_kept)]
    if more is not None:
        operands.append(more)
    scratch = [
        pltpu.VMEM((total, blocks[0].shape[1]), BF16),
        pltpu.VMEM((len(weights), size, stacked), BF16),
        pltpu.VMEM((len(which), total, stacked), BF16),
        pltpu.VMEM((len(which), total, 2 * size), BF16),
        pltpu.VMEM((total, 2 * size), BF16),
        pltpu.SemaphoreType.DMA((len(operands) + len(sides) * (len(past_blocks) + len(past_kept)),)),
        pltpu.SemaphoreType.DMA((len(out),)),
    ]
    if sides:
        earlier = len(past_blocks) * rows
        scratch += [
            pltpu.VMEM((len(sides), 2, earlier, size), BF16),
            pltpu.VMEM((earlier, stacked), BF16),
            pltpu.VMEM((size, stacked), BF16),
            pltpu.VMEM((len(sides), size, stacked), BF16),
        ]
    halves = (len(past_blocks), len(past_kept), sides, more is not None)
    return pl.pallas_call(
        functools.partial(rows_kernel, experts, count, sizes, which, halves),
        out_shape=out,
        in_specs=[smem()] + [hbm()] * len(operands),
        out_specs=[hbm()] * len(out),
        scratch_shapes=scratch,
        cost_estimate=cost(24 * total * size * stacked * len(which) * (1 if len(which) == 2 else 10), 1 << 20),
        compiler_params=params(),
    )(scal, *operands)


def half_kernel(count, groups, sides, *refs):
    refs = list(refs)
    blocks = [refs.pop(0) for _ in range(count)]
    scaled = [refs.pop(0) for _ in range(groups)]
    grads = [refs.pop(0) for _ in range(groups)]
    more, out, lefts, made, extra, done, sems, out_sems = refs
    size, stacked = done.shape
    both = stacked // 3 * 2
    rows = blocks[0].shape[0]
    at = pl.multiple_of(sides[0] * size, size)
    started = []

    def start(source, target):
        copy = pltpu.make_async_copy(source, target, sems.at[len(started)])
        copy.start()
        started.append(copy)

    for i, b in enumerate(blocks):
        start(b.at[:, pl.ds(at, size)], lefts.at[0, pl.ds(i * rows, rows), :])
    row = 0
    for g in grads:
        start(g, made.at[pl.ds(row, g.shape[0]), :])
        row += g.shape[0]
    start(more, extra)
    early = len(started)
    row = 0
    for x in scaled:
        start(x.at[:, pl.ds(at, size)], lefts.at[1, pl.ds(row, x.shape[0]), :])
        row += x.shape[0]
    leaving = []
    for kind, (first, wide) in enumerate(((0, both), (both, stacked - both))):
        for c in started[:early] if kind == 0 else started[early:]:
            c.wait()
        new = dot(lefts[kind], made[:, first : first + wide], ((0,), (0,)))
        done[:, first : first + wide] = (new + extra[:, first : first + wide].astype(F32)).astype(BF16)
        copy = pltpu.make_async_copy(
            done.at[:, pl.ds(first, wide)], out.at[:, pl.ds(first, wide)], out_sems.at[len(leaving)]
        )
        copy.start()
        leaving.append(copy)
    for c in leaving:
        c.wait()


def half_call(sides, blocks, kept, more):
    grads, scaled = [k[0] for k in kept], [k[1] for k in kept]
    size = scaled[0].shape[1] // 2
    stacked = grads[0].shape[1]
    total = len(blocks) * blocks[0].shape[0]
    operands = [*blocks, *scaled, *grads, more]
    return pl.pallas_call(
        functools.partial(half_kernel, len(blocks), len(kept)),
        out_shape=jax.ShapeDtypeStruct((size, stacked), BF16),
        in_specs=[smem()] + [hbm()] * len(operands),
        out_specs=hbm(),
        scratch_shapes=[
            pltpu.VMEM((2, total, size), BF16),
            pltpu.VMEM((total, stacked), BF16),
            pltpu.VMEM((size, stacked), BF16),
            pltpu.VMEM((size, stacked), BF16),
            pltpu.SemaphoreType.DMA((len(operands),)),
            pltpu.SemaphoreType.DMA((2,)),
        ],
        cost_estimate=cost(1024, 1024),
        compiler_params=params(),
    )(sides, *operands)


Z, Y, CORES = 4, 2, 2


def pairs_of(move):
    out = []
    for z in range(Z):
        for y in range(Y):
            for c in range(CORES):
                to = move(z, y, c)
                if to is not None:
                    out.append(((z * Y + y) * CORES + c, (to[0] * Y + to[1]) * CORES + to[2]))
    return out


def along_z(table):
    return pairs_of(lambda z, y, c: (table[z], y, c) if z in table else None)


SWAP_CORE = pairs_of(lambda z, y, c: (z, y, 1 - c))
SWAP_Y = pairs_of(lambda z, y, c: (z, 1 - y, c))
OUTER = along_z({0: 1, 1: 0, 2: 3, 3: 2})
INNER = along_z({1: 2, 2: 1})
OUTWARD = along_z({1: 0, 2: 3})
INWARD = along_z({0: 1, 3: 2})
SKIP_TO_OUTER = along_z({1: 3, 2: 0})


def after(value, *others):
    return lax.optimization_barrier((value,) + others)[0]


def dense_body(tokens, d_output, combine, routes, gate_weight, up_weight, down_weight):
    experts = lax.axis_size("expert")
    part = lax.axis_index("dp")
    expert = lax.axis_index("expert")
    z = expert // (Y * CORES)
    inner = (z == 1) | (z == 2)
    scal = jnp.stack([part, expert]).astype(jnp.int32)
    mine = part[None].astype(jnp.int32)
    other = (1 - part)[None].astype(jnp.int32)

    move = lambda a, pairs: lax.ppermute(a, "expert", pairs)
    across = lambda a: lax.ppermute(a, "dp", [(0, 1), (1, 0)])

    swap = lambda a: move(a, SWAP_CORE)
    own, w_own = pack(experts, tokens, d_output, combine, routes, gate_weight[0], up_weight[0], down_weight[0])
    w_part = across(w_own)

    b1 = move(own, OUTER)
    f1 = move(own, INNER)
    y0 = move(own, SWAP_Y)
    f2 = move(b1, INNER)
    y1 = move(after(b1, y0), SWAP_Y)
    g1 = move(f1, OUTWARD)
    b2 = jnp.where(inner, f1, g1)
    y2 = move(after(b2, y1, f2), SWAP_Y)
    g2 = move(f2, OUTWARD)

    w_core = swap(after(w_own, y1, f2))
    w_both = swap(after(w_part, y1, f2))
    weights = [w_own, w_part, w_core, w_both]
    p0, p1, p2, q0, q1, *kept_a = rows_call(experts, scal, [[own], [b1], [b2], [y0], [y1]], weights)
    b3 = jnp.where(inner, f2, after(g2, p0))
    y3 = move(after(b3, y2), SWAP_Y)
    early = [own, b1, b2, y0, y1]

    p3, q2, *kept_b, to_other, to_mine = rows_call(
        experts, scal, [[b3], [y2]], weights, past=(early, [kept_a[2:]]), sides=(1, 0)
    )
    y3 = after(y3, q2)
    cy3 = swap(y3)
    got_other, got_mine = swap(after(to_other, y3)), swap(after(to_mine, y3, cy3))
    r2 = move(after(q2, y3), SWAP_Y)
    r1 = move(after(q1, y3), SWAP_Y)

    blocks = early + [b3, y2]
    kept = [kept_a[:2], kept_b[:2]]
    last, pair, *kept_c, send = rows_call(
        experts, scal, [[y3], [cy3]], weights[:2], which=(0,), past=(blocks, kept), sides=(1,), more=got_other
    )
    from_part = across(send)
    add = lambda *terms: sum(t.astype(F32) for t in terms).astype(BF16)
    r3 = move(add(last, swap(after(pair, r2, r1, got_mine))), SWAP_Y)
    s1 = add(p1, r1)
    s2 = add(p2, r2)
    s2 = add(s2, move(s2, INWARD))
    s3 = add(p3, r3)
    s3 = add(s3, move(s3, INWARD))
    keep = half_call(after(mine, send, s3), blocks + [y3, cy3], kept + [kept_c], more=got_mine)

    r0 = move(after(q0, r3, keep), SWAP_Y)
    from_part = after(from_part, s3)
    hidden_units = gate_weight.shape[2]
    whole = lambda a: keep[:, a : a + hidden_units].astype(F32) + from_part[:, a : a + hidden_units].astype(F32)
    d_gate, d_up, d_down = whole(0), whole(hidden_units), whole(2 * hidden_units).T
    d_tokens = add(after(p0, from_part), r0, move(s1, OUTER), move(s2, INNER), move(s3, SKIP_TO_OUTER))
    return (d_tokens, d_gate[None], d_up[None], d_down[None])


def route_slots(routes, experts):
    matches = (routes[:, :, None] == jnp.arange(experts, dtype=jnp.int32)[None, None, :]).astype(
        jnp.int32
    )
    per_token = jnp.sum(matches, axis=1)
    earlier = jnp.cumsum(per_token, axis=0) - per_token
    return jnp.sum(matches * earlier[:, None, :], axis=2)


def row_work(row_inputs, row_grads, gate_up, down_matrix):
    hidden_units = down_matrix.shape[0]
    preact = jnp.dot(row_inputs, gate_up, preferred_element_type=jnp.float32)
    gate_pre = preact[:, :hidden_units]
    up_pre = preact[:, hidden_units:]
    gate_sigmoid = jax.nn.sigmoid(gate_pre)
    hidden = (gate_pre * gate_sigmoid * up_pre).astype(jnp.bfloat16)
    d_hidden = jnp.dot(row_grads, down_matrix.T, preferred_element_type=jnp.float32)
    d_gate_pre = d_hidden * up_pre * gate_sigmoid * (1.0 + gate_pre * (1.0 - gate_sigmoid))
    d_up_pre = d_hidden * gate_pre * gate_sigmoid
    d_preact = jnp.concatenate([d_gate_pre, d_up_pre], axis=1).astype(jnp.bfloat16)
    d_rows = jnp.dot(d_preact, gate_up.T, preferred_element_type=jnp.float32).astype(jnp.bfloat16)
    return (d_rows, hidden, d_preact)


def routed_body(tokens, d_output, combine, routes, gate_weight, up_weight, down_weight):
    experts = lax.axis_size("expert")
    tok_count = tokens.shape[0]
    model_width = tokens.shape[1]
    top_count = routes.shape[1]
    capacity = max(2, (9 * tok_count * top_count + 8 * experts - 1) // (8 * experts))
    slot_count = experts * capacity
    slot_index = route_slots(routes, experts)
    position = (routes * capacity + slot_index).reshape(-1)
    spread_inputs = jnp.repeat(tokens, top_count, axis=0)
    scaled = (
        (combine[:, :, None] * d_output[:, None, :].astype(jnp.float32))
        .astype(jnp.bfloat16)
        .reshape(-1, model_width)
    )
    send_inputs = (
        jnp.zeros((slot_count, model_width), jnp.bfloat16)
        .at[position]
        .set(spread_inputs)
        .reshape(experts, capacity, model_width)
    )
    send_grads = (
        jnp.zeros((slot_count, model_width), jnp.bfloat16)
        .at[position]
        .set(scaled)
        .reshape(experts, capacity, model_width)
    )
    whole_gate, whole_up, whole_down = (
        lax.all_gather(gate_weight, "dp", axis=1, tiled=True),
        lax.all_gather(up_weight, "dp", axis=1, tiled=True),
        lax.all_gather(down_weight, "dp", axis=2, tiled=True),
    )
    gate_up = jnp.concatenate([whole_gate[0], whole_up[0]], axis=1)
    down_matrix = whole_down[0]
    hidden_units = down_matrix.shape[0]
    recv_inputs, recv_grads = (
        lax.all_to_all(send_inputs, "expert", split_axis=0, concat_axis=0, tiled=True),
        lax.all_to_all(send_grads, "expert", split_axis=0, concat_axis=0, tiled=True),
    )
    flat_inputs = recv_inputs.reshape(-1, model_width)
    flat_grads = recv_grads.reshape(-1, model_width)
    d_rows, hidden, d_preact = row_work(flat_inputs, flat_grads, gate_up, down_matrix)
    returned = lax.all_to_all(
        d_rows.reshape(experts, capacity, model_width),
        "expert",
        split_axis=0,
        concat_axis=0,
        tiled=True,
    )
    route_rows = returned.reshape(-1, model_width)[position].reshape(
        tok_count, top_count, model_width
    )
    d_tokens = jnp.sum(route_rows.astype(jnp.float32), axis=1).astype(jnp.bfloat16)
    gate_up_grad = jnp.dot(flat_inputs.T, d_preact, preferred_element_type=jnp.float32)
    down_grad = jnp.dot(flat_grads.T, hidden, preferred_element_type=jnp.float32)
    stacked = jnp.concatenate([gate_up_grad, down_grad], axis=1)
    summed = lax.psum_scatter(
        stacked.astype(jnp.bfloat16), "dp", scatter_dimension=0, tiled=True
    ).astype(jnp.float32)
    d_gate_weight = summed[:, :hidden_units][None]
    d_up_weight = summed[:, hidden_units : 2 * hidden_units][None]
    d_down_weight = summed[:, 2 * hidden_units :].T[None]
    return (d_tokens, d_gate_weight, d_up_weight, d_down_weight)


def solution(mesh):
    placed = (
        P(("dp", "expert"), None),
        P(("dp", "expert"), None),
        P(("dp", "expert"), None),
        P(("dp", "expert"), None),
        P("expert", "dp", None),
        P("expert", "dp", None),
        P("expert", None, "dp"),
    )
    dense = mesh.shape["expert"] == Z * Y * CORES and mesh.shape["dp"] == 2
    return jax.shard_map(
        dense_body if dense else routed_body,
        mesh=mesh,
        in_specs=placed,
        out_specs=(
            P(("dp", "expert"), None),
            P("expert", "dp", None),
            P("expert", "dp", None),
            P("expert", None, "dp"),
        ),
        check_vma=False,
    )
```

```python
import functools

import jax
import jax.numpy as jnp
from jax import lax
from jax.experimental import pallas as pl
from jax.experimental.pallas import tpu as pltpu
from jax.sharding import PartitionSpec as P

F32 = jnp.float32
BF16 = jnp.bfloat16
LANES = 128
VMEM_BYTES = 56 * 1024 * 1024


def vmem():
    return pl.BlockSpec(memory_space=pltpu.VMEM)


def smem():
    return pl.BlockSpec(memory_space=pltpu.SMEM)


def hbm():
    return pl.BlockSpec(memory_space=pl.ANY)


def params():
    return pltpu.CompilerParams(vmem_limit_bytes=VMEM_BYTES)


def cost(flops, moved):
    return pl.CostEstimate(flops=int(flops), bytes_accessed=int(moved), transcendentals=0)


def dot(a, b, dims):
    return lax.dot_general(a, b, (dims, ((), ())), preferred_element_type=F32)


def pack_kernel(experts, tokens, d_output, combine, routes, gate, up, down, out, w_out, parts, turned, sems):
    rows, width = tokens.shape
    hidden_units = gate.shape[1]
    copies = []

    def start(source, target):
        copy = pltpu.make_async_copy(source, target, sems.at[len(copies)])
        copy.start()
        copies.append(copy)

    start(tokens, out.at[:, pl.ds(0, width)])
    start(d_output, out.at[:, pl.ds(width, width)])
    start(gate, w_out.at[:, pl.ds(0, hidden_units)])
    start(up, w_out.at[:, pl.ds(hidden_units, hidden_units)])
    turned[...] = down[...].T
    start(turned, w_out.at[:, pl.ds(2 * hidden_units, hidden_units)])
    line = lax.broadcasted_iota(jnp.int32, (LANES, rows), 0)
    expert = lax.rem(line, experts)
    dense = jnp.zeros((LANES, rows), F32)
    for k in range(routes.shape[0]):
        dense = dense + jnp.where(expert == routes[k : k + 1, :], combine[k : k + 1, :], 0.0)
    high = dense.astype(BF16).astype(F32)
    rest = dense - high
    middle = rest.astype(BF16).astype(F32)
    low = rest - middle
    whole = jnp.where(
        line < experts,
        high,
        jnp.where(line < 2 * experts, middle, jnp.where(line < 3 * experts, low, 0.0)),
    )
    parts[...] = whole.T.astype(BF16)
    start(parts, out.at[:, pl.ds(2 * width, LANES)])
    for c in copies:
        c.wait()


def pack(experts, tokens, d_output, combine, routes, gate, up, down):
    rows, width = tokens.shape
    size, hidden_units = gate.shape
    return pl.pallas_call(
        functools.partial(pack_kernel, experts),
        out_shape=[
            jax.ShapeDtypeStruct((rows, 2 * width + LANES), BF16),
            jax.ShapeDtypeStruct((size, 3 * hidden_units), BF16),
        ],
        in_specs=[vmem()] * 7,
        out_specs=[hbm(), hbm()],
        scratch_shapes=[
            pltpu.VMEM((rows, LANES), BF16),
            pltpu.VMEM((size, hidden_units), BF16),
            pltpu.SemaphoreType.DMA((6,)),
        ],
        cost_estimate=cost(0, 1 << 20),
        compiler_params=params(),
    )(tokens, d_output, combine.T, routes.T, gate, up, down)


def rows_kernel(experts, count, sizes, which, halves, scal, *refs):
    refs = list(refs)
    blocks = [refs.pop(0) for _ in range(count)]
    raw = [refs.pop(0) for _ in range(2 * len(which))]
    past, kinds, wanted_sides, adds = halves
    past_blocks = [refs.pop(0) for _ in range(past)]
    past_grads = [refs.pop(0) for _ in range(kinds)]
    past_scaled = [refs.pop(0) for _ in range(kinds)]
    more = refs.pop(0) if adds else None
    out_rows = [refs.pop(0) for _ in sizes]
    kept = [refs.pop(0) for _ in range(2 * len(which))]
    products = [refs.pop(0) for _ in wanted_sides]
    block, held, grads, scaled, d_rows, in_sems, out_sems = refs[:7]
    part, expert = scal[0], scal[1]
    size, stacked = raw[0].shape
    hidden_units = stacked // 3
    both = 2 * hidden_units
    width = 2 * size
    rows = blocks[0].shape[0]
    sides = [pl.multiple_of(part * size, size), pl.multiple_of((1 - part) * size, size)]
    started, leaving = [], []

    def start(source, target):
        copy = pltpu.make_async_copy(source, target, in_sems.at[len(started)])
        copy.start()
        started.append(copy)
        return copy

    def leave(source, target):
        copy = pltpu.make_async_copy(source, target, out_sems.at[len(leaving)])
        copy.start()
        leaving.append(copy)

    arrivals = [start(b, block.at[pl.ds(i * rows, rows), :]) for i, b in enumerate(blocks)]
    weights = [start(w, held.at[i]) for i, w in enumerate(raw)]
    later = []
    if wanted_sides:
        lefts, made, extra, done = refs[7:]
        row = 0
        for g, x in zip(past_grads, past_scaled):
            n = g.shape[0]
            later.append(start(g, made.at[pl.ds(row, n), :]))
            for k, side in enumerate(wanted_sides):
                later.append(start(x.at[:, pl.ds(sides[side], size)], lefts.at[k, 1, pl.ds(row, n), :]))
            row += n
        for i, b in enumerate(past_blocks):
            for k, side in enumerate(wanted_sides):
                later.append(start(b.at[:, pl.ds(sides[side], size)], lefts.at[k, 0, pl.ds(i * rows, rows), :]))
        if adds:
            later.append(start(more, extra))
    for c in arrivals:
        c.wait()
    parts = block[:, 2 * width :].astype(F32)
    lane = lax.broadcasted_iota(jnp.int32, parts.shape, 1)
    first = []
    for i, one in enumerate(which):
        for c in weights[2 * i : 2 * i + 2]:
            c.wait()
        wanted = expert if one == 0 else expert + 1 - 2 * lax.rem(expert, 2)
        mine = (lax.rem(lane, experts) == wanted) & (lane < 3 * experts)
        weight = jnp.sum(jnp.where(mine, parts, 0.0), axis=1, keepdims=True)
        preact = None
        d_hidden = None
        for side in range(2):
            at = sides[side]
            grad = block[:, pl.ds(pl.multiple_of(width + at, size), size)]
            scaled_half = (weight * grad.astype(F32)).astype(BF16)
            scaled[i, :, pl.ds(at, size)] = scaled_half
            p = dot(block[:, pl.ds(at, size)], held[2 * i + side, :, :both], ((1,), (0,)))
            h = dot(scaled_half, held[2 * i + side, :, both:], ((1,), (0,)))
            preact = p if side == 0 else preact + p
            d_hidden = h if side == 0 else d_hidden + h
        first.append((preact, d_hidden))
    for i in range(len(which)):
        leave(scaled.at[i], kept[2 * i + 1])
    second = []
    for i in range(len(which)):
        preact, d_hidden = first[i]
        gate_pre = preact[:, :hidden_units]
        up_pre = preact[:, hidden_units:]
        sig = jax.nn.sigmoid(gate_pre)
        silu = gate_pre * sig
        d_gate = (d_hidden * up_pre * sig * (1.0 + gate_pre * (1.0 - sig))).astype(BF16)
        d_up = (d_hidden * silu).astype(BF16)
        grads[i, :, :hidden_units] = d_gate
        grads[i, :, hidden_units:both] = d_up
        grads[i, :, both:] = (silu * up_pre).astype(BF16)
        d_preact = jnp.concatenate([d_gate, d_up], axis=1)
        second.append([dot(d_preact, held[2 * i + side, :, :both], ((1,), (1,))) for side in range(2)])
    for i in range(len(which)):
        leave(grads.at[i], kept[2 * i])
    for side in range(2):
        d_rows[:, pl.ds(sides[side], size)] = sum(x[side] for x in second).astype(BF16)
    row = 0
    for out, n in zip(out_rows, sizes):
        leave(d_rows.at[pl.ds(row, n), :], out)
        row += n
    for c in later:
        c.wait()
    end = len(which) - 1
    for k, side in enumerate(wanted_sides):
        at = sides[side]
        for kind, span in enumerate((slice(0, both), slice(both, stacked))):
            now = block[:, pl.ds(at, size)] if kind == 0 else scaled[end, :, pl.ds(at, size)]
            new = dot(lefts[k, kind], made[:, span], ((0,), (0,))) + dot(now, grads[end, :, span], ((0,), (0,)))
            if adds:
                new = new + extra[:, span].astype(F32)
            done[k, :, span] = new.astype(BF16)
        leave(done.at[k], products[k])
    for c in leaving:
        c.wait()


def rows_call(experts, scal, groups, weights, which=(0, 1), past=((), ()), sides=(), more=None):
    blocks = [b for group in groups for b in group]
    count = len(blocks)
    rows = blocks[0].shape[0]
    size, stacked = weights[0].shape
    total = count * rows
    sizes = [len(group) * rows for group in groups]
    sds = jax.ShapeDtypeStruct
    out = [sds((n, 2 * size), BF16) for n in sizes]
    out += [sds((total, stacked), BF16), sds((total, 2 * size), BF16)] * len(which)
    out += [sds((size, stacked), BF16)] * len(sides)
    past_blocks, past_kept = past
    operands = [*blocks, *weights, *past_blocks, *(k[0] for k in past_kept), *(k[1] for k in past_kept)]
    if more is not None:
        operands.append(more)
    scratch = [
        pltpu.VMEM((total, blocks[0].shape[1]), BF16),
        pltpu.VMEM((len(weights), size, stacked), BF16),
        pltpu.VMEM((len(which), total, stacked), BF16),
        pltpu.VMEM((len(which), total, 2 * size), BF16),
        pltpu.VMEM((total, 2 * size), BF16),
        pltpu.SemaphoreType.DMA((len(operands) + len(sides) * (len(past_blocks) + len(past_kept)),)),
        pltpu.SemaphoreType.DMA((len(out),)),
    ]
    if sides:
        earlier = len(past_blocks) * rows
        scratch += [
            pltpu.VMEM((len(sides), 2, earlier, size), BF16),
            pltpu.VMEM((earlier, stacked), BF16),
            pltpu.VMEM((size, stacked), BF16),
            pltpu.VMEM((len(sides), size, stacked), BF16),
        ]
    halves = (len(past_blocks), len(past_kept), sides, more is not None)
    return pl.pallas_call(
        functools.partial(rows_kernel, experts, count, sizes, which, halves),
        out_shape=out,
        in_specs=[smem()] + [hbm()] * len(operands),
        out_specs=[hbm()] * len(out),
        scratch_shapes=scratch,
        cost_estimate=cost(24 * total * size * stacked * len(which) * (1 if len(which) == 2 else 10), 1 << 20),
        compiler_params=params(),
    )(scal, *operands)


def half_kernel(count, groups, sides, *refs):
    refs = list(refs)
    blocks = [refs.pop(0) for _ in range(count)]
    scaled = [refs.pop(0) for _ in range(groups)]
    grads = [refs.pop(0) for _ in range(groups)]
    more, out, lefts, made, extra, done, sems, out_sems = refs
    size, stacked = done.shape
    both = stacked // 3 * 2
    rows = blocks[0].shape[0]
    at = pl.multiple_of(sides[0] * size, size)
    started = []

    def start(source, target):
        copy = pltpu.make_async_copy(source, target, sems.at[len(started)])
        copy.start()
        started.append(copy)

    for i, b in enumerate(blocks):
        start(b.at[:, pl.ds(at, size)], lefts.at[0, pl.ds(i * rows, rows), :])
    row = 0
    for g in grads:
        start(g, made.at[pl.ds(row, g.shape[0]), :])
        row += g.shape[0]
    start(more, extra)
    early = len(started)
    row = 0
    for x in scaled:
        start(x.at[:, pl.ds(at, size)], lefts.at[1, pl.ds(row, x.shape[0]), :])
        row += x.shape[0]
    leaving = []
    for kind, (first, wide) in enumerate(((0, both), (both, stacked - both))):
        for c in started[:early] if kind == 0 else started[early:]:
            c.wait()
        new = dot(lefts[kind], made[:, first : first + wide], ((0,), (0,)))
        done[:, first : first + wide] = (new + extra[:, first : first + wide].astype(F32)).astype(BF16)
        copy = pltpu.make_async_copy(
            done.at[:, pl.ds(first, wide)], out.at[:, pl.ds(first, wide)], out_sems.at[len(leaving)]
        )
        copy.start()
        leaving.append(copy)
    for c in leaving:
        c.wait()


def half_call(sides, blocks, kept, more):
    grads, scaled = [k[0] for k in kept], [k[1] for k in kept]
    size = scaled[0].shape[1] // 2
    stacked = grads[0].shape[1]
    total = len(blocks) * blocks[0].shape[0]
    operands = [*blocks, *scaled, *grads, more]
    return pl.pallas_call(
        functools.partial(half_kernel, len(blocks), len(kept)),
        out_shape=jax.ShapeDtypeStruct((size, stacked), BF16),
        in_specs=[smem()] + [hbm()] * len(operands),
        out_specs=hbm(),
        scratch_shapes=[
            pltpu.VMEM((2, total, size), BF16),
            pltpu.VMEM((total, stacked), BF16),
            pltpu.VMEM((size, stacked), BF16),
            pltpu.VMEM((size, stacked), BF16),
            pltpu.SemaphoreType.DMA((len(operands),)),
            pltpu.SemaphoreType.DMA((2,)),
        ],
        cost_estimate=cost(1024, 1024),
        compiler_params=params(),
    )(sides, *operands)


Z, Y, CORES = 4, 2, 2


def pairs_of(move):
    out = []
    for z in range(Z):
        for y in range(Y):
            for c in range(CORES):
                to = move(z, y, c)
                if to is not None:
                    out.append(((z * Y + y) * CORES + c, (to[0] * Y + to[1]) * CORES + to[2]))
    return out


def along_z(table):
    return pairs_of(lambda z, y, c: (table[z], y, c) if z in table else None)


SWAP_CORE = pairs_of(lambda z, y, c: (z, y, 1 - c))
SWAP_Y = pairs_of(lambda z, y, c: (z, 1 - y, c))
OUTER = along_z({0: 1, 1: 0, 2: 3, 3: 2})
INNER = along_z({1: 2, 2: 1})
OUTWARD = along_z({1: 0, 2: 3})
INWARD = along_z({0: 1, 3: 2})
SKIP_TO_OUTER = along_z({1: 3, 2: 0})


def after(value, *others):
    return lax.optimization_barrier((value,) + others)[0]


def dense_body(tokens, d_output, combine, routes, gate_weight, up_weight, down_weight):
    experts = lax.axis_size("expert")
    part = lax.axis_index("dp")
    expert = lax.axis_index("expert")
    z = expert // (Y * CORES)
    inner = (z == 1) | (z == 2)
    scal = jnp.stack([part, expert]).astype(jnp.int32)
    mine = part[None].astype(jnp.int32)
    other = (1 - part)[None].astype(jnp.int32)

    move = lambda a, pairs: lax.ppermute(a, "expert", pairs)
    across = lambda a: lax.ppermute(a, "dp", [(0, 1), (1, 0)])

    swap = lambda a: move(a, SWAP_CORE)
    own, w_own = pack(experts, tokens, d_output, combine, routes, gate_weight[0], up_weight[0], down_weight[0])
    w_part = across(w_own)

    b1 = move(own, OUTER)
    f1 = move(own, INNER)
    y0 = move(own, SWAP_Y)
    f2 = move(b1, INNER)
    y1 = move(after(b1, y0), SWAP_Y)
    g1 = move(f1, OUTWARD)
    b2 = jnp.where(inner, f1, g1)
    y2 = move(after(b2, y1, f2), SWAP_Y)
    g2 = move(f2, OUTWARD)

    w_core = swap(after(w_own, y1, f2))
    w_both = swap(after(w_part, y1, f2))
    weights = [w_own, w_part, w_core, w_both]
    p0, p1, p2, q0, q1, *kept_a = rows_call(experts, scal, [[own], [b1], [b2], [y0], [y1]], weights)
    b3 = jnp.where(inner, f2, after(g2, p0))
    y3 = move(after(b3, y2), SWAP_Y)
    early = [own, b1, b2, y0, y1]

    p3, q2, *kept_b, to_other, to_mine = rows_call(
        experts, scal, [[b3], [y2]], weights, past=(early, [kept_a[2:]]), sides=(1, 0)
    )
    y3 = after(y3, q2)
    cy3 = swap(y3)
    got_other, got_mine = swap(after(to_other, y3)), swap(after(to_mine, y3, cy3))
    r2 = move(after(q2, y3), SWAP_Y)
    r1 = move(after(q1, y3), SWAP_Y)

    blocks = early + [b3, y2]
    kept = [kept_a[:2], kept_b[:2]]
    last, pair, *kept_c, send = rows_call(
        experts, scal, [[y3], [cy3]], weights[:2], which=(0,), past=(blocks, kept), sides=(1,), more=got_other
    )
    from_part = across(send)
    add = lambda *terms: sum(t.astype(F32) for t in terms).astype(BF16)
    r3 = move(add(last, swap(after(pair, r2, r1, got_mine))), SWAP_Y)
    r0 = move(after(q0, r3), SWAP_Y)
    s2 = add(p2, r2)
    s2 = add(s2, move(s2, INWARD))
    s3 = add(p3, r3)
    s3 = add(s3, move(s3, INWARD))
    keep = half_call(after(mine, send, s3), blocks + [y3, cy3], kept + [kept_c], more=got_mine)

    s1 = after(add(p1, r1), keep)
    from_part = after(from_part, s3)
    hidden_units = gate_weight.shape[2]
    whole = lambda a: keep[:, a : a + hidden_units].astype(F32) + from_part[:, a : a + hidden_units].astype(F32)
    d_gate, d_up, d_down = whole(0), whole(hidden_units), whole(2 * hidden_units).T
    d_tokens = add(after(p0, from_part), r0, move(s1, OUTER), move(s2, INNER), move(s3, SKIP_TO_OUTER))
    return (d_tokens, d_gate[None], d_up[None], d_down[None])


def route_slots(routes, experts):
    matches = (routes[:, :, None] == jnp.arange(experts, dtype=jnp.int32)[None, None, :]).astype(
        jnp.int32
    )
    per_token = jnp.sum(matches, axis=1)
    earlier = jnp.cumsum(per_token, axis=0) - per_token
    return jnp.sum(matches * earlier[:, None, :], axis=2)


def row_work(row_inputs, row_grads, gate_up, down_matrix):
    hidden_units = down_matrix.shape[0]
    preact = jnp.dot(row_inputs, gate_up, preferred_element_type=jnp.float32)
    gate_pre = preact[:, :hidden_units]
    up_pre = preact[:, hidden_units:]
    gate_sigmoid = jax.nn.sigmoid(gate_pre)
    hidden = (gate_pre * gate_sigmoid * up_pre).astype(jnp.bfloat16)
    d_hidden = jnp.dot(row_grads, down_matrix.T, preferred_element_type=jnp.float32)
    d_gate_pre = d_hidden * up_pre * gate_sigmoid * (1.0 + gate_pre * (1.0 - gate_sigmoid))
    d_up_pre = d_hidden * gate_pre * gate_sigmoid
    d_preact = jnp.concatenate([d_gate_pre, d_up_pre], axis=1).astype(jnp.bfloat16)
    d_rows = jnp.dot(d_preact, gate_up.T, preferred_element_type=jnp.float32).astype(jnp.bfloat16)
    return (d_rows, hidden, d_preact)


def routed_body(tokens, d_output, combine, routes, gate_weight, up_weight, down_weight):
    experts = lax.axis_size("expert")
    tok_count = tokens.shape[0]
    model_width = tokens.shape[1]
    top_count = routes.shape[1]
    capacity = max(2, (9 * tok_count * top_count + 8 * experts - 1) // (8 * experts))
    slot_count = experts * capacity
    slot_index = route_slots(routes, experts)
    position = (routes * capacity + slot_index).reshape(-1)
    spread_inputs = jnp.repeat(tokens, top_count, axis=0)
    scaled = (
        (combine[:, :, None] * d_output[:, None, :].astype(jnp.float32))
        .astype(jnp.bfloat16)
        .reshape(-1, model_width)
    )
    send_inputs = (
        jnp.zeros((slot_count, model_width), jnp.bfloat16)
        .at[position]
        .set(spread_inputs)
        .reshape(experts, capacity, model_width)
    )
    send_grads = (
        jnp.zeros((slot_count, model_width), jnp.bfloat16)
        .at[position]
        .set(scaled)
        .reshape(experts, capacity, model_width)
    )
    whole_gate, whole_up, whole_down = (
        lax.all_gather(gate_weight, "dp", axis=1, tiled=True),
        lax.all_gather(up_weight, "dp", axis=1, tiled=True),
        lax.all_gather(down_weight, "dp", axis=2, tiled=True),
    )
    gate_up = jnp.concatenate([whole_gate[0], whole_up[0]], axis=1)
    down_matrix = whole_down[0]
    hidden_units = down_matrix.shape[0]
    recv_inputs, recv_grads = (
        lax.all_to_all(send_inputs, "expert", split_axis=0, concat_axis=0, tiled=True),
        lax.all_to_all(send_grads, "expert", split_axis=0, concat_axis=0, tiled=True),
    )
    flat_inputs = recv_inputs.reshape(-1, model_width)
    flat_grads = recv_grads.reshape(-1, model_width)
    d_rows, hidden, d_preact = row_work(flat_inputs, flat_grads, gate_up, down_matrix)
    returned = lax.all_to_all(
        d_rows.reshape(experts, capacity, model_width),
        "expert",
        split_axis=0,
        concat_axis=0,
        tiled=True,
    )
    route_rows = returned.reshape(-1, model_width)[position].reshape(
        tok_count, top_count, model_width
    )
    d_tokens = jnp.sum(route_rows.astype(jnp.float32), axis=1).astype(jnp.bfloat16)
    gate_up_grad = jnp.dot(flat_inputs.T, d_preact, preferred_element_type=jnp.float32)
    down_grad = jnp.dot(flat_grads.T, hidden, preferred_element_type=jnp.float32)
    stacked = jnp.concatenate([gate_up_grad, down_grad], axis=1)
    summed = lax.psum_scatter(
        stacked.astype(jnp.bfloat16), "dp", scatter_dimension=0, tiled=True
    ).astype(jnp.float32)
    d_gate_weight = summed[:, :hidden_units][None]
    d_up_weight = summed[:, hidden_units : 2 * hidden_units][None]
    d_down_weight = summed[:, 2 * hidden_units :].T[None]
    return (d_tokens, d_gate_weight, d_up_weight, d_down_weight)


def solution(mesh):
    placed = (
        P(("dp", "expert"), None),
        P(("dp", "expert"), None),
        P(("dp", "expert"), None),
        P(("dp", "expert"), None),
        P("expert", "dp", None),
        P("expert", "dp", None),
        P("expert", None, "dp"),
    )
    dense = mesh.shape["expert"] == Z * Y * CORES and mesh.shape["dp"] == 2
    return jax.shard_map(
        dense_body if dense else routed_body,
        mesh=mesh,
        in_specs=placed,
        out_specs=(
            P(("dp", "expert"), None),
            P("expert", "dp", None),
            P("expert", "dp", None),
            P("expert", None, "dp"),
        ),
        check_vma=False,
    )
```

```python
import functools

import jax
import jax.numpy as jnp
from jax import lax
from jax.experimental import pallas as pl
from jax.experimental.pallas import tpu as pltpu
from jax.sharding import PartitionSpec as P

F32 = jnp.float32
BF16 = jnp.bfloat16
LANES = 128
VMEM_BYTES = 56 * 1024 * 1024


def vmem():
    return pl.BlockSpec(memory_space=pltpu.VMEM)


def smem():
    return pl.BlockSpec(memory_space=pltpu.SMEM)


def hbm():
    return pl.BlockSpec(memory_space=pl.ANY)


def params():
    return pltpu.CompilerParams(vmem_limit_bytes=VMEM_BYTES)


def cost(flops, moved):
    return pl.CostEstimate(flops=int(flops), bytes_accessed=int(moved), transcendentals=0)


def dot(a, b, dims):
    return lax.dot_general(a, b, (dims, ((), ())), preferred_element_type=F32)


def pack_kernel(experts, tokens, d_output, combine, routes, gate, up, down, out, w_out, parts, turned, sems):
    rows, width = tokens.shape
    hidden_units = gate.shape[1]
    copies = []

    def start(source, target):
        copy = pltpu.make_async_copy(source, target, sems.at[len(copies)])
        copy.start()
        copies.append(copy)

    start(tokens, out.at[:, pl.ds(0, width)])
    start(d_output, out.at[:, pl.ds(width, width)])
    start(gate, w_out.at[:, pl.ds(0, hidden_units)])
    start(up, w_out.at[:, pl.ds(hidden_units, hidden_units)])
    turned[...] = down[...].T
    start(turned, w_out.at[:, pl.ds(2 * hidden_units, hidden_units)])
    line = lax.broadcasted_iota(jnp.int32, (LANES, rows), 0)
    expert = lax.rem(line, experts)
    dense = jnp.zeros((LANES, rows), F32)
    for k in range(routes.shape[0]):
        dense = dense + jnp.where(expert == routes[k : k + 1, :], combine[k : k + 1, :], 0.0)
    high = dense.astype(BF16).astype(F32)
    rest = dense - high
    middle = rest.astype(BF16).astype(F32)
    low = rest - middle
    whole = jnp.where(
        line < experts,
        high,
        jnp.where(line < 2 * experts, middle, jnp.where(line < 3 * experts, low, 0.0)),
    )
    parts[...] = whole.T.astype(BF16)
    start(parts, out.at[:, pl.ds(2 * width, LANES)])
    for c in copies:
        c.wait()


def pack(experts, tokens, d_output, combine, routes, gate, up, down):
    rows, width = tokens.shape
    size, hidden_units = gate.shape
    return pl.pallas_call(
        functools.partial(pack_kernel, experts),
        out_shape=[
            jax.ShapeDtypeStruct((rows, 2 * width + LANES), BF16),
            jax.ShapeDtypeStruct((size, 3 * hidden_units), BF16),
        ],
        in_specs=[vmem()] * 7,
        out_specs=[hbm(), hbm()],
        scratch_shapes=[
            pltpu.VMEM((rows, LANES), BF16),
            pltpu.VMEM((size, hidden_units), BF16),
            pltpu.SemaphoreType.DMA((6,)),
        ],
        cost_estimate=cost(0, 1 << 20),
        compiler_params=params(),
    )(tokens, d_output, combine.T, routes.T, gate, up, down)


def rows_kernel(experts, count, sizes, which, halves, scal, *refs):
    refs = list(refs)
    blocks = [refs.pop(0) for _ in range(count)]
    raw = [refs.pop(0) for _ in range(2 * len(which))]
    past, kinds, wanted_sides, adds = halves
    past_blocks = [refs.pop(0) for _ in range(past)]
    past_grads = [refs.pop(0) for _ in range(kinds)]
    past_scaled = [refs.pop(0) for _ in range(kinds)]
    more = refs.pop(0) if adds else None
    out_rows = [refs.pop(0) for _ in sizes]
    kept = [refs.pop(0) for _ in range(2 * len(which))]
    products = [refs.pop(0) for _ in wanted_sides]
    block, held, grads, scaled, d_rows, in_sems, out_sems = refs[:7]
    part, expert = scal[0], scal[1]
    size, stacked = raw[0].shape
    hidden_units = stacked // 3
    both = 2 * hidden_units
    width = 2 * size
    rows = blocks[0].shape[0]
    sides = [pl.multiple_of(part * size, size), pl.multiple_of((1 - part) * size, size)]
    started, leaving = [], []

    def start(source, target):
        copy = pltpu.make_async_copy(source, target, in_sems.at[len(started)])
        copy.start()
        started.append(copy)
        return copy

    def leave(source, target):
        copy = pltpu.make_async_copy(source, target, out_sems.at[len(leaving)])
        copy.start()
        leaving.append(copy)

    arrivals = [start(b, block.at[pl.ds(i * rows, rows), :]) for i, b in enumerate(blocks)]
    weights = [start(w, held.at[i]) for i, w in enumerate(raw)]
    later = []
    if wanted_sides:
        lefts, made, extra, done = refs[7:]
        row = 0
        for g, x in zip(past_grads, past_scaled):
            n = g.shape[0]
            later.append(start(g, made.at[pl.ds(row, n), :]))
            for k, side in enumerate(wanted_sides):
                later.append(start(x.at[:, pl.ds(sides[side], size)], lefts.at[k, 1, pl.ds(row, n), :]))
            row += n
        for i, b in enumerate(past_blocks):
            for k, side in enumerate(wanted_sides):
                later.append(start(b.at[:, pl.ds(sides[side], size)], lefts.at[k, 0, pl.ds(i * rows, rows), :]))
        if adds:
            later.append(start(more, extra))
    for c in arrivals:
        c.wait()
    parts = block[:, 2 * width :].astype(F32)
    lane = lax.broadcasted_iota(jnp.int32, parts.shape, 1)
    first = []
    for i, one in enumerate(which):
        for c in weights[2 * i : 2 * i + 2]:
            c.wait()
        wanted = expert if one == 0 else expert + 1 - 2 * lax.rem(expert, 2)
        mine = (lax.rem(lane, experts) == wanted) & (lane < 3 * experts)
        weight = jnp.sum(jnp.where(mine, parts, 0.0), axis=1, keepdims=True)
        preact = None
        d_hidden = None
        for side in range(2):
            at = sides[side]
            grad = block[:, pl.ds(pl.multiple_of(width + at, size), size)]
            scaled_half = (weight * grad.astype(F32)).astype(BF16)
            scaled[i, :, pl.ds(at, size)] = scaled_half
            p = dot(block[:, pl.ds(at, size)], held[2 * i + side, :, :both], ((1,), (0,)))
            h = dot(scaled_half, held[2 * i + side, :, both:], ((1,), (0,)))
            preact = p if side == 0 else preact + p
            d_hidden = h if side == 0 else d_hidden + h
        first.append((preact, d_hidden))
    for i in range(len(which)):
        leave(scaled.at[i], kept[2 * i + 1])
    second = []
    for i in range(len(which)):
        preact, d_hidden = first[i]
        gate_pre = preact[:, :hidden_units]
        up_pre = preact[:, hidden_units:]
        sig = jax.nn.sigmoid(gate_pre)
        silu = gate_pre * sig
        d_gate = (d_hidden * up_pre * sig * (1.0 + gate_pre * (1.0 - sig))).astype(BF16)
        d_up = (d_hidden * silu).astype(BF16)
        grads[i, :, :hidden_units] = d_gate
        grads[i, :, hidden_units:both] = d_up
        grads[i, :, both:] = (silu * up_pre).astype(BF16)
        d_preact = jnp.concatenate([d_gate, d_up], axis=1)
        second.append([dot(d_preact, held[2 * i + side, :, :both], ((1,), (1,))) for side in range(2)])
    for i in range(len(which)):
        leave(grads.at[i], kept[2 * i])
    for side in range(2):
        d_rows[:, pl.ds(sides[side], size)] = sum(x[side] for x in second).astype(BF16)
    row = 0
    for out, n in zip(out_rows, sizes):
        leave(d_rows.at[pl.ds(row, n), :], out)
        row += n
    for c in later:
        c.wait()
    end = len(which) - 1
    for k, side in enumerate(wanted_sides):
        at = sides[side]
        for kind, span in enumerate((slice(0, both), slice(both, stacked))):
            now = block[:, pl.ds(at, size)] if kind == 0 else scaled[end, :, pl.ds(at, size)]
            new = dot(lefts[k, kind], made[:, span], ((0,), (0,))) + dot(now, grads[end, :, span], ((0,), (0,)))
            if adds:
                new = new + extra[:, span].astype(F32)
            done[k, :, span] = new.astype(BF16)
        leave(done.at[k], products[k])
    for c in leaving:
        c.wait()


def rows_call(experts, scal, groups, weights, which=(0, 1), past=((), ()), sides=(), more=None):
    blocks = [b for group in groups for b in group]
    count = len(blocks)
    rows = blocks[0].shape[0]
    size, stacked = weights[0].shape
    total = count * rows
    sizes = [len(group) * rows for group in groups]
    sds = jax.ShapeDtypeStruct
    out = [sds((n, 2 * size), BF16) for n in sizes]
    out += [sds((total, stacked), BF16), sds((total, 2 * size), BF16)] * len(which)
    out += [sds((size, stacked), BF16)] * len(sides)
    past_blocks, past_kept = past
    operands = [*blocks, *weights, *past_blocks, *(k[0] for k in past_kept), *(k[1] for k in past_kept)]
    if more is not None:
        operands.append(more)
    scratch = [
        pltpu.VMEM((total, blocks[0].shape[1]), BF16),
        pltpu.VMEM((len(weights), size, stacked), BF16),
        pltpu.VMEM((len(which), total, stacked), BF16),
        pltpu.VMEM((len(which), total, 2 * size), BF16),
        pltpu.VMEM((total, 2 * size), BF16),
        pltpu.SemaphoreType.DMA((len(operands) + len(sides) * (len(past_blocks) + len(past_kept)),)),
        pltpu.SemaphoreType.DMA((len(out),)),
    ]
    if sides:
        earlier = len(past_blocks) * rows
        scratch += [
            pltpu.VMEM((len(sides), 2, earlier, size), BF16),
            pltpu.VMEM((earlier, stacked), BF16),
            pltpu.VMEM((size, stacked), BF16),
            pltpu.VMEM((len(sides), size, stacked), BF16),
        ]
    halves = (len(past_blocks), len(past_kept), sides, more is not None)
    return pl.pallas_call(
        functools.partial(rows_kernel, experts, count, sizes, which, halves),
        out_shape=out,
        in_specs=[smem()] + [hbm()] * len(operands),
        out_specs=[hbm()] * len(out),
        scratch_shapes=scratch,
        cost_estimate=cost(24 * total * size * stacked * len(which) * (1 if len(which) == 2 else 10), 1 << 20),
        compiler_params=params(),
    )(scal, *operands)


def half_kernel(count, groups, sides, *refs):
    refs = list(refs)
    blocks = [refs.pop(0) for _ in range(count)]
    scaled = [refs.pop(0) for _ in range(groups)]
    grads = [refs.pop(0) for _ in range(groups)]
    more, out, lefts, made, extra, done, sems, out_sems = refs
    size, stacked = done.shape
    both = stacked // 3 * 2
    rows = blocks[0].shape[0]
    at = pl.multiple_of(sides[0] * size, size)
    started = []

    def start(source, target):
        copy = pltpu.make_async_copy(source, target, sems.at[len(started)])
        copy.start()
        started.append(copy)

    for i, b in enumerate(blocks):
        start(b.at[:, pl.ds(at, size)], lefts.at[0, pl.ds(i * rows, rows), :])
    row = 0
    for g in grads:
        start(g, made.at[pl.ds(row, g.shape[0]), :])
        row += g.shape[0]
    start(more, extra)
    early = len(started)
    row = 0
    for x in scaled:
        start(x.at[:, pl.ds(at, size)], lefts.at[1, pl.ds(row, x.shape[0]), :])
        row += x.shape[0]
    leaving = []
    for kind, (first, wide) in enumerate(((0, both), (both, stacked - both))):
        for c in started[:early] if kind == 0 else started[early:]:
            c.wait()
        new = dot(lefts[kind], made[:, first : first + wide], ((0,), (0,)))
        done[:, first : first + wide] = (new + extra[:, first : first + wide].astype(F32)).astype(BF16)
        copy = pltpu.make_async_copy(
            done.at[:, pl.ds(first, wide)], out.at[:, pl.ds(first, wide)], out_sems.at[len(leaving)]
        )
        copy.start()
        leaving.append(copy)
    for c in leaving:
        c.wait()


def half_call(sides, blocks, kept, more):
    grads, scaled = [k[0] for k in kept], [k[1] for k in kept]
    size = scaled[0].shape[1] // 2
    stacked = grads[0].shape[1]
    total = len(blocks) * blocks[0].shape[0]
    operands = [*blocks, *scaled, *grads, more]
    return pl.pallas_call(
        functools.partial(half_kernel, len(blocks), len(kept)),
        out_shape=jax.ShapeDtypeStruct((size, stacked), BF16),
        in_specs=[smem()] + [hbm()] * len(operands),
        out_specs=hbm(),
        scratch_shapes=[
            pltpu.VMEM((2, total, size), BF16),
            pltpu.VMEM((total, stacked), BF16),
            pltpu.VMEM((size, stacked), BF16),
            pltpu.VMEM((size, stacked), BF16),
            pltpu.SemaphoreType.DMA((len(operands),)),
            pltpu.SemaphoreType.DMA((2,)),
        ],
        cost_estimate=cost(1024, 1024),
        compiler_params=params(),
    )(sides, *operands)


Z, Y, CORES = 4, 2, 2


def pairs_of(move):
    out = []
    for z in range(Z):
        for y in range(Y):
            for c in range(CORES):
                to = move(z, y, c)
                if to is not None:
                    out.append(((z * Y + y) * CORES + c, (to[0] * Y + to[1]) * CORES + to[2]))
    return out


def along_z(table):
    return pairs_of(lambda z, y, c: (table[z], y, c) if z in table else None)


SWAP_CORE = pairs_of(lambda z, y, c: (z, y, 1 - c))
SWAP_Y = pairs_of(lambda z, y, c: (z, 1 - y, c))
OUTER = along_z({0: 1, 1: 0, 2: 3, 3: 2})
INNER = along_z({1: 2, 2: 1})
OUTWARD = along_z({1: 0, 2: 3})
INWARD = along_z({0: 1, 3: 2})
SKIP_TO_OUTER = along_z({1: 3, 2: 0})


def after(value, *others):
    return lax.optimization_barrier((value,) + others)[0]


def dense_body(tokens, d_output, combine, routes, gate_weight, up_weight, down_weight):
    experts = lax.axis_size("expert")
    part = lax.axis_index("dp")
    expert = lax.axis_index("expert")
    z = expert // (Y * CORES)
    inner = (z == 1) | (z == 2)
    scal = jnp.stack([part, expert]).astype(jnp.int32)
    mine = part[None].astype(jnp.int32)
    other = (1 - part)[None].astype(jnp.int32)

    move = lambda a, pairs: lax.ppermute(a, "expert", pairs)
    across = lambda a: lax.ppermute(a, "dp", [(0, 1), (1, 0)])

    swap = lambda a: move(a, SWAP_CORE)
    own, w_own = pack(experts, tokens, d_output, combine, routes, gate_weight[0], up_weight[0], down_weight[0])
    w_part = across(w_own)

    b1 = move(own, OUTER)
    f1 = move(own, INNER)
    y0 = move(own, SWAP_Y)
    f2 = move(b1, INNER)
    y1 = move(after(b1, y0), SWAP_Y)
    g1 = move(f1, OUTWARD)
    b2 = jnp.where(inner, f1, g1)
    y2 = move(after(b2, y1, f2), SWAP_Y)
    g2 = move(f2, OUTWARD)

    w_core = swap(after(w_own, y1, f2))
    w_both = swap(after(w_part, y1, f2))
    weights = [w_own, w_part, w_core, w_both]
    p0, p1, p2, q0, q1, *kept_a = rows_call(experts, scal, [[own], [b1], [b2], [y0], [y1]], weights)
    b3 = jnp.where(inner, f2, after(g2, p0))
    y3 = move(after(b3, y2), SWAP_Y)
    early = [own, b1, b2, y0, y1]

    p3, q2, *kept_b, to_other, to_mine = rows_call(
        experts, scal, [[b3], [y2]], weights, past=(early, [kept_a[2:]]), sides=(1, 0)
    )
    y3 = after(y3, q2)
    cy3 = swap(y3)
    got_other, got_mine = swap(after(to_other, y3)), swap(after(to_mine, y3, cy3))
    r2 = move(after(q2, y3), SWAP_Y)

    blocks = early + [b3, y2]
    kept = [kept_a[:2], kept_b[:2]]
    last, pair, *kept_c, send = rows_call(
        experts, scal, [[y3], [cy3]], weights[:2], which=(0,), past=(blocks, kept), sides=(1,), more=got_other
    )
    from_part = across(send)
    add = lambda *terms: sum(t.astype(F32) for t in terms).astype(BF16)
    r3 = move(add(last, swap(after(pair, r2, got_mine))), SWAP_Y)
    r1, r0 = (move(after(q, r3), SWAP_Y) for q in (q1, q0))
    s2 = add(p2, r2)
    s2 = add(s2, move(s2, INWARD))
    s3 = add(p3, r3)
    s3 = add(s3, move(s3, INWARD))
    keep = half_call(after(mine, send, s3), blocks + [y3, cy3], kept + [kept_c], more=got_mine)

    s1 = after(add(p1, r1), keep)
    from_part = after(from_part, s3)
    hidden_units = gate_weight.shape[2]
    whole = lambda a: keep[:, a : a + hidden_units].astype(F32) + from_part[:, a : a + hidden_units].astype(F32)
    d_gate, d_up, d_down = whole(0), whole(hidden_units), whole(2 * hidden_units).T
    d_tokens = add(after(p0, from_part), r0, move(s1, OUTER), move(s2, INNER), move(s3, SKIP_TO_OUTER))
    return (d_tokens, d_gate[None], d_up[None], d_down[None])


def route_slots(routes, experts):
    matches = (routes[:, :, None] == jnp.arange(experts, dtype=jnp.int32)[None, None, :]).astype(
        jnp.int32
    )
    per_token = jnp.sum(matches, axis=1)
    earlier = jnp.cumsum(per_token, axis=0) - per_token
    return jnp.sum(matches * earlier[:, None, :], axis=2)


def row_work(row_inputs, row_grads, gate_up, down_matrix):
    hidden_units = down_matrix.shape[0]
    preact = jnp.dot(row_inputs, gate_up, preferred_element_type=jnp.float32)
    gate_pre = preact[:, :hidden_units]
    up_pre = preact[:, hidden_units:]
    gate_sigmoid = jax.nn.sigmoid(gate_pre)
    hidden = (gate_pre * gate_sigmoid * up_pre).astype(jnp.bfloat16)
    d_hidden = jnp.dot(row_grads, down_matrix.T, preferred_element_type=jnp.float32)
    d_gate_pre = d_hidden * up_pre * gate_sigmoid * (1.0 + gate_pre * (1.0 - gate_sigmoid))
    d_up_pre = d_hidden * gate_pre * gate_sigmoid
    d_preact = jnp.concatenate([d_gate_pre, d_up_pre], axis=1).astype(jnp.bfloat16)
    d_rows = jnp.dot(d_preact, gate_up.T, preferred_element_type=jnp.float32).astype(jnp.bfloat16)
    return (d_rows, hidden, d_preact)


def routed_body(tokens, d_output, combine, routes, gate_weight, up_weight, down_weight):
    experts = lax.axis_size("expert")
    tok_count = tokens.shape[0]
    model_width = tokens.shape[1]
    top_count = routes.shape[1]
    capacity = max(2, (9 * tok_count * top_count + 8 * experts - 1) // (8 * experts))
    slot_count = experts * capacity
    slot_index = route_slots(routes, experts)
    position = (routes * capacity + slot_index).reshape(-1)
    spread_inputs = jnp.repeat(tokens, top_count, axis=0)
    scaled = (
        (combine[:, :, None] * d_output[:, None, :].astype(jnp.float32))
        .astype(jnp.bfloat16)
        .reshape(-1, model_width)
    )
    send_inputs = (
        jnp.zeros((slot_count, model_width), jnp.bfloat16)
        .at[position]
        .set(spread_inputs)
        .reshape(experts, capacity, model_width)
    )
    send_grads = (
        jnp.zeros((slot_count, model_width), jnp.bfloat16)
        .at[position]
        .set(scaled)
        .reshape(experts, capacity, model_width)
    )
    whole_gate, whole_up, whole_down = (
        lax.all_gather(gate_weight, "dp", axis=1, tiled=True),
        lax.all_gather(up_weight, "dp", axis=1, tiled=True),
        lax.all_gather(down_weight, "dp", axis=2, tiled=True),
    )
    gate_up = jnp.concatenate([whole_gate[0], whole_up[0]], axis=1)
    down_matrix = whole_down[0]
    hidden_units = down_matrix.shape[0]
    recv_inputs, recv_grads = (
        lax.all_to_all(send_inputs, "expert", split_axis=0, concat_axis=0, tiled=True),
        lax.all_to_all(send_grads, "expert", split_axis=0, concat_axis=0, tiled=True),
    )
    flat_inputs = recv_inputs.reshape(-1, model_width)
    flat_grads = recv_grads.reshape(-1, model_width)
    d_rows, hidden, d_preact = row_work(flat_inputs, flat_grads, gate_up, down_matrix)
    returned = lax.all_to_all(
        d_rows.reshape(experts, capacity, model_width),
        "expert",
        split_axis=0,
        concat_axis=0,
        tiled=True,
    )
    route_rows = returned.reshape(-1, model_width)[position].reshape(
        tok_count, top_count, model_width
    )
    d_tokens = jnp.sum(route_rows.astype(jnp.float32), axis=1).astype(jnp.bfloat16)
    gate_up_grad = jnp.dot(flat_inputs.T, d_preact, preferred_element_type=jnp.float32)
    down_grad = jnp.dot(flat_grads.T, hidden, preferred_element_type=jnp.float32)
    stacked = jnp.concatenate([gate_up_grad, down_grad], axis=1)
    summed = lax.psum_scatter(
        stacked.astype(jnp.bfloat16), "dp", scatter_dimension=0, tiled=True
    ).astype(jnp.float32)
    d_gate_weight = summed[:, :hidden_units][None]
    d_up_weight = summed[:, hidden_units : 2 * hidden_units][None]
    d_down_weight = summed[:, 2 * hidden_units :].T[None]
    return (d_tokens, d_gate_weight, d_up_weight, d_down_weight)


def solution(mesh):
    placed = (
        P(("dp", "expert"), None),
        P(("dp", "expert"), None),
        P(("dp", "expert"), None),
        P(("dp", "expert"), None),
        P("expert", "dp", None),
        P("expert", "dp", None),
        P("expert", None, "dp"),
    )
    dense = mesh.shape["expert"] == Z * Y * CORES and mesh.shape["dp"] == 2
    return jax.shard_map(
        dense_body if dense else routed_body,
        mesh=mesh,
        in_specs=placed,
        out_specs=(
            P(("dp", "expert"), None),
            P("expert", "dp", None),
            P("expert", "dp", None),
            P("expert", None, "dp"),
        ),
        check_vma=False,
    )
```

```python
import functools

import jax
import jax.numpy as jnp
from jax import lax
from jax.experimental import pallas as pl
from jax.experimental.pallas import tpu as pltpu
from jax.sharding import PartitionSpec as P

F32 = jnp.float32
BF16 = jnp.bfloat16
LANES = 128
VMEM_BYTES = 56 * 1024 * 1024


def vmem():
    return pl.BlockSpec(memory_space=pltpu.VMEM)


def smem():
    return pl.BlockSpec(memory_space=pltpu.SMEM)


def hbm():
    return pl.BlockSpec(memory_space=pl.ANY)


def params():
    return pltpu.CompilerParams(vmem_limit_bytes=VMEM_BYTES)


def cost(flops, moved):
    return pl.CostEstimate(flops=int(flops), bytes_accessed=int(moved), transcendentals=0)


def dot(a, b, dims):
    return lax.dot_general(a, b, (dims, ((), ())), preferred_element_type=F32)


def pack_kernel(experts, tokens, d_output, combine, routes, gate, up, down, out, w_out, parts, turned, sems):
    rows, width = tokens.shape
    hidden_units = gate.shape[1]
    copies = []

    def start(source, target):
        copy = pltpu.make_async_copy(source, target, sems.at[len(copies)])
        copy.start()
        copies.append(copy)

    start(tokens, out.at[:, pl.ds(0, width)])
    start(d_output, out.at[:, pl.ds(width, width)])
    start(gate, w_out.at[:, pl.ds(0, hidden_units)])
    start(up, w_out.at[:, pl.ds(hidden_units, hidden_units)])
    turned[...] = down[...].T
    start(turned, w_out.at[:, pl.ds(2 * hidden_units, hidden_units)])
    line = lax.broadcasted_iota(jnp.int32, (LANES, rows), 0)
    expert = lax.rem(line, experts)
    dense = jnp.zeros((LANES, rows), F32)
    for k in range(routes.shape[0]):
        dense = dense + jnp.where(expert == routes[k : k + 1, :], combine[k : k + 1, :], 0.0)
    high = dense.astype(BF16).astype(F32)
    rest = dense - high
    middle = rest.astype(BF16).astype(F32)
    low = rest - middle
    whole = jnp.where(
        line < experts,
        high,
        jnp.where(line < 2 * experts, middle, jnp.where(line < 3 * experts, low, 0.0)),
    )
    parts[...] = whole.T.astype(BF16)
    start(parts, out.at[:, pl.ds(2 * width, LANES)])
    for c in copies:
        c.wait()


def pack(experts, tokens, d_output, combine, routes, gate, up, down):
    rows, width = tokens.shape
    size, hidden_units = gate.shape
    return pl.pallas_call(
        functools.partial(pack_kernel, experts),
        out_shape=[
            jax.ShapeDtypeStruct((rows, 2 * width + LANES), BF16),
            jax.ShapeDtypeStruct((size, 3 * hidden_units), BF16),
        ],
        in_specs=[vmem()] * 7,
        out_specs=[hbm(), hbm()],
        scratch_shapes=[
            pltpu.VMEM((rows, LANES), BF16),
            pltpu.VMEM((size, hidden_units), BF16),
            pltpu.SemaphoreType.DMA((6,)),
        ],
        cost_estimate=cost(0, 1 << 20),
        compiler_params=params(),
    )(tokens, d_output, combine.T, routes.T, gate, up, down)


def rows_kernel(experts, count, sizes, which, halves, scal, *refs):
    refs = list(refs)
    blocks = [refs.pop(0) for _ in range(count)]
    raw = [refs.pop(0) for _ in range(2 * len(which))]
    past, kinds, wanted_sides, adds = halves
    past_blocks = [refs.pop(0) for _ in range(past)]
    past_grads = [refs.pop(0) for _ in range(kinds)]
    past_scaled = [refs.pop(0) for _ in range(kinds)]
    more = refs.pop(0) if adds else None
    out_rows = [refs.pop(0) for _ in sizes]
    kept = [refs.pop(0) for _ in range(2 * len(which))]
    products = [refs.pop(0) for _ in wanted_sides]
    block, held, grads, scaled, d_rows, in_sems, out_sems = refs[:7]
    part, expert = scal[0], scal[1]
    size, stacked = raw[0].shape
    hidden_units = stacked // 3
    both = 2 * hidden_units
    width = 2 * size
    rows = blocks[0].shape[0]
    sides = [pl.multiple_of(part * size, size), pl.multiple_of((1 - part) * size, size)]
    started, leaving = [], []

    def start(source, target):
        copy = pltpu.make_async_copy(source, target, in_sems.at[len(started)])
        copy.start()
        started.append(copy)
        return copy

    def leave(source, target):
        copy = pltpu.make_async_copy(source, target, out_sems.at[len(leaving)])
        copy.start()
        leaving.append(copy)

    arrivals = [start(b, block.at[pl.ds(i * rows, rows), :]) for i, b in enumerate(blocks)]
    weights = [start(w, held.at[i]) for i, w in enumerate(raw)]
    later = []
    if wanted_sides:
        lefts, made, extra, done = refs[7:]
        row = 0
        for g, x in zip(past_grads, past_scaled):
            n = g.shape[0]
            later.append(start(g, made.at[pl.ds(row, n), :]))
            for k, side in enumerate(wanted_sides):
                later.append(start(x.at[:, pl.ds(sides[side], size)], lefts.at[k, 1, pl.ds(row, n), :]))
            row += n
        for i, b in enumerate(past_blocks):
            for k, side in enumerate(wanted_sides):
                later.append(start(b.at[:, pl.ds(sides[side], size)], lefts.at[k, 0, pl.ds(i * rows, rows), :]))
        if adds:
            later.append(start(more, extra))
    for c in arrivals:
        c.wait()
    parts = block[:, 2 * width :].astype(F32)
    lane = lax.broadcasted_iota(jnp.int32, parts.shape, 1)
    first = []
    for i, one in enumerate(which):
        for c in weights[2 * i : 2 * i + 2]:
            c.wait()
        wanted = expert if one == 0 else expert + 1 - 2 * lax.rem(expert, 2)
        mine = (lax.rem(lane, experts) == wanted) & (lane < 3 * experts)
        weight = jnp.sum(jnp.where(mine, parts, 0.0), axis=1, keepdims=True)
        preact = None
        d_hidden = None
        for side in range(2):
            at = sides[side]
            grad = block[:, pl.ds(pl.multiple_of(width + at, size), size)]
            scaled_half = (weight * grad.astype(F32)).astype(BF16)
            scaled[i, :, pl.ds(at, size)] = scaled_half
            p = dot(block[:, pl.ds(at, size)], held[2 * i + side, :, :both], ((1,), (0,)))
            h = dot(scaled_half, held[2 * i + side, :, both:], ((1,), (0,)))
            preact = p if side == 0 else preact + p
            d_hidden = h if side == 0 else d_hidden + h
        first.append((preact, d_hidden))
    for i in range(len(which)):
        leave(scaled.at[i], kept[2 * i + 1])
    second = []
    for i in range(len(which)):
        preact, d_hidden = first[i]
        gate_pre = preact[:, :hidden_units]
        up_pre = preact[:, hidden_units:]
        sig = jax.nn.sigmoid(gate_pre)
        silu = gate_pre * sig
        d_gate = (d_hidden * up_pre * sig * (1.0 + gate_pre * (1.0 - sig))).astype(BF16)
        d_up = (d_hidden * silu).astype(BF16)
        grads[i, :, :hidden_units] = d_gate
        grads[i, :, hidden_units:both] = d_up
        grads[i, :, both:] = (silu * up_pre).astype(BF16)
        d_preact = jnp.concatenate([d_gate, d_up], axis=1)
        second.append([dot(d_preact, held[2 * i + side, :, :both], ((1,), (1,))) for side in range(2)])
    for i in range(len(which)):
        leave(grads.at[i], kept[2 * i])
    for side in range(2):
        d_rows[:, pl.ds(sides[side], size)] = sum(x[side] for x in second).astype(BF16)
    row = 0
    for out, n in zip(out_rows, sizes):
        leave(d_rows.at[pl.ds(row, n), :], out)
        row += n
    for c in later:
        c.wait()
    end = len(which) - 1
    for k, side in enumerate(wanted_sides):
        at = sides[side]
        for kind, span in enumerate((slice(0, both), slice(both, stacked))):
            now = block[:, pl.ds(at, size)] if kind == 0 else scaled[end, :, pl.ds(at, size)]
            new = dot(lefts[k, kind], made[:, span], ((0,), (0,))) + dot(now, grads[end, :, span], ((0,), (0,)))
            if adds:
                new = new + extra[:, span].astype(F32)
            done[k, :, span] = new.astype(BF16)
        leave(done.at[k], products[k])
    for c in leaving:
        c.wait()


def rows_call(experts, scal, groups, weights, which=(0, 1), past=((), ()), sides=(), more=None):
    blocks = [b for group in groups for b in group]
    count = len(blocks)
    rows = blocks[0].shape[0]
    size, stacked = weights[0].shape
    total = count * rows
    sizes = [len(group) * rows for group in groups]
    sds = jax.ShapeDtypeStruct
    out = [sds((n, 2 * size), BF16) for n in sizes]
    out += [sds((total, stacked), BF16), sds((total, 2 * size), BF16)] * len(which)
    out += [sds((size, stacked), BF16)] * len(sides)
    past_blocks, past_kept = past
    operands = [*blocks, *weights, *past_blocks, *(k[0] for k in past_kept), *(k[1] for k in past_kept)]
    if more is not None:
        operands.append(more)
    scratch = [
        pltpu.VMEM((total, blocks[0].shape[1]), BF16),
        pltpu.VMEM((len(weights), size, stacked), BF16),
        pltpu.VMEM((len(which), total, stacked), BF16),
        pltpu.VMEM((len(which), total, 2 * size), BF16),
        pltpu.VMEM((total, 2 * size), BF16),
        pltpu.SemaphoreType.DMA((len(operands) + len(sides) * (len(past_blocks) + len(past_kept)),)),
        pltpu.SemaphoreType.DMA((len(out),)),
    ]
    if sides:
        earlier = len(past_blocks) * rows
        scratch += [
            pltpu.VMEM((len(sides), 2, earlier, size), BF16),
            pltpu.VMEM((earlier, stacked), BF16),
            pltpu.VMEM((size, stacked), BF16),
            pltpu.VMEM((len(sides), size, stacked), BF16),
        ]
    halves = (len(past_blocks), len(past_kept), sides, more is not None)
    return pl.pallas_call(
        functools.partial(rows_kernel, experts, count, sizes, which, halves),
        out_shape=out,
        in_specs=[smem()] + [hbm()] * len(operands),
        out_specs=[hbm()] * len(out),
        scratch_shapes=scratch,
        cost_estimate=cost(24 * total * size * stacked * len(which) * (1 if len(which) == 2 else 10), 1 << 20),
        compiler_params=params(),
    )(scal, *operands)


def half_kernel(count, groups, sides, *refs):
    refs = list(refs)
    blocks = [refs.pop(0) for _ in range(count)]
    scaled = [refs.pop(0) for _ in range(groups)]
    grads = [refs.pop(0) for _ in range(groups)]
    more, out, lefts, made, extra, done, sems, out_sems = refs
    size, stacked = done.shape
    both = stacked // 3 * 2
    rows = blocks[0].shape[0]
    at = pl.multiple_of(sides[0] * size, size)
    started = []

    def start(source, target):
        copy = pltpu.make_async_copy(source, target, sems.at[len(started)])
        copy.start()
        started.append(copy)

    for i, b in enumerate(blocks):
        start(b.at[:, pl.ds(at, size)], lefts.at[0, pl.ds(i * rows, rows), :])
    row = 0
    for g in grads:
        start(g, made.at[pl.ds(row, g.shape[0]), :])
        row += g.shape[0]
    start(more, extra)
    early = len(started)
    row = 0
    for x in scaled:
        start(x.at[:, pl.ds(at, size)], lefts.at[1, pl.ds(row, x.shape[0]), :])
        row += x.shape[0]
    leaving = []
    for kind, (first, wide) in enumerate(((0, both), (both, stacked - both))):
        for c in started[:early] if kind == 0 else started[early:]:
            c.wait()
        new = dot(lefts[kind], made[:, first : first + wide], ((0,), (0,)))
        done[:, first : first + wide] = (new + extra[:, first : first + wide].astype(F32)).astype(BF16)
        copy = pltpu.make_async_copy(
            done.at[:, pl.ds(first, wide)], out.at[:, pl.ds(first, wide)], out_sems.at[len(leaving)]
        )
        copy.start()
        leaving.append(copy)
    for c in leaving:
        c.wait()


def half_call(sides, blocks, kept, more):
    grads, scaled = [k[0] for k in kept], [k[1] for k in kept]
    size = scaled[0].shape[1] // 2
    stacked = grads[0].shape[1]
    total = len(blocks) * blocks[0].shape[0]
    operands = [*blocks, *scaled, *grads, more]
    return pl.pallas_call(
        functools.partial(half_kernel, len(blocks), len(kept)),
        out_shape=jax.ShapeDtypeStruct((size, stacked), BF16),
        in_specs=[smem()] + [hbm()] * len(operands),
        out_specs=hbm(),
        scratch_shapes=[
            pltpu.VMEM((2, total, size), BF16),
            pltpu.VMEM((total, stacked), BF16),
            pltpu.VMEM((size, stacked), BF16),
            pltpu.VMEM((size, stacked), BF16),
            pltpu.SemaphoreType.DMA((len(operands),)),
            pltpu.SemaphoreType.DMA((2,)),
        ],
        cost_estimate=cost(1024, 1024),
        compiler_params=params(),
    )(sides, *operands)


Z, Y, CORES = 4, 2, 2


def pairs_of(move):
    out = []
    for z in range(Z):
        for y in range(Y):
            for c in range(CORES):
                to = move(z, y, c)
                if to is not None:
                    out.append(((z * Y + y) * CORES + c, (to[0] * Y + to[1]) * CORES + to[2]))
    return out


def along_z(table):
    return pairs_of(lambda z, y, c: (table[z], y, c) if z in table else None)


SWAP_CORE = pairs_of(lambda z, y, c: (z, y, 1 - c))
SWAP_Y = pairs_of(lambda z, y, c: (z, 1 - y, c))
OUTER = along_z({0: 1, 1: 0, 2: 3, 3: 2})
INNER = along_z({1: 2, 2: 1})
OUTWARD = along_z({1: 0, 2: 3})
INWARD = along_z({0: 1, 3: 2})
SKIP_TO_OUTER = along_z({1: 3, 2: 0})


def after(value, *others):
    return lax.optimization_barrier((value,) + others)[0]


def dense_body(tokens, d_output, combine, routes, gate_weight, up_weight, down_weight):
    experts = lax.axis_size("expert")
    part = lax.axis_index("dp")
    expert = lax.axis_index("expert")
    z = expert // (Y * CORES)
    inner = (z == 1) | (z == 2)
    scal = jnp.stack([part, expert]).astype(jnp.int32)
    mine = part[None].astype(jnp.int32)
    other = (1 - part)[None].astype(jnp.int32)

    move = lambda a, pairs: lax.ppermute(a, "expert", pairs)
    across = lambda a: lax.ppermute(a, "dp", [(0, 1), (1, 0)])

    swap = lambda a: move(a, SWAP_CORE)
    own, w_own = pack(experts, tokens, d_output, combine, routes, gate_weight[0], up_weight[0], down_weight[0])
    w_part = across(w_own)

    b1 = move(own, OUTER)
    f1 = move(own, INNER)
    y0 = move(own, SWAP_Y)
    f2 = move(b1, INNER)
    y1 = move(after(b1, y0), SWAP_Y)
    g1 = move(f1, OUTWARD)
    b2 = jnp.where(inner, f1, g1)
    y2 = move(after(b2, y1, f2), SWAP_Y)
    g2 = move(f2, OUTWARD)

    w_core = swap(after(w_own, y1, f2))
    w_both = swap(after(w_part, y1, f2))
    weights = [w_own, w_part, w_core, w_both]
    p0, p1, p2, q0, q1, *kept_a = rows_call(experts, scal, [[own], [b1], [b2], [y0], [y1]], weights)
    b3 = jnp.where(inner, f2, after(g2, p0))
    y3 = move(after(b3, y2), SWAP_Y)
    early = [own, b1, b2, y0, y1]

    p3, q2, *kept_b, to_other, to_mine = rows_call(
        experts, scal, [[b3], [y2]], weights, past=(early, [kept_a[2:]]), sides=(1, 0)
    )
    y3 = after(y3, q2)
    cy3 = swap(y3)
    got_other, got_mine = swap(after(to_other, y3)), swap(after(to_mine, y3, cy3))
    r2 = move(after(q2, y3), SWAP_Y)

    blocks = early + [b3, y2]
    kept = [kept_a[:2], kept_b[:2]]
    last, pair, *kept_c, send = rows_call(
        experts, scal, [[y3], [cy3]], weights[:2], which=(0,), past=(blocks, kept), sides=(1,), more=got_other
    )
    from_part = across(send)
    add = lambda *terms: sum(t.astype(F32) for t in terms).astype(BF16)
    r3 = move(add(last, swap(after(pair, r2, got_mine))), SWAP_Y)
    r1 = move(after(q1, r3), SWAP_Y)
    s2 = add(p2, r2)
    s2 = add(s2, move(s2, INWARD))
    s3 = add(p3, r3)
    s3 = add(s3, move(s3, INWARD))
    keep = half_call(after(mine, send, s3), blocks + [y3, cy3], kept + [kept_c], more=got_mine)

    s1 = add(p1, r1)
    r0 = move(after(q0, keep), SWAP_Y)
    from_part = after(from_part, s3)
    hidden_units = gate_weight.shape[2]
    whole = lambda a: keep[:, a : a + hidden_units].astype(F32) + from_part[:, a : a + hidden_units].astype(F32)
    d_gate, d_up, d_down = whole(0), whole(hidden_units), whole(2 * hidden_units).T
    d_tokens = add(after(p0, from_part), r0, move(s1, OUTER), move(s2, INNER), move(s3, SKIP_TO_OUTER))
    return (d_tokens, d_gate[None], d_up[None], d_down[None])


def route_slots(routes, experts):
    matches = (routes[:, :, None] == jnp.arange(experts, dtype=jnp.int32)[None, None, :]).astype(
        jnp.int32
    )
    per_token = jnp.sum(matches, axis=1)
    earlier = jnp.cumsum(per_token, axis=0) - per_token
    return jnp.sum(matches * earlier[:, None, :], axis=2)


def row_work(row_inputs, row_grads, gate_up, down_matrix):
    hidden_units = down_matrix.shape[0]
    preact = jnp.dot(row_inputs, gate_up, preferred_element_type=jnp.float32)
    gate_pre = preact[:, :hidden_units]
    up_pre = preact[:, hidden_units:]
    gate_sigmoid = jax.nn.sigmoid(gate_pre)
    hidden = (gate_pre * gate_sigmoid * up_pre).astype(jnp.bfloat16)
    d_hidden = jnp.dot(row_grads, down_matrix.T, preferred_element_type=jnp.float32)
    d_gate_pre = d_hidden * up_pre * gate_sigmoid * (1.0 + gate_pre * (1.0 - gate_sigmoid))
    d_up_pre = d_hidden * gate_pre * gate_sigmoid
    d_preact = jnp.concatenate([d_gate_pre, d_up_pre], axis=1).astype(jnp.bfloat16)
    d_rows = jnp.dot(d_preact, gate_up.T, preferred_element_type=jnp.float32).astype(jnp.bfloat16)
    return (d_rows, hidden, d_preact)


def routed_body(tokens, d_output, combine, routes, gate_weight, up_weight, down_weight):
    experts = lax.axis_size("expert")
    tok_count = tokens.shape[0]
    model_width = tokens.shape[1]
    top_count = routes.shape[1]
    capacity = max(2, (9 * tok_count * top_count + 8 * experts - 1) // (8 * experts))
    slot_count = experts * capacity
    slot_index = route_slots(routes, experts)
    position = (routes * capacity + slot_index).reshape(-1)
    spread_inputs = jnp.repeat(tokens, top_count, axis=0)
    scaled = (
        (combine[:, :, None] * d_output[:, None, :].astype(jnp.float32))
        .astype(jnp.bfloat16)
        .reshape(-1, model_width)
    )
    send_inputs = (
        jnp.zeros((slot_count, model_width), jnp.bfloat16)
        .at[position]
        .set(spread_inputs)
        .reshape(experts, capacity, model_width)
    )
    send_grads = (
        jnp.zeros((slot_count, model_width), jnp.bfloat16)
        .at[position]
        .set(scaled)
        .reshape(experts, capacity, model_width)
    )
    whole_gate, whole_up, whole_down = (
        lax.all_gather(gate_weight, "dp", axis=1, tiled=True),
        lax.all_gather(up_weight, "dp", axis=1, tiled=True),
        lax.all_gather(down_weight, "dp", axis=2, tiled=True),
    )
    gate_up = jnp.concatenate([whole_gate[0], whole_up[0]], axis=1)
    down_matrix = whole_down[0]
    hidden_units = down_matrix.shape[0]
    recv_inputs, recv_grads = (
        lax.all_to_all(send_inputs, "expert", split_axis=0, concat_axis=0, tiled=True),
        lax.all_to_all(send_grads, "expert", split_axis=0, concat_axis=0, tiled=True),
    )
    flat_inputs = recv_inputs.reshape(-1, model_width)
    flat_grads = recv_grads.reshape(-1, model_width)
    d_rows, hidden, d_preact = row_work(flat_inputs, flat_grads, gate_up, down_matrix)
    returned = lax.all_to_all(
        d_rows.reshape(experts, capacity, model_width),
        "expert",
        split_axis=0,
        concat_axis=0,
        tiled=True,
    )
    route_rows = returned.reshape(-1, model_width)[position].reshape(
        tok_count, top_count, model_width
    )
    d_tokens = jnp.sum(route_rows.astype(jnp.float32), axis=1).astype(jnp.bfloat16)
    gate_up_grad = jnp.dot(flat_inputs.T, d_preact, preferred_element_type=jnp.float32)
    down_grad = jnp.dot(flat_grads.T, hidden, preferred_element_type=jnp.float32)
    stacked = jnp.concatenate([gate_up_grad, down_grad], axis=1)
    summed = lax.psum_scatter(
        stacked.astype(jnp.bfloat16), "dp", scatter_dimension=0, tiled=True
    ).astype(jnp.float32)
    d_gate_weight = summed[:, :hidden_units][None]
    d_up_weight = summed[:, hidden_units : 2 * hidden_units][None]
    d_down_weight = summed[:, 2 * hidden_units :].T[None]
    return (d_tokens, d_gate_weight, d_up_weight, d_down_weight)


def solution(mesh):
    placed = (
        P(("dp", "expert"), None),
        P(("dp", "expert"), None),
        P(("dp", "expert"), None),
        P(("dp", "expert"), None),
        P("expert", "dp", None),
        P("expert", "dp", None),
        P("expert", None, "dp"),
    )
    dense = mesh.shape["expert"] == Z * Y * CORES and mesh.shape["dp"] == 2
    return jax.shard_map(
        dense_body if dense else routed_body,
        mesh=mesh,
        in_specs=placed,
        out_specs=(
            P(("dp", "expert"), None),
            P("expert", "dp", None),
            P("expert", "dp", None),
            P("expert", None, "dp"),
        ),
        check_vma=False,
    )
```
